32 devices in a mesh: grp: 2 (over y), seq: 16 (over z, x, core).
Axes of the slice: x: 2, y: 2, z: 4, core: 2. Of those that a mesh axis runs over, the one named last changes fastest.
Arguments:
- tokens: bfloat16 [32768, 512], P(('grp', 'seq')), parts along dimension 0, may hold values from -6 to 6
- cotangent: bfloat16 [32768, 512], P(('grp', 'seq')), parts along dimension 0, may hold values from -6 to 6
- factor_one: bfloat16 [16, 1024, 1024], P('seq'), may hold values from -0.1875 to 0.1875
- factor_two: bfloat16 [1024, 16, 16], P('seq'), may hold values from -1.5 to 1.5
- up_blocks: bfloat16 [4, 128, 512], replicated, may hold values from -0.5 to 0.5
- down_blocks: bfloat16 [4, 512, 128], replicated, may hold values from -0.25 to 0.25
Outputs:
- grad_tokens: bfloat16 [32768, 512], P(('grp', 'seq')), parts along dimension 0
- grad_one: float32 [32, 1024, 1024], P(('grp', 'seq')), parts along dimension 0
- grad_two: float32 [2048, 16, 16], P(('grp', 'seq')), parts along dimension 0
- grad_up: float32 [8, 128, 512], P('grp'), parts along dimension 0
- grad_down: float32 [8, 512, 128], P('grp'), parts along dimension 0
The draws below stay inside these ranges and needn't reach their ends.
There are 2 independent parts, one for each index of `grp`. The reference program is written for one: setup_inputs(seed, part) draws one part's arguments, and reference() takes and returns one part's arrays. A program takes and returns all parts, laid end to end along the dimension named above; an argument that names none is the same for every part. Nothing has to cross between parts.
All inputs are finite; a program needn't handle non-finite values.
Results may differ from the reference program's by a relative error of at most 0.012.
Values may be sent and summed in bfloat16 or wider, within the bound.
No kernel may reach another device: no remote copies, remote signals or barrier semaphores. Data moves between devices by JAX's collectives and lax.ppermute only.
A program may use at most 128 MiB of HBM per device.

```python
import jax
import jax.numpy as jnp

B = 1024
C = 512
FF = 2048
NCB = 4
NB = 16
TOKENS = 16384


def block_scale(key, shape, shards, low, top_value):
    def one(axis_at, parts):
        steps = jax.random.uniform(jax.random.fold_in(jax.random.fold_in(key, 6), axis_at), (parts,), jnp.float32, low / len(shards), top_value / len(shards))
        return jnp.repeat(jnp.exp(steps), shape[axis_at] // parts).reshape((-1,) + (1,) * (len(shape) - axis_at - 1))

    loudness = one(*shards[0])
    for cut in shards[1:]:
        loudness = loudness * one(*cut)
    return loudness


def scatter_about(rng, dims, scale, limit, shards=(), dtype=jnp.bfloat16):
    loudness = block_scale(rng, dims, shards, -0.22, 0.18) if shards else 1.0
    result = jax.random.normal(rng, dims, jnp.float32) * scale * loudness
    return jnp.minimum(jnp.maximum(result, -limit), limit).astype(dtype)


def setup_inputs(seed: int = 0, part: int = 0) -> dict:
    keys = jax.random.split(jax.random.key(seed), 7)
    own_keys = jax.random.split(jax.random.fold_in(keys[6], part), 7)
    return {
        "tokens": scatter_about(own_keys[0], (TOKENS, C), 1.0, 6.0, ((0, 16),)),
        "cotangent": scatter_about(own_keys[1], (TOKENS, C), 1.0, 6.0, ((0, 16),)),
        "factor_one": scatter_about(keys[2], (NB, B, B), B ** -0.5, 0.1875, ((0, 16),)),
        "factor_two": scatter_about(keys[3], (B, NB, NB), NB ** -0.5, 1.5, ((0, 16),)),
        "up_blocks": scatter_about(keys[4], (NCB, C // NCB, FF // NCB), (C // NCB) ** -0.5, 0.5),
        "down_blocks": scatter_about(keys[5], (NCB, FF // NCB, C // NCB), (FF // NCB) ** -0.5, 0.25),
    }


def silu_slope(values):
    logistic = jax.nn.sigmoid(values)
    return logistic * (1.0 + values * (1.0 - logistic))


def swap_groups(hidden, groups):
    leading = hidden.shape[0]
    inner = hidden.shape[2]
    return hidden.reshape(leading, groups, groups, inner // groups).transpose(0, 2, 1, 3).reshape(leading, groups, inner)


def reference(tokens, cotangent, factor_one, factor_two, up_blocks, down_blocks):
    scale_all = float(TOKENS) ** -0.5
    one_f = factor_one.astype(jnp.float32)
    two_f = factor_two.astype(jnp.float32)
    up_f = up_blocks.astype(jnp.float32)
    down_f = down_blocks.astype(jnp.float32)
    blocked = tokens.reshape(NB, B, C)
    features = blocked.astype(jnp.float32)
    first_mix = jnp.einsum('jki,jic->jkc', one_f, features).astype(jnp.bfloat16)
    first_f = first_mix.astype(jnp.float32)
    second_mix = jnp.einsum('kmj,jkc->mkc', two_f, first_f).astype(jnp.bfloat16)
    mixed_f = second_mix.astype(jnp.float32)
    gate_value = jax.nn.silu(features)
    hidden_state = (features + mixed_f * gate_value).astype(jnp.bfloat16)
    groups = NCB
    row_count = TOKENS
    hidden_rows = hidden_state.reshape(row_count, groups, C // groups).astype(jnp.float32)
    grad_rows = cotangent.reshape(row_count, groups, C // groups).astype(jnp.float32)
    before_act = jnp.einsum('rbc,bcf->rbf', hidden_rows, up_f)
    activated = jax.nn.silu(before_act).astype(jnp.bfloat16)
    permuted = swap_groups(activated, groups).astype(jnp.float32)
    grad_down = jnp.einsum('rbf,rbc->bfc', permuted, grad_rows) * scale_all
    grad_perm = jnp.einsum('rbc,bfc->rbf', grad_rows, down_f)
    grad_act = swap_groups(grad_perm, groups)
    grad_before = (grad_act * silu_slope(before_act)).astype(jnp.bfloat16).astype(jnp.float32)
    grad_up = jnp.einsum('rbc,rbf->bcf', hidden_rows, grad_before) * scale_all
    grad_hidden = (grad_rows + jnp.einsum('rbf,bcf->rbc', grad_before, up_f)).reshape(NB, B, C).astype(jnp.bfloat16)
    grad_hidden_f = grad_hidden.astype(jnp.float32)
    grad_mixed = (grad_hidden_f * gate_value).astype(jnp.bfloat16).astype(jnp.float32)
    gate_grad = (grad_hidden_f * (1.0 + mixed_f * silu_slope(features))).astype(jnp.bfloat16)
    grad_first = jnp.einsum('kmj,mkc->jkc', two_f, grad_mixed).astype(jnp.bfloat16).astype(jnp.float32)
    grad_two = jnp.einsum('mkc,jkc->kmj', grad_mixed, first_f) * scale_all
    grad_tokens = (gate_grad.astype(jnp.float32) + jnp.einsum('jki,jkc->jic', one_f, grad_first)).astype(jnp.bfloat16)
    grad_one = jnp.einsum('jkc,jic->jki', grad_first, features) * scale_all
    return grad_tokens.reshape(TOKENS, C), grad_one, grad_two, grad_up, grad_down
```

```python
import jax
import jax.numpy as jnp
from jax import lax
from jax.experimental import pallas as pl
from jax.experimental.pallas import tpu as pltpu
from jax.sharding import PartitionSpec as P

BF = jnp.bfloat16
F32 = jnp.float32
PIECES = 1
VMEM_BYTES = 40 * 1024 * 1024


def sigmoid(z):
    return 0.5 + 0.5 * jnp.tanh(0.5 * z)


def dot(a, b, ca, cb, **kw):
    return lax.dot_general(a, b, (((ca,), (cb,)), ((), ())), preferred_element_type=F32, **kw)


def rows_of(ref):
    value = ref[...]
    return value.reshape(-1, value.shape[-1])


def params(steps=1):
    return pltpu.CompilerParams(
        dimension_semantics=("arbitrary",) * steps, vmem_limit_bytes=VMEM_BYTES
    )


def cost(flops, moved, trans=0):
    return pl.CostEstimate(flops=int(flops), bytes_accessed=int(moved), transcendentals=int(trans))


class Plan:
    def __init__(self, count, block, channels):
        self.count = count
        self.block = block
        self.channels = channels
        self.here = block // count
        self.pieces = PIECES if self.here % (16 * PIECES) == 0 else 1
        self.part = self.here // self.pieces
        self.rows = block // self.pieces
        self.grouped = self.part % 16 == 0

    def view(self, array):
        if self.pieces == 1:
            return array
        return array.reshape(self.count, self.pieces, self.part, array.shape[-1])

    def spec(self, rows, columns, piece, index=lambda i: (i, 0)):
        if self.pieces == 1:
            return pl.BlockSpec((rows, columns), index)

        def whole(i):
            at, col = index(i)
            return (at, piece, 0, col)

        return pl.BlockSpec((rows // self.part, 1, self.part, columns), whole)


def mix_first(plan, factor, blocked, piece):
    def body(factor_ref, x_ref, out_ref):
        out_ref[...] = dot(rows_of(factor_ref), x_ref[...], 1, 0).astype(BF)

    step = min(256, plan.rows)
    return pl.pallas_call(
        body,
        grid=(plan.rows // step,),
        in_specs=[
            plan.spec(step, plan.block, piece),
            pl.BlockSpec((plan.block, plan.channels), lambda i: (0, 0)),
        ],
        out_specs=pl.BlockSpec((step, plan.channels), lambda i: (i, 0)),
        out_shape=jax.ShapeDtypeStruct((plan.rows, plan.channels), BF),
        compiler_params=params(),
        cost_estimate=cost(
            2 * plan.rows * plan.block * plan.channels,
            2 * (plan.rows * plan.block + 2 * plan.block * plan.channels),
        ),
        name="mix_first",
    )(plan.view(factor), blocked)


def spread_factor(plan, factor_two):
    n = plan.count
    groups = plan.here // 16
    wide = n * 16
    turned = factor_two.reshape(groups, 16, n, n).transpose(0, 2, 1, 3).reshape(groups, wide, n)

    def body(in_ref, out_ref):
        col = lax.broadcasted_iota(jnp.int32, (n, wide), 1)
        row = lax.broadcasted_iota(jnp.int32, (n, wide), 0)
        pick = jnp.where(col // 16 == row, 1.0, 0.0).astype(BF)
        full = dot(in_ref[0], pick, 1, 0)
        r = lax.broadcasted_iota(jnp.int32, (wide, wide), 0)
        c = lax.broadcasted_iota(jnp.int32, (wide, wide), 1)
        out_ref[0] = jnp.where(r % 16 == c % 16, full, 0.0).astype(BF)

    return pl.pallas_call(
        body,
        grid=(groups,),
        in_specs=[pl.BlockSpec((1, wide, n), lambda g: (g, 0, 0))],
        out_specs=pl.BlockSpec((1, wide, wide), lambda g: (g, 0, 0)),
        out_shape=jax.ShapeDtypeStruct((groups, wide, wide), BF),
        compiler_params=params(),
        cost_estimate=cost(2 * groups * wide * wide * n, 2 * groups * wide * wide),
        name="spread_factor",
    )(turned)


def mix_second(plan, spread, cols, piece, back):
    n = plan.count
    wide = n * 16
    groups = plan.part // 16

    def body(m_ref, in_ref, out_ref):
        rows = in_ref[...].reshape(wide, plan.channels)
        got = dot(m_ref[0], rows, 0 if back else 1, 0).astype(BF)
        out_ref[...] = got.reshape(n, 16, plan.channels)

    out = pl.pallas_call(
        body,
        grid=(groups,),
        in_specs=[
            pl.BlockSpec((1, wide, wide), lambda g: (piece * groups + g, 0, 0)),
            pl.BlockSpec((n, 16, plan.channels), lambda g: (0, g, 0)),
        ],
        out_specs=pl.BlockSpec((n, 16, plan.channels), lambda g: (0, g, 0)),
        out_shape=jax.ShapeDtypeStruct((n, plan.part, plan.channels), BF),
        compiler_params=params(),
        cost_estimate=cost(
            2 * groups * wide * wide * plan.channels,
            4 * plan.rows * plan.channels + 2 * groups * wide * wide,
        ),
        name="mix_second_back" if back else "mix_second",
    )(spread, cols.reshape(n, plan.part, plan.channels))
    return out.reshape(plan.rows, plan.channels)


def grad_second(plan, grads, firsts, scale):
    n = plan.count
    wide = n * 16
    groups = plan.part // 16

    def body(g_ref, u_ref, out_ref):
        g = g_ref[...].reshape(wide, plan.channels)
        u = u_ref[...].reshape(wide, plan.channels)
        full = dot(g, u, 1, 1)
        r = lax.broadcasted_iota(jnp.int32, (wide, wide), 0)
        c = lax.broadcasted_iota(jnp.int32, (wide, wide), 1)
        kept = jnp.where(r % 16 == c % 16, full, 0.0)
        row = lax.broadcasted_iota(jnp.int32, (wide, n), 0)
        col = lax.broadcasted_iota(jnp.int32, (wide, n), 1)
        pick = jnp.where(row // 16 == col, 1.0, 0.0)
        out_ref[0] = dot(kept, pick, 1, 0, precision=lax.Precision.HIGHEST) * scale

    out = pl.pallas_call(
        body,
        grid=(groups,),
        in_specs=[pl.BlockSpec((n, 16, plan.channels), lambda g: (0, g, 0))] * 2,
        out_specs=pl.BlockSpec((1, wide, n), lambda g: (g, 0, 0)),
        out_shape=jax.ShapeDtypeStruct((groups, wide, n), F32),
        compiler_params=params(),
        cost_estimate=cost(
            2 * groups * wide * wide * plan.channels, 4 * plan.rows * plan.channels
        ),
        name="grad_second",
    )(
        grads.reshape(n, plan.part, plan.channels),
        firsts.reshape(n, plan.part, plan.channels),
    )
    return out.reshape(groups, n, 16, n).transpose(0, 2, 1, 3).reshape(plan.part, n, n)


def middle(plan, blocked, incoming, mixed, up_blocks, down_blocks, piece, before):
    groups, width, inner = up_blocks.shape
    sub = inner // groups
    step = min(256, plan.rows)

    def body(*refs):
        x_ref, g_ref, v_ref, up_ref, down_ref = refs[:5]
        dv_ref, r_ref, w_ref = refs[-3:]

        @pl.when(pl.program_id(0) == 0)
        def _():
            if before is None:
                w_ref[...] = jnp.zeros_like(w_ref)
            else:
                w_ref[...] = refs[5][...]

        x = rows_of(x_ref).astype(F32)
        g = rows_of(g_ref)
        v = v_ref[...].astype(F32)
        sx = sigmoid(x)
        gate = x * sx
        h = (x + v * gate).astype(BF)
        h_parts = [h[:, b * width : (b + 1) * width] for b in range(groups)]
        g_parts = [g[:, b * width : (b + 1) * width] for b in range(groups)]
        acts, slopes, back = [], [], []
        for b in range(groups):
            a = dot(h_parts[b], up_ref[b], 1, 0)
            s = sigmoid(a)
            q = a * s
            acts.append(q.astype(BF))
            slopes.append(s + q * (1.0 - s))
            back.append(dot(g_parts[b], down_ref[b], 1, 1))
        grads = []
        for b in range(groups):
            lanes = slice(b * sub, (b + 1) * sub)
            perm = jnp.concatenate([acts[p][:, lanes] for p in range(groups)], axis=1)
            w_ref[groups + b] += dot(g_parts[b], perm, 0, 0)
            dq = jnp.concatenate([back[p][:, lanes] for p in range(groups)], axis=1)
            da = (dq * slopes[b]).astype(BF)
            w_ref[b] += dot(h_parts[b], da, 0, 0)
            grads.append(dot(da, up_ref[b], 1, 1))
        dh = (g.astype(F32) + jnp.concatenate(grads, axis=1)).astype(BF).astype(F32)
        dv_ref[...] = (dh * gate).astype(BF)
        r_ref[...] = (dh * (1.0 + v * (sx + gate * (1.0 - sx)))).astype(BF)

    block = pl.BlockSpec((step, plan.channels), lambda i: (i, 0))
    full = pl.BlockSpec((2 * groups, width, inner), lambda i: (0, 0, 0))
    in_specs = [
        plan.spec(step, plan.channels, piece),
        plan.spec(step, plan.channels, piece),
        block,
        pl.BlockSpec(up_blocks.shape, lambda i: (0, 0, 0)),
        pl.BlockSpec(down_blocks.shape, lambda i: (0, 0, 0)),
    ]
    operands = [plan.view(blocked), plan.view(incoming), mixed, up_blocks, down_blocks]
    if before is not None:
        in_specs.append(full)
        operands.append(before)
    hidden = plan.rows * groups * inner
    return pl.pallas_call(
        body,
        grid=(plan.rows // step,),
        in_specs=in_specs,
        out_specs=[block, block, full],
        out_shape=[
            jax.ShapeDtypeStruct((plan.rows, plan.channels), BF),
            jax.ShapeDtypeStruct((plan.rows, plan.channels), BF),
            jax.ShapeDtypeStruct((2 * groups, width, inner), F32),
        ],
        compiler_params=params(),
        cost_estimate=cost(
            10 * hidden * width, 10 * plan.rows * plan.channels + 8 * groups * width * inner, hidden
        ),
        name="middle",
    )(*operands)


def finish(plan, factor, grad_firsts, blocked, gate_grads, piece, scale, rows_before, sum_before):
    last = piece == plan.pieces - 1
    step = min(256, plan.block)
    n_gates = plan.pieces if last else 0

    def body(*refs):
        factor_ref, d_ref, x_ref = refs[:3]
        one_ref, out_ref = refs[-2:]
        d = d_ref[...]
        one = dot(d, x_ref[...], 1, 1) * scale
        one_ref[...] = one.reshape(one_ref.shape)
        total = dot(rows_of(factor_ref), d, 0, 0)
        at = 3
        if piece > 0:
            total = total + refs[4][...]
            at = 5
        if last:
            if plan.pieces == 1:
                out_ref[...] = (total + refs[at][...].astype(F32)).astype(BF)
            else:
                total = total.reshape(step // plan.here, plan.pieces, plan.part, plan.channels)
                for q in range(plan.pieces):
                    got = (total[:, q] + refs[at + q][...].astype(F32)).astype(BF)
                    out_ref[:, q] = got
        else:
            out_ref[...] = total

    wide = pl.BlockSpec((step, plan.channels), lambda i: (i, 0))
    in_specs = [
        plan.spec(plan.rows, step, piece, lambda i: (0, i)),
        pl.BlockSpec((plan.rows, plan.channels), lambda i: (0, 0)),
        wide,
    ]
    operands = [plan.view(factor), grad_firsts, blocked]
    aliases = {}
    if piece > 0:
        in_specs += [pl.BlockSpec(memory_space=pl.ANY), wide]
        operands += [rows_before, sum_before]
        aliases = {3: 0}
    if last:
        if plan.pieces == 1:
            in_specs.append(wide)
            operands += gate_grads
            out_spec = wide
            out_shape = (plan.block, plan.channels)
        else:
            in_specs += [
                pl.BlockSpec((step // plan.here, plan.part, plan.channels), lambda i: (i, 0, 0))
            ] * n_gates
            operands += [r.reshape(plan.count, plan.part, plan.channels) for r in gate_grads]
            out_spec = pl.BlockSpec(
                (step // plan.here, plan.pieces, plan.part, plan.channels), lambda i: (i, 0, 0, 0)
            )
            out_shape = (plan.count, plan.pieces, plan.part, plan.channels)
    else:
        out_spec = wide
        out_shape = (plan.block, plan.channels)
    one_shape = (plan.block, plan.block)
    if plan.pieces > 1:
        one_shape = (plan.count, plan.pieces, plan.part, plan.block)
    return pl.pallas_call(
        body,
        grid=(plan.block // step,),
        in_specs=in_specs,
        out_specs=[plan.spec(plan.rows, step, piece, lambda i: (0, i)), out_spec],
        out_shape=[
            jax.ShapeDtypeStruct(one_shape, F32),
            jax.ShapeDtypeStruct(out_shape, BF if last else F32),
        ],
        input_output_aliases=aliases,
        compiler_params=params(),
        cost_estimate=cost(
            4 * plan.rows * plan.block * plan.channels,
            6 * plan.rows * plan.block + 8 * plan.block * plan.channels,
        ),
        name="finish",
    )(*operands)


def sum_over(values, count):
    if count & (count - 1) or values.shape[0] % count:
        return lax.psum(values, "seq")
    me = lax.axis_index("seq")
    total = values
    steps = [1 << s for s in range(count.bit_length() - 1)]
    for step in steps:
        halves = total.reshape(2, total.shape[0] // 2, total.shape[1])
        mine = (me // step) % 2
        keep = lax.dynamic_index_in_dim(halves, mine, 0, keepdims=False)
        send = lax.dynamic_index_in_dim(halves, 1 - mine, 0, keepdims=False).astype(BF)
        got = lax.ppermute(send, "seq", [(i, i ^ step) for i in range(count)])
        total = keep + got.astype(F32)
    total = total.astype(BF)
    for step in reversed(steps):
        mine = (me // step) % 2
        got = lax.ppermute(total, "seq", [(i, i ^ step) for i in range(count)])
        low = jnp.where(mine == 0, total, got)
        high = jnp.where(mine == 0, got, total)
        total = jnp.concatenate([low, high], axis=0)
    return total


def write_weights(total, up_shape, down_shape, scale):
    groups, width, inner = up_shape

    def body(up_in, down_in, up_ref, down_ref):
        up_ref[0] = up_in[...].astype(F32) * scale
        down_ref[0] = (down_in[...].astype(F32) * scale).T

    return pl.pallas_call(
        body,
        grid=(groups,),
        in_specs=[
            pl.BlockSpec((width, inner), lambda b: (b, 0)),
            pl.BlockSpec((width, inner), lambda b: (groups + b, 0)),
        ],
        out_specs=[
            pl.BlockSpec((1, width, inner), lambda b: (b, 0, 0)),
            pl.BlockSpec((1, inner, width), lambda b: (b, 0, 0)),
        ],
        out_shape=[
            jax.ShapeDtypeStruct(up_shape, F32),
            jax.ShapeDtypeStruct(down_shape, F32),
        ],
        compiler_params=params(),
        cost_estimate=cost(groups * width * inner, 12 * groups * width * inner),
        name="write_weights",
    )(total, total)


def on_device(tokens, cotangent, factor_one, factor_two, up_blocks, down_blocks):
    count = lax.axis_size("seq")
    block, channels = factor_one.shape[1], tokens.shape[1]
    plan = Plan(count, block, channels)
    scale = float(count * tokens.shape[0]) ** (-0.5)
    factor = factor_one.reshape(block, block)
    pieces = range(plan.pieces)

    def exchange(rows):
        cut = rows.reshape(count, plan.part, channels)
        got = lax.all_to_all(cut, "seq", split_axis=0, concat_axis=0, tiled=True)
        return got.reshape(plan.rows, channels)

    if plan.grouped:
        spread = spread_factor(plan, factor_two)

    def second(cols, piece, back):
        if plan.grouped:
            return mix_second(plan, spread, cols, piece, back)
        cut = cols.reshape(count, plan.part, channels)
        names = "kmj,mkc->jkc" if back else "kmj,jkc->mkc"
        got = jnp.einsum(names, factor_two, cut, preferred_element_type=F32).astype(BF)
        return got.reshape(plan.rows, channels)

    def second_grad(grads, firsts):
        if plan.grouped:
            return grad_second(plan, grads, firsts, scale)
        shape = (count, plan.part, channels)
        got = jnp.einsum(
            "mkc,jkc->kmj", grads.reshape(shape), firsts.reshape(shape), preferred_element_type=F32
        )
        return got * scale

    firsts = [exchange(mix_first(plan, factor, tokens, q)) for q in pieces]
    mixed = [exchange(second(firsts[q], q, False)) for q in pieces]
    weights = None
    grad_mixed, gate_grads = [], []
    for q in pieces:
        dv, r, weights = middle(
            plan, tokens, cotangent, mixed[q], up_blocks, down_blocks, q, weights
        )
        grad_mixed.append(exchange(dv))
        gate_grads.append(r)
    grad_firsts = [exchange(second(grad_mixed[q], q, True)) for q in pieces]
    two = [second_grad(grad_mixed[q], firsts[q]) for q in pieces]
    total = sum_over(weights.reshape(-1, weights.shape[-1]), count)
    grad_up, grad_down = write_weights(total, up_blocks.shape, down_blocks.shape, scale)
    one, tokens_sum = None, None
    for q in pieces:
        one, tokens_sum = finish(
            plan, factor, grad_firsts[q], tokens, gate_grads, q, scale, one, tokens_sum
        )
    return (
        tokens_sum.reshape(tokens.shape),
        one.reshape(1, block, block),
        jnp.concatenate(two, axis=0),
        grad_up,
        grad_down,
    )


def solution(mesh):
    return jax.shard_map(
        on_device,
        mesh=mesh,
        in_specs=(
            P(("grp", "seq"), None),
            P(("grp", "seq"), None),
            P("seq", None, None),
            P("seq", None, None),
            P(),
            P(),
        ),
        out_specs=(
            P(("grp", "seq"), None),
            P(("grp", "seq"), None, None),
            P(("grp", "seq"), None, None),
            P("grp", None, None),
            P("grp", None, None),
        ),
        check_vma=False,
    )
```

```python
import jax
import jax.numpy as jnp
from jax import lax
from jax.experimental import pallas as pl
from jax.experimental.pallas import tpu as pltpu
from jax.sharding import PartitionSpec as P

BF = jnp.bfloat16
F32 = jnp.float32
PIECES = 2
VMEM_BYTES = 60 * 1024 * 1024


def sigmoid(z):
    return 0.5 + 0.5 * jnp.tanh(0.5 * z)


def dot(a, b, ca, cb, **kw):
    return lax.dot_general(a, b, (((ca,), (cb,)), ((), ())), preferred_element_type=F32, **kw)


def rows_of(ref):
    value = ref[...]
    return value.reshape(-1, value.shape[-1])


def params(steps=1):
    return pltpu.CompilerParams(
        dimension_semantics=("arbitrary",) * steps, vmem_limit_bytes=VMEM_BYTES
    )


def cost(flops, moved, trans=0):
    return pl.CostEstimate(flops=int(flops), bytes_accessed=int(moved), transcendentals=int(trans))


class Plan:
    def __init__(self, count, block, channels):
        self.count = count
        self.block = block
        self.channels = channels
        self.here = block // count
        self.pieces = PIECES if self.here % (16 * PIECES) == 0 else 1
        self.part = self.here // self.pieces
        self.rows = block // self.pieces
        self.grouped = self.part % 16 == 0

    def view(self, array):
        if self.pieces == 1:
            return array
        return array.reshape(self.count, self.pieces, self.part, array.shape[-1])

    def spec(self, rows, columns, piece, index=lambda i: (i, 0)):
        if self.pieces == 1:
            return pl.BlockSpec((rows, columns), index)

        def whole(i):
            at, col = index(i)
            return (at, piece, 0, col)

        return pl.BlockSpec((rows // self.part, 1, self.part, columns), whole)


def mix_first(plan, factor, blocked, piece):
    def body(factor_ref, x_ref, out_ref):
        out_ref[...] = dot(rows_of(factor_ref), x_ref[...], 1, 0).astype(BF)

    step = min(256, plan.rows)
    return pl.pallas_call(
        body,
        grid=(plan.rows // step,),
        in_specs=[
            plan.spec(step, plan.block, piece),
            pl.BlockSpec((plan.block, plan.channels), lambda i: (0, 0)),
        ],
        out_specs=pl.BlockSpec((step, plan.channels), lambda i: (i, 0)),
        out_shape=jax.ShapeDtypeStruct((plan.rows, plan.channels), BF),
        compiler_params=params(),
        cost_estimate=cost(
            2 * plan.rows * plan.block * plan.channels,
            2 * (plan.rows * plan.block + 2 * plan.block * plan.channels),
        ),
        name="mix_first",
    )(plan.view(factor), blocked)


def spread_factor(plan, factor_two):
    n = plan.count
    groups = plan.here // 16
    wide = n * 16
    turned = factor_two.reshape(groups, 16, n, n).transpose(0, 2, 1, 3).reshape(groups, wide, n)

    def body(in_ref, out_ref):
        col = lax.broadcasted_iota(jnp.int32, (n, wide), 1)
        row = lax.broadcasted_iota(jnp.int32, (n, wide), 0)
        pick = jnp.where(col // 16 == row, 1.0, 0.0).astype(BF)
        full = dot(in_ref[0], pick, 1, 0)
        r = lax.broadcasted_iota(jnp.int32, (wide, wide), 0)
        c = lax.broadcasted_iota(jnp.int32, (wide, wide), 1)
        out_ref[0] = jnp.where(r % 16 == c % 16, full, 0.0).astype(BF)

    return pl.pallas_call(
        body,
        grid=(groups,),
        in_specs=[pl.BlockSpec((1, wide, n), lambda g: (g, 0, 0))],
        out_specs=pl.BlockSpec((1, wide, wide), lambda g: (g, 0, 0)),
        out_shape=jax.ShapeDtypeStruct((groups, wide, wide), BF),
        compiler_params=params(),
        cost_estimate=cost(2 * groups * wide * wide * n, 2 * groups * wide * wide),
        name="spread_factor",
    )(turned)


def mix_second(plan, spread, cols, piece, back):
    n = plan.count
    wide = n * 16
    groups = plan.part // 16

    def body(m_ref, in_ref, out_ref):
        rows = in_ref[...].reshape(wide, plan.channels)
        got = dot(m_ref[0], rows, 0 if back else 1, 0).astype(BF)
        out_ref[...] = got.reshape(n, 16, plan.channels)

    out = pl.pallas_call(
        body,
        grid=(groups,),
        in_specs=[
            pl.BlockSpec((1, wide, wide), lambda g: (piece * groups + g, 0, 0)),
            pl.BlockSpec((n, 16, plan.channels), lambda g: (0, g, 0)),
        ],
        out_specs=pl.BlockSpec((n, 16, plan.channels), lambda g: (0, g, 0)),
        out_shape=jax.ShapeDtypeStruct((n, plan.part, plan.channels), BF),
        compiler_params=params(),
        cost_estimate=cost(
            2 * groups * wide * wide * plan.channels,
            4 * plan.rows * plan.channels + 2 * groups * wide * wide,
        ),
        name="mix_second_back" if back else "mix_second",
    )(spread, cols.reshape(n, plan.part, plan.channels))
    return out.reshape(plan.rows, plan.channels)


def grad_second(plan, grads, firsts, scale):
    n = plan.count
    wide = n * 16
    groups = plan.part // 16

    def body(g_ref, u_ref, out_ref):
        g = g_ref[...].reshape(wide, plan.channels)
        u = u_ref[...].reshape(wide, plan.channels)
        full = dot(g, u, 1, 1)
        r = lax.broadcasted_iota(jnp.int32, (wide, wide), 0)
        c = lax.broadcasted_iota(jnp.int32, (wide, wide), 1)
        kept = jnp.where(r % 16 == c % 16, full, 0.0)
        row = lax.broadcasted_iota(jnp.int32, (wide, n), 0)
        col = lax.broadcasted_iota(jnp.int32, (wide, n), 1)
        pick = jnp.where(row // 16 == col, 1.0, 0.0)
        out_ref[0] = dot(kept, pick, 1, 0, precision=lax.Precision.HIGHEST) * scale

    out = pl.pallas_call(
        body,
        grid=(groups,),
        in_specs=[pl.BlockSpec((n, 16, plan.channels), lambda g: (0, g, 0))] * 2,
        out_specs=pl.BlockSpec((1, wide, n), lambda g: (g, 0, 0)),
        out_shape=jax.ShapeDtypeStruct((groups, wide, n), F32),
        compiler_params=params(),
        cost_estimate=cost(
            2 * groups * wide * wide * plan.channels, 4 * plan.rows * plan.channels
        ),
        name="grad_second",
    )(
        grads.reshape(n, plan.part, plan.channels),
        firsts.reshape(n, plan.part, plan.channels),
    )
    return out.reshape(groups, n, 16, n).transpose(0, 2, 1, 3).reshape(plan.part, n, n)


def middle(plan, blocked, incoming, mixed, up_blocks, down_blocks, piece, before):
    groups, width, inner = up_blocks.shape
    sub = inner // groups
    step = min(256, plan.rows)

    def body(*refs):
        x_ref, g_ref, v_ref, up_ref, down_ref = refs[:5]
        dv_ref, r_ref, w_ref = refs[-3:]

        @pl.when(pl.program_id(0) == 0)
        def _():
            if before is None:
                w_ref[...] = jnp.zeros_like(w_ref)
            else:
                w_ref[...] = refs[5][...]

        x = rows_of(x_ref).astype(F32)
        g = rows_of(g_ref)
        v = v_ref[...].astype(F32)
        sx = sigmoid(x)
        gate = x * sx
        h = (x + v * gate).astype(BF)
        h_parts = [h[:, b * width : (b + 1) * width] for b in range(groups)]
        g_parts = [g[:, b * width : (b + 1) * width] for b in range(groups)]
        acts, slopes, back = [], [], []
        for b in range(groups):
            a = dot(h_parts[b], up_ref[b], 1, 0)
            s = sigmoid(a)
            q = a * s
            acts.append(q.astype(BF))
            slopes.append(s + q * (1.0 - s))
            back.append(dot(g_parts[b], down_ref[b], 1, 1))
        grads = []
        for b in range(groups):
            lanes = slice(b * sub, (b + 1) * sub)
            perm = jnp.concatenate([acts[p][:, lanes] for p in range(groups)], axis=1)
            w_ref[groups + b] += dot(g_parts[b], perm, 0, 0)
            dq = jnp.concatenate([back[p][:, lanes] for p in range(groups)], axis=1)
            da = (dq * slopes[b]).astype(BF)
            w_ref[b] += dot(h_parts[b], da, 0, 0)
            grads.append(dot(da, up_ref[b], 1, 1))
        dh = (g.astype(F32) + jnp.concatenate(grads, axis=1)).astype(BF).astype(F32)
        dv_ref[...] = (dh * gate).astype(BF)
        r_ref[...] = (dh * (1.0 + v * (sx + gate * (1.0 - sx)))).astype(BF)

    block = pl.BlockSpec((step, plan.channels), lambda i: (i, 0))
    full = pl.BlockSpec((2 * groups, width, inner), lambda i: (0, 0, 0))
    in_specs = [
        plan.spec(step, plan.channels, piece),
        plan.spec(step, plan.channels, piece),
        block,
        pl.BlockSpec(up_blocks.shape, lambda i: (0, 0, 0)),
        pl.BlockSpec(down_blocks.shape, lambda i: (0, 0, 0)),
    ]
    operands = [plan.view(blocked), plan.view(incoming), mixed, up_blocks, down_blocks]
    if before is not None:
        in_specs.append(full)
        operands.append(before)
    hidden = plan.rows * groups * inner
    return pl.pallas_call(
        body,
        grid=(plan.rows // step,),
        in_specs=in_specs,
        out_specs=[block, block, full],
        out_shape=[
            jax.ShapeDtypeStruct((plan.rows, plan.channels), BF),
            jax.ShapeDtypeStruct((plan.rows, plan.channels), BF),
            jax.ShapeDtypeStruct((2 * groups, width, inner), F32),
        ],
        compiler_params=params(),
        cost_estimate=cost(
            10 * hidden * width, 10 * plan.rows * plan.channels + 8 * groups * width * inner, hidden
        ),
        name="middle",
    )(*operands)


def finish(plan, factor, grad_firsts, blocked, gate_grads, piece, scale, rows_before, sum_before):
    last = piece == plan.pieces - 1
    step = min(256, plan.block)
    n_gates = plan.pieces if last else 0

    def body(*refs):
        factor_ref, d_ref, x_ref = refs[:3]
        one_ref, out_ref = refs[-2:]
        d = d_ref[...]
        one = dot(d, x_ref[...], 1, 1) * scale
        one_ref[...] = one.reshape(one_ref.shape)
        total = dot(rows_of(factor_ref), d, 0, 0)
        at = 3
        if piece > 0:
            total = total + refs[4][...]
            at = 5
        if last:
            if plan.pieces == 1:
                out_ref[...] = (total + refs[at][...].astype(F32)).astype(BF)
            else:
                total = total.reshape(step // plan.here, plan.pieces, plan.part, plan.channels)
                for q in range(plan.pieces):
                    got = (total[:, q] + refs[at + q][...].astype(F32)).astype(BF)
                    out_ref[:, q] = got
        else:
            out_ref[...] = total

    wide = pl.BlockSpec((step, plan.channels), lambda i: (i, 0))
    in_specs = [
        plan.spec(plan.rows, step, piece, lambda i: (0, i)),
        pl.BlockSpec((plan.rows, plan.channels), lambda i: (0, 0)),
        wide,
    ]
    operands = [plan.view(factor), grad_firsts, blocked]
    aliases = {}
    if piece > 0:
        in_specs += [pl.BlockSpec(memory_space=pl.ANY), wide]
        operands += [rows_before, sum_before]
        aliases = {3: 0}
    if last:
        if plan.pieces == 1:
            in_specs.append(wide)
            operands += gate_grads
            out_spec = wide
            out_shape = (plan.block, plan.channels)
        else:
            in_specs += [
                pl.BlockSpec((step // plan.here, plan.part, plan.channels), lambda i: (i, 0, 0))
            ] * n_gates
            operands += [r.reshape(plan.count, plan.part, plan.channels) for r in gate_grads]
            out_spec = pl.BlockSpec(
                (step // plan.here, plan.pieces, plan.part, plan.channels), lambda i: (i, 0, 0, 0)
            )
            out_shape = (plan.count, plan.pieces, plan.part, plan.channels)
    else:
        out_spec = wide
        out_shape = (plan.block, plan.channels)
    one_shape = (plan.block, plan.block)
    if plan.pieces > 1:
        one_shape = (plan.count, plan.pieces, plan.part, plan.block)
    return pl.pallas_call(
        body,
        grid=(plan.block // step,),
        in_specs=in_specs,
        out_specs=[plan.spec(plan.rows, step, piece, lambda i: (0, i)), out_spec],
        out_shape=[
            jax.ShapeDtypeStruct(one_shape, F32),
            jax.ShapeDtypeStruct(out_shape, BF if last else F32),
        ],
        input_output_aliases=aliases,
        compiler_params=params(),
        cost_estimate=cost(
            4 * plan.rows * plan.block * plan.channels,
            6 * plan.rows * plan.block + 8 * plan.block * plan.channels,
        ),
        name="finish",
    )(*operands)


def sum_over(values, count):
    if count & (count - 1) or values.shape[0] % count:
        return lax.psum(values, "seq")
    me = lax.axis_index("seq")
    total = values
    steps = [1 << s for s in range(count.bit_length() - 1)]
    for step in steps:
        halves = total.reshape(2, total.shape[0] // 2, total.shape[1])
        mine = (me // step) % 2
        keep = lax.dynamic_index_in_dim(halves, mine, 0, keepdims=False)
        send = lax.dynamic_index_in_dim(halves, 1 - mine, 0, keepdims=False).astype(BF)
        got = lax.ppermute(send, "seq", [(i, i ^ step) for i in range(count)])
        total = keep + got.astype(F32)
    total = total.astype(BF)
    for step in reversed(steps):
        mine = (me // step) % 2
        got = lax.ppermute(total, "seq", [(i, i ^ step) for i in range(count)])
        low = jnp.where(mine == 0, total, got)
        high = jnp.where(mine == 0, got, total)
        total = jnp.concatenate([low, high], axis=0)
    return total


def write_weights(total, up_shape, down_shape, scale):
    groups, width, inner = up_shape

    def body(up_in, down_in, up_ref, down_ref):
        up_ref[0] = up_in[...].astype(F32) * scale
        down_ref[0] = (down_in[...].astype(F32) * scale).T

    return pl.pallas_call(
        body,
        grid=(groups,),
        in_specs=[
            pl.BlockSpec((width, inner), lambda b: (b, 0)),
            pl.BlockSpec((width, inner), lambda b: (groups + b, 0)),
        ],
        out_specs=[
            pl.BlockSpec((1, width, inner), lambda b: (b, 0, 0)),
            pl.BlockSpec((1, inner, width), lambda b: (b, 0, 0)),
        ],
        out_shape=[
            jax.ShapeDtypeStruct(up_shape, F32),
            jax.ShapeDtypeStruct(down_shape, F32),
        ],
        compiler_params=params(),
        cost_estimate=cost(groups * width * inner, 12 * groups * width * inner),
        name="write_weights",
    )(total, total)


def on_device(tokens, cotangent, factor_one, factor_two, up_blocks, down_blocks):
    count = lax.axis_size("seq")
    block, channels = factor_one.shape[1], tokens.shape[1]
    plan = Plan(count, block, channels)
    scale = float(count * tokens.shape[0]) ** (-0.5)
    factor = factor_one.reshape(block, block)
    pieces = range(plan.pieces)

    def exchange(rows):
        cut = rows.reshape(count, plan.part, channels)
        got = lax.all_to_all(cut, "seq", split_axis=0, concat_axis=0, tiled=True)
        return got.reshape(plan.rows, channels)

    if plan.grouped:
        spread = spread_factor(plan, factor_two)

    def second(cols, piece, back):
        if plan.grouped:
            return mix_second(plan, spread, cols, piece, back)
        cut = cols.reshape(count, plan.part, channels)
        names = "kmj,mkc->jkc" if back else "kmj,jkc->mkc"
        got = jnp.einsum(names, factor_two, cut, preferred_element_type=F32).astype(BF)
        return got.reshape(plan.rows, channels)

    def second_grad(grads, firsts):
        if plan.grouped:
            return grad_second(plan, grads, firsts, scale)
        shape = (count, plan.part, channels)
        got = jnp.einsum(
            "mkc,jkc->kmj", grads.reshape(shape), firsts.reshape(shape), preferred_element_type=F32
        )
        return got * scale

    firsts = [exchange(mix_first(plan, factor, tokens, q)) for q in pieces]
    mixed = [exchange(second(firsts[q], q, False)) for q in pieces]
    weights = None
    grad_mixed, gate_grads = [], []
    for q in pieces:
        dv, r, weights = middle(
            plan, tokens, cotangent, mixed[q], up_blocks, down_blocks, q, weights
        )
        grad_mixed.append(exchange(dv))
        gate_grads.append(r)
    grad_firsts = [exchange(second(grad_mixed[q], q, True)) for q in pieces]
    two = [second_grad(grad_mixed[q], firsts[q]) for q in pieces]
    total = sum_over(weights.reshape(-1, weights.shape[-1]), count)
    grad_up, grad_down = write_weights(total, up_blocks.shape, down_blocks.shape, scale)
    one, tokens_sum = None, None
    for q in pieces:
        one, tokens_sum = finish(
            plan, factor, grad_firsts[q], tokens, gate_grads, q, scale, one, tokens_sum
        )
    return (
        tokens_sum.reshape(tokens.shape),
        one.reshape(1, block, block),
        jnp.concatenate(two, axis=0),
        grad_up,
        grad_down,
    )


def solution(mesh):
    return jax.shard_map(
        on_device,
        mesh=mesh,
        in_specs=(
            P(("grp", "seq"), None),
            P(("grp", "seq"), None),
            P("seq", None, None),
            P("seq", None, None),
            P(),
            P(),
        ),
        out_specs=(
            P(("grp", "seq"), None),
            P(("grp", "seq"), None, None),
            P(("grp", "seq"), None, None),
            P("grp", None, None),
            P("grp", None, None),
        ),
        check_vma=False,
    )
```

```python
import jax
import jax.numpy as jnp
from jax import lax
from jax.experimental import pallas as pl
from jax.experimental.pallas import tpu as pltpu
from jax.sharding import PartitionSpec as P

BF = jnp.bfloat16
F32 = jnp.float32
PIECES = 1
VMEM_BYTES = 60 * 1024 * 1024
SCALAR = pl.BlockSpec(memory_space=pltpu.SMEM)


def sigmoid(z):
    return 0.5 + 0.5 * jnp.tanh(0.5 * z)


def dot(a, b, ca, cb, **kw):
    return lax.dot_general(a, b, (((ca,), (cb,)), ((), ())), preferred_element_type=F32, **kw)


def rows_of(ref):
    value = ref[...]
    return value.reshape(-1, value.shape[-1])


def params(steps=1):
    return pltpu.CompilerParams(
        dimension_semantics=("arbitrary",) * steps, vmem_limit_bytes=VMEM_BYTES
    )


def cost(flops, moved, trans=0):
    return pl.CostEstimate(flops=int(flops), bytes_accessed=int(moved), transcendentals=int(trans))


class Plan:
    def __init__(self, count, block, channels):
        self.count = count
        self.block = block
        self.channels = channels
        self.here = block // count
        self.pieces = PIECES if self.here % (16 * PIECES) == 0 else 1
        self.part = self.here // self.pieces
        self.rows = block // self.pieces
        self.grouped = self.part % 16 == 0
        self.direct = self.grouped and count <= 16
        self.arrays = count if self.direct else 1
        self.block_shape = (self.part, channels) if self.direct else (count, self.part, channels)

    def block_specs(self):
        return [
            pl.BlockSpec(self.block_shape, lambda i: (0,) * len(self.block_shape))
        ] * self.arrays

    def block_shapes(self):
        return [jax.ShapeDtypeStruct(self.block_shape, BF)] * self.arrays

    def whole(self):
        return pltpu.VMEM((self.count, self.part, self.channels), BF)

    def view(self, array):
        if self.pieces == 1:
            return array
        return array.reshape(self.count, self.pieces, self.part, array.shape[-1])

    def spec(self, rows, columns, piece, index=lambda i: (i, 0)):
        if self.pieces == 1:
            return pl.BlockSpec((rows, columns), index)

        def whole(i):
            at, col = index(i)
            return (at, piece, 0, col)

        return pl.BlockSpec((rows // self.part, 1, self.part, columns), whole)


def assemble(refs, whole, me):
    if len(refs) == 1:
        whole[...] = refs[0][...]
    else:
        for s, ref in enumerate(refs):
            whole[me ^ s] = ref[...]


def hand_out(whole, refs, me):
    if len(refs) == 1:
        refs[0][...] = whole[...]
    else:
        for s, ref in enumerate(refs):
            ref[...] = whole[me ^ s]


def mix_first(plan, me, factor, blocked, piece):
    step = min(256, plan.rows)
    last = plan.rows // step - 1

    def body(me_ref, factor_ref, x_ref, *rest):
        outs, whole = rest[:-1], rest[-1]
        i = pl.program_id(0)
        got = dot(rows_of(factor_ref), x_ref[...], 1, 0).astype(BF)
        whole[pl.ds(i * (step // plan.part), step // plan.part)] = got.reshape(
            step // plan.part, plan.part, plan.channels
        )

        @pl.when(i == last)
        def _():
            hand_out(whole, outs, me_ref[0])

    return pl.pallas_call(
        body,
        grid=(last + 1,),
        in_specs=[
            SCALAR,
            plan.spec(step, plan.block, piece),
            pl.BlockSpec((plan.block, plan.channels), lambda i: (0, 0)),
        ],
        out_specs=plan.block_specs(),
        out_shape=plan.block_shapes(),
        scratch_shapes=[plan.whole()],
        compiler_params=params(),
        cost_estimate=cost(
            2 * plan.rows * plan.block * plan.channels,
            2 * (plan.rows * plan.block + 2 * plan.block * plan.channels),
        ),
        name="mix_first",
    )(me, plan.view(factor), blocked)


def spread_factor(plan, factor_two):
    n = plan.count
    groups = plan.here // 16
    wide = n * 16
    turned = factor_two.reshape(groups, 16, n, n).transpose(0, 2, 1, 3).reshape(groups, wide, n)

    def body(in_ref, out_ref):
        col = lax.broadcasted_iota(jnp.int32, (n, wide), 1)
        row = lax.broadcasted_iota(jnp.int32, (n, wide), 0)
        pick = jnp.where(col // 16 == row, 1.0, 0.0).astype(BF)
        r = lax.broadcasted_iota(jnp.int32, (wide, wide), 0)
        c = lax.broadcasted_iota(jnp.int32, (wide, wide), 1)
        same = r % 16 == c % 16
        for g in range(groups):
            full = dot(in_ref[g], pick, 1, 0)
            out_ref[g] = jnp.where(same, full, 0.0).astype(BF)

    return pl.pallas_call(
        body,
        out_shape=jax.ShapeDtypeStruct((groups, wide, wide), BF),
        compiler_params=params(0),
        cost_estimate=cost(2 * groups * wide * wide * n, 2 * groups * wide * wide),
        name="spread_factor",
    )(turned)


def mix_second(plan, me, spread, cols, piece, back):
    n = plan.count
    wide = n * 16
    groups = plan.part // 16
    number = plan.arrays

    def body(me_ref, m_ref, *rest):
        ins, outs, (whole, made) = rest[:number], rest[number : 2 * number], rest[2 * number :]
        assemble(ins, whole, me_ref[0])
        for g in range(groups):
            at = slice(g * 16, (g + 1) * 16)
            rows = whole[:, at, :].reshape(wide, plan.channels)
            got = dot(m_ref[g], rows, 0 if back else 1, 0).astype(BF)
            made[:, at, :] = got.reshape(n, 16, plan.channels)
        hand_out(made, outs, me_ref[0])

    return pl.pallas_call(
        body,
        grid=(1,),
        in_specs=[SCALAR, pl.BlockSpec((groups, wide, wide), lambda i: (piece, 0, 0))]
        + plan.block_specs(),
        out_specs=plan.block_specs(),
        out_shape=plan.block_shapes(),
        scratch_shapes=[plan.whole(), plan.whole()],
        compiler_params=params(),
        cost_estimate=cost(
            2 * groups * wide * wide * plan.channels,
            4 * plan.rows * plan.channels + 2 * groups * wide * wide,
        ),
        name="mix_second_back" if back else "mix_second",
    )(me, spread, *cols)


def grad_second(plan, me, grads, firsts, scale):
    n = plan.count
    wide = n * 16
    groups = plan.part // 16
    number = plan.arrays

    def body(me_ref, *rest):
        out_ref, gs, us = rest[2 * number :]
        assemble(rest[:number], gs, me_ref[0])
        assemble(rest[number : 2 * number], us, me_ref[0])
        r = lax.broadcasted_iota(jnp.int32, (wide, wide), 0)
        c = lax.broadcasted_iota(jnp.int32, (wide, wide), 1)
        same = r % 16 == c % 16
        row = lax.broadcasted_iota(jnp.int32, (wide, n), 0)
        col = lax.broadcasted_iota(jnp.int32, (wide, n), 1)
        pick = jnp.where(row // 16 == col, 1.0, 0.0)
        for g in range(groups):
            at = slice(g * 16, (g + 1) * 16)
            full = dot(
                gs[:, at, :].reshape(wide, plan.channels),
                us[:, at, :].reshape(wide, plan.channels),
                1,
                1,
            )
            kept = jnp.where(same, full, 0.0)
            out_ref[g] = dot(kept, pick, 1, 0, precision=lax.Precision.HIGHEST) * scale

    out = pl.pallas_call(
        body,
        grid=(1,),
        in_specs=[SCALAR] + plan.block_specs() + plan.block_specs(),
        out_specs=pl.BlockSpec((groups, wide, n), lambda i: (0, 0, 0)),
        out_shape=jax.ShapeDtypeStruct((groups, wide, n), F32),
        scratch_shapes=[plan.whole(), plan.whole()],
        compiler_params=params(),
        cost_estimate=cost(
            2 * groups * wide * wide * plan.channels, 4 * plan.rows * plan.channels
        ),
        name="grad_second",
    )(me, *grads, *firsts)
    return out.reshape(groups, n, 16, n).transpose(0, 2, 1, 3).reshape(plan.part, n, n)


def middle(plan, me, blocked, incoming, mixed, up_blocks, down_blocks, piece, before):
    groups, width, inner = up_blocks.shape
    sub = inner // groups
    step = min(256, plan.rows)
    last = plan.rows // step - 1
    number = plan.arrays
    devices = step // plan.part

    def body(me_ref, x_ref, g_ref, up_ref, down_ref, *rest):
        mixed_refs, rest = rest[:number], rest[number:]
        if before is not None:
            before_ref, rest = rest[0], rest[1:]
        r_ref, w_ref = rest[:2]
        outs, (v_all, dv_all) = rest[2 : 2 + number], rest[2 + number :]
        i = pl.program_id(0)

        @pl.when(i == 0)
        def _():
            assemble(mixed_refs, v_all, me_ref[0])
            if before is None:
                w_ref[...] = jnp.zeros_like(w_ref)
            else:
                w_ref[...] = before_ref[...]

        here = pl.ds(i * devices, devices)
        x = rows_of(x_ref).astype(F32)
        g = rows_of(g_ref)
        v = v_all[here].reshape(step, plan.channels).astype(F32)
        sx = sigmoid(x)
        gate = x * sx
        h = (x + v * gate).astype(BF)
        h_parts = [h[:, b * width : (b + 1) * width] for b in range(groups)]
        g_parts = [g[:, b * width : (b + 1) * width] for b in range(groups)]
        acts, slopes, back = [], [], []
        for b in range(groups):
            a = dot(h_parts[b], up_ref[b], 1, 0)
            s = sigmoid(a)
            q = a * s
            acts.append(q.astype(BF))
            slopes.append(s + q * (1.0 - s))
            back.append(dot(g_parts[b], down_ref[b], 1, 1))
        grads = []
        for b in range(groups):
            lanes = slice(b * sub, (b + 1) * sub)
            perm = jnp.concatenate([acts[p][:, lanes] for p in range(groups)], axis=1)
            w_ref[groups + b] += dot(g_parts[b], perm, 0, 0)
            dq = jnp.concatenate([back[p][:, lanes] for p in range(groups)], axis=1)
            da = (dq * slopes[b]).astype(BF)
            w_ref[b] += dot(h_parts[b], da, 0, 0)
            grads.append(dot(da, up_ref[b], 1, 1))
        dh = (g.astype(F32) + jnp.concatenate(grads, axis=1)).astype(BF).astype(F32)
        dv_all[here] = (dh * gate).astype(BF).reshape(devices, plan.part, plan.channels)
        r_ref[...] = (dh * (1.0 + v * (sx + gate * (1.0 - sx)))).astype(BF)

        @pl.when(i == last)
        def _():
            hand_out(dv_all, outs, me_ref[0])

    block = pl.BlockSpec((step, plan.channels), lambda i: (i, 0))
    full = pl.BlockSpec((2 * groups, width, inner), lambda i: (0, 0, 0))
    in_specs = [
        SCALAR,
        plan.spec(step, plan.channels, piece),
        plan.spec(step, plan.channels, piece),
        pl.BlockSpec(up_blocks.shape, lambda i: (0, 0, 0)),
        pl.BlockSpec(down_blocks.shape, lambda i: (0, 0, 0)),
    ] + plan.block_specs()
    operands = [me, plan.view(blocked), plan.view(incoming), up_blocks, down_blocks, *mixed]
    if before is not None:
        in_specs.append(full)
        operands.append(before)
    hidden = plan.rows * groups * inner
    got = pl.pallas_call(
        body,
        grid=(last + 1,),
        in_specs=in_specs,
        out_specs=[block, full] + plan.block_specs(),
        out_shape=[
            jax.ShapeDtypeStruct((plan.rows, plan.channels), BF),
            jax.ShapeDtypeStruct((2 * groups, width, inner), F32),
        ]
        + plan.block_shapes(),
        scratch_shapes=[plan.whole(), plan.whole()],
        compiler_params=params(),
        cost_estimate=cost(
            10 * hidden * width, 10 * plan.rows * plan.channels + 8 * groups * width * inner, hidden
        ),
        name="middle",
    )(*operands)
    return got[2:], got[0], got[1]


def finish(plan, me, factor, grad_firsts, blocked, gate_grads, piece, scale, rows_before, sum_before):
    final = piece == plan.pieces - 1
    step = min(256, plan.block)
    n_gates = plan.pieces if final else 0
    number = plan.arrays

    def body(*refs):
        me_ref, factor_ref, x_ref = refs[:3]
        ins = refs[3 : 3 + number]
        others = refs[3 + number : -3]
        one_ref, out_ref, d_all = refs[-3:]

        @pl.when(pl.program_id(0) == 0)
        def _():
            assemble(ins, d_all, me_ref[0])

        d = d_all[...].reshape(plan.rows, plan.channels)
        one = dot(d, x_ref[...], 1, 1) * scale
        one_ref[...] = one.reshape(one_ref.shape)
        total = dot(rows_of(factor_ref), d, 0, 0)
        if piece > 0:
            total = total + others[1][...]
            others = others[2:]
        if final:
            if plan.pieces == 1:
                out_ref[...] = (total + others[0][...].astype(F32)).astype(BF)
            else:
                total = total.reshape(step // plan.here, plan.pieces, plan.part, plan.channels)
                for q in range(plan.pieces):
                    out_ref[:, q] = (total[:, q] + others[q][...].astype(F32)).astype(BF)
        else:
            out_ref[...] = total

    wide = pl.BlockSpec((step, plan.channels), lambda i: (i, 0))
    in_specs = [SCALAR, plan.spec(plan.rows, step, piece, lambda i: (0, i)), wide]
    in_specs += plan.block_specs()
    operands = [me, plan.view(factor), blocked, *grad_firsts]
    aliases = {}
    if piece > 0:
        aliases = {len(operands): 0}
        in_specs += [pl.BlockSpec(memory_space=pl.ANY), wide]
        operands += [rows_before, sum_before]
    out_spec, out_shape = wide, (plan.block, plan.channels)
    if final and plan.pieces == 1:
        in_specs.append(wide)
        operands += gate_grads
    elif final:
        in_specs += [
            pl.BlockSpec((step // plan.here, plan.part, plan.channels), lambda i: (i, 0, 0))
        ] * n_gates
        operands += [r.reshape(plan.count, plan.part, plan.channels) for r in gate_grads]
        out_spec = pl.BlockSpec(
            (step // plan.here, plan.pieces, plan.part, plan.channels), lambda i: (i, 0, 0, 0)
        )
        out_shape = (plan.count, plan.pieces, plan.part, plan.channels)
    one_shape = (plan.block, plan.block)
    if plan.pieces > 1:
        one_shape = (plan.count, plan.pieces, plan.part, plan.block)
    return pl.pallas_call(
        body,
        grid=(plan.block // step,),
        in_specs=in_specs,
        out_specs=[plan.spec(plan.rows, step, piece, lambda i: (0, i)), out_spec],
        out_shape=[
            jax.ShapeDtypeStruct(one_shape, F32),
            jax.ShapeDtypeStruct(out_shape, BF if final else F32),
        ],
        scratch_shapes=[plan.whole()],
        input_output_aliases=aliases,
        compiler_params=params(),
        cost_estimate=cost(
            4 * plan.rows * plan.block * plan.channels,
            6 * plan.rows * plan.block + 8 * plan.block * plan.channels,
        ),
        name="finish",
    )(*operands)


def sum_over(values, count):
    if count & (count - 1) or values.shape[0] % count:
        return lax.psum(values, "seq")
    me = lax.axis_index("seq")
    total = values
    steps = [1 << s for s in range(count.bit_length() - 1)]
    for step in steps:
        halves = total.reshape(2, total.shape[0] // 2, total.shape[1])
        mine = (me // step) % 2
        keep = lax.dynamic_index_in_dim(halves, mine, 0, keepdims=False)
        send = lax.dynamic_index_in_dim(halves, 1 - mine, 0, keepdims=False).astype(BF)
        got = lax.ppermute(send, "seq", [(i, i ^ step) for i in range(count)])
        total = keep + got.astype(F32)
    total = total.astype(BF)
    for step in reversed(steps):
        mine = (me // step) % 2
        got = lax.ppermute(total, "seq", [(i, i ^ step) for i in range(count)])
        low = jnp.where(mine == 0, total, got)
        high = jnp.where(mine == 0, got, total)
        total = jnp.concatenate([low, high], axis=0)
    return total


def write_weights(total, up_shape, down_shape, scale):
    groups, width, inner = up_shape

    def body(up_in, down_in, up_ref, down_ref):
        up_ref[0] = up_in[...].astype(F32) * scale
        down_ref[0] = (down_in[...].astype(F32) * scale).T

    return pl.pallas_call(
        body,
        grid=(groups,),
        in_specs=[
            pl.BlockSpec((width, inner), lambda b: (b, 0)),
            pl.BlockSpec((width, inner), lambda b: (groups + b, 0)),
        ],
        out_specs=[
            pl.BlockSpec((1, width, inner), lambda b: (b, 0, 0)),
            pl.BlockSpec((1, inner, width), lambda b: (b, 0, 0)),
        ],
        out_shape=[
            jax.ShapeDtypeStruct(up_shape, F32),
            jax.ShapeDtypeStruct(down_shape, F32),
        ],
        compiler_params=params(),
        cost_estimate=cost(groups * width * inner, 12 * groups * width * inner),
        name="write_weights",
    )(total, total)


def on_device(tokens, cotangent, factor_one, factor_two, up_blocks, down_blocks):
    count = lax.axis_size("seq")
    block, channels = factor_one.shape[1], tokens.shape[1]
    plan = Plan(count, block, channels)
    scale = float(count * tokens.shape[0]) ** (-0.5)
    factor = factor_one.reshape(block, block)
    pieces = range(plan.pieces)

    me = lax.axis_index("seq").astype(jnp.int32).reshape(1)

    def exchange(blocks):
        if not plan.direct:
            return [lax.all_to_all(blocks[0], "seq", split_axis=0, concat_axis=0, tiled=True)]
        return [blocks[0]] + [
            lax.ppermute(blocks[s], "seq", [(i, i ^ s) for i in range(count)])
            for s in range(1, count)
        ]

    if plan.grouped:
        spread = spread_factor(plan, factor_two)

    def second(cols, piece, back):
        if plan.grouped:
            return mix_second(plan, me, spread, cols, piece, back)
        names = "kmj,mkc->jkc" if back else "kmj,jkc->mkc"
        return [jnp.einsum(names, factor_two, cols[0], preferred_element_type=F32).astype(BF)]

    def second_grad(grads, firsts):
        if plan.grouped:
            return grad_second(plan, me, grads, firsts, scale)
        got = jnp.einsum("mkc,jkc->kmj", grads[0], firsts[0], preferred_element_type=F32)
        return got * scale

    firsts = [exchange(mix_first(plan, me, factor, tokens, q)) for q in pieces]
    mixed = [exchange(second(firsts[q], q, False)) for q in pieces]
    weights = None
    grad_mixed, gate_grads = [], []
    for q in pieces:
        dv, r, weights = middle(
            plan, me, tokens, cotangent, mixed[q], up_blocks, down_blocks, q, weights
        )
        grad_mixed.append(exchange(dv))
        gate_grads.append(r)
    grad_firsts = [exchange(second(grad_mixed[q], q, True)) for q in pieces]
    two = [second_grad(grad_mixed[q], firsts[q]) for q in pieces]
    total = sum_over(weights.reshape(-1, weights.shape[-1]), count)
    grad_up, grad_down = write_weights(total, up_blocks.shape, down_blocks.shape, scale)
    one, tokens_sum = None, None
    for q in pieces:
        one, tokens_sum = finish(
            plan, me, factor, grad_firsts[q], tokens, gate_grads, q, scale, one, tokens_sum
        )
    return (
        tokens_sum.reshape(tokens.shape),
        one.reshape(1, block, block),
        jnp.concatenate(two, axis=0),
        grad_up,
        grad_down,
    )


def solution(mesh):
    return jax.shard_map(
        on_device,
        mesh=mesh,
        in_specs=(
            P(("grp", "seq"), None),
            P(("grp", "seq"), None),
            P("seq", None, None),
            P("seq", None, None),
            P(),
            P(),
        ),
        out_specs=(
            P(("grp", "seq"), None),
            P(("grp", "seq"), None, None),
            P(("grp", "seq"), None, None),
            P("grp", None, None),
            P("grp", None, None),
        ),
        check_vma=False,
    )
```

```python
import jax
import jax.numpy as jnp
from jax import lax
from jax.experimental import pallas as pl
from jax.experimental.pallas import tpu as pltpu
from jax.sharding import PartitionSpec as P

BF = jnp.bfloat16
F32 = jnp.float32
PIECES = 1
VMEM_BYTES = 40 * 1024 * 1024


def sigmoid(z):
    return 0.5 + 0.5 * jnp.tanh(0.5 * z)


def dot(a, b, ca, cb, **kw):
    return lax.dot_general(a, b, (((ca,), (cb,)), ((), ())), preferred_element_type=F32, **kw)


def rows_of(ref):
    value = ref[...]
    return value.reshape(-1, value.shape[-1])


def params(steps=1):
    return pltpu.CompilerParams(
        dimension_semantics=("arbitrary",) * steps, vmem_limit_bytes=VMEM_BYTES
    )


def cost(flops, moved, trans=0):
    return pl.CostEstimate(flops=int(flops), bytes_accessed=int(moved), transcendentals=int(trans))


class Plan:
    def __init__(self, count, block, channels):
        self.count = count
        self.block = block
        self.channels = channels
        self.here = block // count
        self.pieces = PIECES if self.here % (16 * PIECES) == 0 else 1
        self.part = self.here // self.pieces
        self.rows = block // self.pieces
        self.grouped = self.part % 16 == 0

    def view(self, array):
        if self.pieces == 1:
            return array
        return array.reshape(self.count, self.pieces, self.part, array.shape[-1])

    def spec(self, rows, columns, piece, index=lambda i: (i, 0)):
        if self.pieces == 1:
            return pl.BlockSpec((rows, columns), index)

        def whole(i):
            at, col = index(i)
            return (at, piece, 0, col)

        return pl.BlockSpec((rows // self.part, 1, self.part, columns), whole)


def mix_first(plan, factor, blocked, piece):
    def body(factor_ref, x_ref, out_ref):
        out_ref[...] = dot(rows_of(factor_ref), x_ref[...], 1, 0).astype(BF)

    step = min(256, plan.rows)
    return pl.pallas_call(
        body,
        grid=(plan.rows // step,),
        in_specs=[
            plan.spec(step, plan.block, piece),
            pl.BlockSpec((plan.block, plan.channels), lambda i: (0, 0)),
        ],
        out_specs=pl.BlockSpec((step, plan.channels), lambda i: (i, 0)),
        out_shape=jax.ShapeDtypeStruct((plan.rows, plan.channels), BF),
        compiler_params=params(),
        cost_estimate=cost(
            2 * plan.rows * plan.block * plan.channels,
            2 * (plan.rows * plan.block + 2 * plan.block * plan.channels),
        ),
        name="mix_first",
    )(plan.view(factor), blocked)


def spread_factor(plan, factor_two):
    n = plan.count
    groups = plan.here // 16
    wide = n * 16
    turned = factor_two.reshape(groups, 16, n, n).transpose(0, 2, 1, 3).reshape(groups, wide, n)

    def body(in_ref, out_ref):
        col = lax.broadcasted_iota(jnp.int32, (n, wide), 1)
        row = lax.broadcasted_iota(jnp.int32, (n, wide), 0)
        pick = jnp.where(col // 16 == row, 1.0, 0.0).astype(BF)
        full = dot(in_ref[0], pick, 1, 0)
        r = lax.broadcasted_iota(jnp.int32, (wide, wide), 0)
        c = lax.broadcasted_iota(jnp.int32, (wide, wide), 1)
        out_ref[0] = jnp.where(r % 16 == c % 16, full, 0.0).astype(BF)

    return pl.pallas_call(
        body,
        grid=(groups,),
        in_specs=[pl.BlockSpec((1, wide, n), lambda g: (g, 0, 0))],
        out_specs=pl.BlockSpec((1, wide, wide), lambda g: (g, 0, 0)),
        out_shape=jax.ShapeDtypeStruct((groups, wide, wide), BF),
        compiler_params=params(),
        cost_estimate=cost(2 * groups * wide * wide * n, 2 * groups * wide * wide),
        name="spread_factor",
    )(turned)


def mix_second(plan, spread, cols, piece, back):
    n = plan.count
    wide = n * 16
    groups = plan.part // 16

    def body(m_ref, in_ref, out_ref):
        rows = in_ref[...].reshape(wide, plan.channels)
        got = dot(m_ref[0], rows, 0 if back else 1, 0).astype(BF)
        out_ref[...] = got.reshape(n, 16, plan.channels)

    out = pl.pallas_call(
        body,
        grid=(groups,),
        in_specs=[
            pl.BlockSpec((1, wide, wide), lambda g: (piece * groups + g, 0, 0)),
            pl.BlockSpec((n, 16, plan.channels), lambda g: (0, g, 0)),
        ],
        out_specs=pl.BlockSpec((n, 16, plan.channels), lambda g: (0, g, 0)),
        out_shape=jax.ShapeDtypeStruct((n, plan.part, plan.channels), BF),
        compiler_params=params(),
        cost_estimate=cost(
            2 * groups * wide * wide * plan.channels,
            4 * plan.rows * plan.channels + 2 * groups * wide * wide,
        ),
        name="mix_second_back" if back else "mix_second",
    )(spread, cols.reshape(n, plan.part, plan.channels))
    return out.reshape(plan.rows, plan.channels)


def grad_second(plan, grads, firsts, scale):
    n = plan.count
    wide = n * 16
    groups = plan.part // 16

    def body(g_ref, u_ref, out_ref):
        g = g_ref[...].reshape(wide, plan.channels)
        u = u_ref[...].reshape(wide, plan.channels)
        full = dot(g, u, 1, 1)
        r = lax.broadcasted_iota(jnp.int32, (wide, wide), 0)
        c = lax.broadcasted_iota(jnp.int32, (wide, wide), 1)
        kept = jnp.where(r % 16 == c % 16, full, 0.0)
        row = lax.broadcasted_iota(jnp.int32, (wide, n), 0)
        col = lax.broadcasted_iota(jnp.int32, (wide, n), 1)
        pick = jnp.where(row // 16 == col, 1.0, 0.0)
        out_ref[0] = dot(kept, pick, 1, 0, precision=lax.Precision.HIGHEST) * scale

    out = pl.pallas_call(
        body,
        grid=(groups,),
        in_specs=[pl.BlockSpec((n, 16, plan.channels), lambda g: (0, g, 0))] * 2,
        out_specs=pl.BlockSpec((1, wide, n), lambda g: (g, 0, 0)),
        out_shape=jax.ShapeDtypeStruct((groups, wide, n), F32),
        compiler_params=params(),
        cost_estimate=cost(
            2 * groups * wide * wide * plan.channels, 4 * plan.rows * plan.channels
        ),
        name="grad_second",
    )(
        grads.reshape(n, plan.part, plan.channels),
        firsts.reshape(n, plan.part, plan.channels),
    )
    return out.reshape(groups, n, 16, n).transpose(0, 2, 1, 3).reshape(plan.part, n, n)


def middle(plan, blocked, incoming, mixed, up_blocks, down_blocks, piece, before):
    groups, width, inner = up_blocks.shape
    sub = inner // groups
    step = min(256, plan.rows)

    def body(*refs):
        x_ref, g_ref, v_ref, up_ref, down_ref = refs[:5]
        dv_ref, r_ref, w_ref = refs[-3:]

        @pl.when(pl.program_id(0) == 0)
        def _():
            if before is None:
                w_ref[...] = jnp.zeros_like(w_ref)
            else:
                w_ref[...] = refs[5][...]

        x = rows_of(x_ref).astype(F32)
        g = rows_of(g_ref)
        v = v_ref[...].astype(F32)
        sx = sigmoid(x)
        gate = x * sx
        h = (x + v * gate).astype(BF)
        h_parts = [h[:, b * width : (b + 1) * width] for b in range(groups)]
        g_parts = [g[:, b * width : (b + 1) * width] for b in range(groups)]
        acts, slopes, back = [], [], []
        for b in range(groups):
            a = dot(h_parts[b], up_ref[b], 1, 0)
            s = sigmoid(a)
            q = a * s
            acts.append(q.astype(BF))
            slopes.append(s + q * (1.0 - s))
            back.append(dot(g_parts[b], down_ref[b], 1, 1))
        grads = []
        for b in range(groups):
            lanes = slice(b * sub, (b + 1) * sub)
            perm = jnp.concatenate([acts[p][:, lanes] for p in range(groups)], axis=1)
            w_ref[groups + b] += dot(g_parts[b], perm, 0, 0)
            dq = jnp.concatenate([back[p][:, lanes] for p in range(groups)], axis=1)
            da = (dq * slopes[b]).astype(BF)
            w_ref[b] += dot(h_parts[b], da, 0, 0)
            grads.append(dot(da, up_ref[b], 1, 1))
        dh = (g.astype(F32) + jnp.concatenate(grads, axis=1)).astype(BF).astype(F32)
        dv_ref[...] = (dh * gate).astype(BF)
        r_ref[...] = (dh * (1.0 + v * (sx + gate * (1.0 - sx)))).astype(BF)

    block = pl.BlockSpec((step, plan.channels), lambda i: (i, 0))
    full = pl.BlockSpec((2 * groups, width, inner), lambda i: (0, 0, 0))
    in_specs = [
        plan.spec(step, plan.channels, piece),
        plan.spec(step, plan.channels, piece),
        block,
        pl.BlockSpec(up_blocks.shape, lambda i: (0, 0, 0)),
        pl.BlockSpec(down_blocks.shape, lambda i: (0, 0, 0)),
    ]
    operands = [plan.view(blocked), plan.view(incoming), mixed, up_blocks, down_blocks]
    if before is not None:
        in_specs.append(full)
        operands.append(before)
    hidden = plan.rows * groups * inner
    return pl.pallas_call(
        body,
        grid=(plan.rows // step,),
        in_specs=in_specs,
        out_specs=[block, block, full],
        out_shape=[
            jax.ShapeDtypeStruct((plan.rows, plan.channels), BF),
            jax.ShapeDtypeStruct((plan.rows, plan.channels), BF),
            jax.ShapeDtypeStruct((2 * groups, width, inner), F32),
        ],
        compiler_params=params(),
        cost_estimate=cost(
            10 * hidden * width, 10 * plan.rows * plan.channels + 8 * groups * width * inner, hidden
        ),
        name="middle",
    )(*operands)


def finish(plan, factor, grad_firsts, blocked, gate_grads, piece, scale, rows_before, sum_before):
    last = piece == plan.pieces - 1
    step = min(256, plan.block)
    n_gates = plan.pieces if last else 0

    def body(*refs):
        factor_ref, d_ref, x_ref = refs[:3]
        one_ref, out_ref = refs[-2:]
        d = d_ref[...]
        one = dot(d, x_ref[...], 1, 1) * scale
        one_ref[...] = one.reshape(one_ref.shape)
        total = dot(rows_of(factor_ref), d, 0, 0)
        at = 3
        if piece > 0:
            total = total + refs[4][...]
            at = 5
        if last:
            if plan.pieces == 1:
                out_ref[...] = (total + refs[at][...].astype(F32)).astype(BF)
            else:
                total = total.reshape(step // plan.here, plan.pieces, plan.part, plan.channels)
                for q in range(plan.pieces):
                    got = (total[:, q] + refs[at + q][...].astype(F32)).astype(BF)
                    out_ref[:, q] = got
        else:
            out_ref[...] = total

    wide = pl.BlockSpec((step, plan.channels), lambda i: (i, 0))
    in_specs = [
        plan.spec(plan.rows, step, piece, lambda i: (0, i)),
        pl.BlockSpec((plan.rows, plan.channels), lambda i: (0, 0)),
        wide,
    ]
    operands = [plan.view(factor), grad_firsts, blocked]
    aliases = {}
    if piece > 0:
        in_specs += [pl.BlockSpec(memory_space=pl.ANY), wide]
        operands += [rows_before, sum_before]
        aliases = {3: 0}
    if last:
        if plan.pieces == 1:
            in_specs.append(wide)
            operands += gate_grads
            out_spec = wide
            out_shape = (plan.block, plan.channels)
        else:
            in_specs += [
                pl.BlockSpec((step // plan.here, plan.part, plan.channels), lambda i: (i, 0, 0))
            ] * n_gates
            operands += [r.reshape(plan.count, plan.part, plan.channels) for r in gate_grads]
            out_spec = pl.BlockSpec(
                (step // plan.here, plan.pieces, plan.part, plan.channels), lambda i: (i, 0, 0, 0)
            )
            out_shape = (plan.count, plan.pieces, plan.part, plan.channels)
    else:
        out_spec = wide
        out_shape = (plan.block, plan.channels)
    one_shape = (plan.block, plan.block)
    if plan.pieces > 1:
        one_shape = (plan.count, plan.pieces, plan.part, plan.block)
    return pl.pallas_call(
        body,
        grid=(plan.block // step,),
        in_specs=in_specs,
        out_specs=[plan.spec(plan.rows, step, piece, lambda i: (0, i)), out_spec],
        out_shape=[
            jax.ShapeDtypeStruct(one_shape, F32),
            jax.ShapeDtypeStruct(out_shape, BF if last else F32),
        ],
        input_output_aliases=aliases,
        compiler_params=params(),
        cost_estimate=cost(
            4 * plan.rows * plan.block * plan.channels,
            6 * plan.rows * plan.block + 8 * plan.block * plan.channels,
        ),
        name="finish",
    )(*operands)


def radices(count):
    steps, stride = [], 1
    while stride < count:
        radix = 4 if stride >= 4 and count // stride == 4 else 2
        steps.append((stride, radix))
        stride *= radix
    return steps


def swap(values, count, stride, s):
    return lax.ppermute(values, "seq", [(i, i ^ (stride * s)) for i in range(count)])


def scatter_step(total, count, stride, radix):
    digit = (lax.axis_index("seq") // stride) % radix
    cut = total.reshape(radix, total.shape[0] // radix, total.shape[1])
    kept = lax.dynamic_index_in_dim(cut, digit, 0, keepdims=False)
    for s in range(1, radix):
        send = lax.dynamic_index_in_dim(cut, digit ^ s, 0, keepdims=False).astype(BF)
        kept = kept + swap(send, count, stride, s).astype(F32)
    return kept


def gather_step(share, count, stride, radix):
    digit = (lax.axis_index("seq") // stride) % radix
    got = [share] + [swap(share, count, stride, s) for s in range(1, radix)]
    if radix == 2:
        low = jnp.where(digit == 0, got[0], got[1])
        high = jnp.where(digit == 0, got[1], got[0])
        return jnp.concatenate([low, high], axis=0)
    whole = jnp.zeros((radix,) + share.shape, share.dtype)
    for s in range(radix):
        whole = lax.dynamic_update_index_in_dim(whole, got[s], digit ^ s, 0)
    return whole.reshape(radix * share.shape[0], share.shape[1])


def write_weights(total, up_shape, down_shape, scale):
    groups, width, inner = up_shape

    def body(up_in, down_in, up_ref, down_ref):
        up_ref[0] = up_in[...].astype(F32) * scale
        down_ref[0] = (down_in[...].astype(F32) * scale).T

    return pl.pallas_call(
        body,
        grid=(groups,),
        in_specs=[
            pl.BlockSpec((width, inner), lambda b: (b, 0)),
            pl.BlockSpec((width, inner), lambda b: (groups + b, 0)),
        ],
        out_specs=[
            pl.BlockSpec((1, width, inner), lambda b: (b, 0, 0)),
            pl.BlockSpec((1, inner, width), lambda b: (b, 0, 0)),
        ],
        out_shape=[
            jax.ShapeDtypeStruct(up_shape, F32),
            jax.ShapeDtypeStruct(down_shape, F32),
        ],
        compiler_params=params(),
        cost_estimate=cost(groups * width * inner, 12 * groups * width * inner),
        name="write_weights",
    )(total, total)


def on_device(tokens, cotangent, factor_one, factor_two, up_blocks, down_blocks):
    count = lax.axis_size("seq")
    block, channels = factor_one.shape[1], tokens.shape[1]
    plan = Plan(count, block, channels)
    scale = float(count * tokens.shape[0]) ** (-0.5)
    factor = factor_one.reshape(block, block)
    pieces = range(plan.pieces)
    tokens, cotangent, factor, up_blocks, down_blocks = (
        pltpu.with_memory_space_constraint(a, pltpu.HBM)
        for a in (tokens, cotangent, factor, up_blocks, down_blocks)
    )

    def exchange(rows):
        cut = rows.reshape(count, plan.part, channels)
        got = lax.all_to_all(cut, "seq", split_axis=0, concat_axis=0, tiled=True)
        return got.reshape(plan.rows, channels)

    if plan.grouped:
        spread = spread_factor(plan, factor_two)

    def second(cols, piece, back):
        if plan.grouped:
            return mix_second(plan, spread, cols, piece, back)
        cut = cols.reshape(count, plan.part, channels)
        names = "kmj,mkc->jkc" if back else "kmj,jkc->mkc"
        got = jnp.einsum(names, factor_two, cut, preferred_element_type=F32).astype(BF)
        return got.reshape(plan.rows, channels)

    def second_grad(grads, firsts):
        if plan.grouped:
            return grad_second(plan, grads, firsts, scale)
        shape = (count, plan.part, channels)
        got = jnp.einsum(
            "mkc,jkc->kmj", grads.reshape(shape), firsts.reshape(shape), preferred_element_type=F32
        )
        return got * scale

    firsts = [exchange(mix_first(plan, factor, tokens, q)) for q in pieces]
    mixed = [exchange(second(firsts[q], q, False)) for q in pieces]
    weights = None
    grad_mixed, gate_grads = [], []
    for q in pieces:
        dv, r, weights = middle(
            plan, tokens, cotangent, mixed[q], up_blocks, down_blocks, q, weights
        )
        grad_mixed.append(exchange(dv))
        gate_grads.append(r)
    total = weights.reshape(-1, weights.shape[-1])
    steps = radices(count)
    for step in steps:
        total = scatter_step(total, count, *step)
    total = total.astype(BF)
    back = [second(grad_mixed[q], q, True) for q in pieces]
    back, total = lax.optimization_barrier((back, total))
    for step in reversed(steps):
        total = gather_step(total, count, *step)
    grad_firsts = [exchange(b) for b in back]
    two = [second_grad(grad_mixed[q], firsts[q]) for q in pieces]
    grad_up, grad_down = write_weights(total, up_blocks.shape, down_blocks.shape, scale)
    one, tokens_sum = None, None
    for q in pieces:
        one, tokens_sum = finish(
            plan, factor, grad_firsts[q], tokens, gate_grads, q, scale, one, tokens_sum
        )
    return (
        tokens_sum.reshape(tokens.shape),
        one.reshape(1, block, block),
        jnp.concatenate(two, axis=0),
        grad_up,
        grad_down,
    )


def solution(mesh):
    return jax.shard_map(
        on_device,
        mesh=mesh,
        in_specs=(
            P(("grp", "seq"), None),
            P(("grp", "seq"), None),
            P("seq", None, None),
            P("seq", None, None),
            P(),
            P(),
        ),
        out_specs=(
            P(("grp", "seq"), None),
            P(("grp", "seq"), None, None),
            P(("grp", "seq"), None, None),
            P("grp", None, None),
            P("grp", None, None),
        ),
        check_vma=False,
    )
```

```python
import jax
import jax.numpy as jnp
from jax import lax
from jax.experimental import pallas as pl
from jax.experimental.pallas import tpu as pltpu
from jax.sharding import PartitionSpec as P

BF = jnp.bfloat16
F32 = jnp.float32
PIECES = 2
INNER = 4
VMEM_BYTES = 40 * 1024 * 1024
SCALAR = pl.BlockSpec(memory_space=pltpu.SMEM)


def in_hbm(array):
    return pltpu.with_memory_space_constraint(array, pltpu.HBM)


def sigmoid(z):
    return 0.5 + 0.5 * jnp.tanh(0.5 * z)


def dot(a, b, ca, cb, **kw):
    return lax.dot_general(a, b, (((ca,), (cb,)), ((), ())), preferred_element_type=F32, **kw)


def rows_of(ref):
    value = ref[...]
    return value.reshape(-1, value.shape[-1])


def params(steps=1):
    return pltpu.CompilerParams(
        dimension_semantics=("arbitrary",) * steps, vmem_limit_bytes=VMEM_BYTES
    )


def cost(flops, moved, trans=0):
    return pl.CostEstimate(flops=int(flops), bytes_accessed=int(moved), transcendentals=int(trans))


class Plan:
    def __init__(self, count, block, channels):
        self.count = count
        self.block = block
        self.channels = channels
        self.here = block // count
        self.pieces = PIECES if self.here % (16 * PIECES) == 0 else 1
        self.part = self.here // self.pieces
        self.rows = block // self.pieces
        self.grouped = self.part % 16 == 0

    def view(self, array):
        if self.pieces > 1:
            array = array.reshape(self.count, self.pieces, self.part, array.shape[-1])
        return in_hbm(array)

    def spec(self, rows, columns, piece, index=lambda i: (i, 0)):
        if self.pieces == 1:
            return pl.BlockSpec((rows, columns), index)

        def whole(i):
            at, col = index(i)
            return (at, piece, 0, col)

        return pl.BlockSpec((rows // self.part, 1, self.part, columns), whole)


def mix_first(plan, factor, blocked, piece):
    def body(factor_ref, x_ref, out_ref):
        out_ref[...] = dot(rows_of(factor_ref), x_ref[...], 1, 0).astype(BF)

    step = min(256, plan.rows)
    return pl.pallas_call(
        body,
        grid=(plan.rows // step,),
        in_specs=[
            plan.spec(step, plan.block, piece),
            pl.BlockSpec((plan.block, plan.channels), lambda i: (0, 0)),
        ],
        out_specs=pl.BlockSpec((step, plan.channels), lambda i: (i, 0)),
        out_shape=jax.ShapeDtypeStruct((plan.rows, plan.channels), BF),
        compiler_params=params(),
        cost_estimate=cost(
            2 * plan.rows * plan.block * plan.channels,
            2 * (plan.rows * plan.block + 2 * plan.block * plan.channels),
        ),
        name="mix_first",
    )(plan.view(factor), in_hbm(blocked))


def spread_factor(plan, inner, factor_plane):
    n, outer = plan.count * INNER, plan.count
    groups = plan.here // 16
    tall, wide = outer * 16, n * 16
    cut = factor_plane.reshape(groups, 16, n, n)
    rows = cut.reshape(groups, 16, outer, INNER, n)
    fwd = lax.dynamic_index_in_dim(rows, inner, 3, keepdims=False).transpose(0, 2, 1, 3)
    cols = cut.reshape(groups, 16, n, outer, INNER)
    bwd = lax.dynamic_index_in_dim(cols, inner, 4, keepdims=False).transpose(0, 3, 1, 2)
    both = jnp.stack([fwd, bwd]).reshape(2 * groups, tall, n)

    def body(inner_ref, in_ref, out_ref):
        pick = picker(n, outer, inner_ref[0], False).astype(BF)
        same = same_position(tall, wide)
        for g in range(in_ref.shape[0]):
            full = dot(in_ref[g], pick, 1, 0)
            out_ref[g] = jnp.where(same, full, 0.0).astype(BF)

    half = groups
    return pl.pallas_call(
        body,
        grid=(2,),
        in_specs=[SCALAR, pl.BlockSpec((half, tall, n), lambda i: (i, 0, 0))],
        out_specs=pl.BlockSpec((half, tall, wide), lambda i: (i, 0, 0)),
        out_shape=jax.ShapeDtypeStruct((2 * groups, tall, wide), BF),
        compiler_params=params(),
        cost_estimate=cost(4 * groups * tall * wide * n, 4 * groups * tall * wide),
        name="spread_factor",
    )(inner.reshape(1), both)


def picker(n, outer, inner, turned):
    wide = n * 16
    shape = (wide, n) if turned else (n, wide)
    col = lax.broadcasted_iota(jnp.int32, shape, 0 if turned else 1) // 16
    block = lax.broadcasted_iota(jnp.int32, shape, 1 if turned else 0)
    return jnp.where((col % outer) * INNER + ((col // outer) ^ inner) == block, 1.0, 0.0)


def same_position(tall, wide):
    r = lax.broadcasted_iota(jnp.int32, (tall, wide), 0)
    c = lax.broadcasted_iota(jnp.int32, (tall, wide), 1)
    return r % 16 == c % 16


def group_rows(refs, g):
    at = slice(g * 16, (g + 1) * 16)
    parts = [r[:, at, :].reshape(-1, r.shape[-1]) for r in refs]
    return parts[0] if len(parts) == 1 else jnp.concatenate(parts, axis=0)


def mix_second(plan, spread, cols, piece, back):
    outer = plan.count
    groups = plan.part // 16
    tall, wide = outer * 16, outer * INNER * 16
    shape = (outer, plan.part, plan.channels)
    base = (plan.pieces if back else 0) + piece

    def body(m_ref, *rest):
        ins, out_ref = rest[:-1], rest[-1]
        for g in range(groups):
            got = dot(m_ref[g], group_rows(ins, g), 1, 0).astype(BF)
            out_ref[:, g * 16 : (g + 1) * 16, :] = got.reshape(outer, 16, plan.channels)

    full = pl.BlockSpec(shape, lambda i: (0, 0, 0))
    return pl.pallas_call(
        body,
        grid=(1,),
        in_specs=[pl.BlockSpec((groups, tall, wide), lambda i: (base, 0, 0))] + [full] * INNER,
        out_specs=full,
        out_shape=jax.ShapeDtypeStruct(shape, BF),
        compiler_params=params(),
        cost_estimate=cost(
            2 * groups * tall * wide * plan.channels,
            2 * (INNER + 1) * plan.rows * plan.channels + 2 * groups * tall * wide,
        ),
        name="mix_second_back" if back else "mix_second",
    )(spread, *cols)


def grad_second(plan, inner, grads, firsts, scale):
    outer, n = plan.count, plan.count * INNER
    groups = plan.part // 16
    tall, wide = outer * 16, n * 16

    def body(inner_ref, g_ref, *rest):
        us, out_ref = rest[:-1], rest[-1]
        same = same_position(tall, wide)
        pick = picker(n, outer, inner_ref[0], True)
        for g in range(groups):
            full = dot(group_rows([g_ref], g), group_rows(us, g), 1, 1)
            kept = jnp.where(same, full, 0.0)
            out_ref[g] = dot(kept, pick, 1, 0, precision=lax.Precision.HIGHEST) * scale

    full = pl.BlockSpec((outer, plan.part, plan.channels), lambda i: (0, 0, 0))
    out = pl.pallas_call(
        body,
        grid=(1,),
        in_specs=[SCALAR] + [full] * (INNER + 1),
        out_specs=pl.BlockSpec((groups, tall, n), lambda i: (0, 0, 0)),
        out_shape=jax.ShapeDtypeStruct((groups, tall, n), F32),
        compiler_params=params(),
        cost_estimate=cost(
            2 * groups * tall * wide * plan.channels, 2 * (INNER + 1) * plan.rows * plan.channels
        ),
        name="grad_second",
    )(inner.reshape(1), grads, *firsts)
    return out.reshape(groups, outer, 16, n).transpose(0, 2, 1, 3).reshape(plan.part, outer, n)


def middle(plan, blocked, incoming, mixed, up_blocks, down_blocks, piece, before):
    groups, width, inner = up_blocks.shape
    sub = inner // groups
    step = min(256, plan.rows)

    def body(*refs):
        x_ref, g_ref, v_ref, up_ref, down_ref = refs[:5]
        dv_ref, r_ref, w_ref = refs[-3:]

        @pl.when(pl.program_id(0) == 0)
        def _():
            if before is None:
                w_ref[...] = jnp.zeros_like(w_ref)
            else:
                w_ref[...] = refs[5][...]

        x = rows_of(x_ref).astype(F32)
        g = rows_of(g_ref)
        v = v_ref[...].astype(F32)
        sx = sigmoid(x)
        gate = x * sx
        h = (x + v * gate).astype(BF)
        h_parts = [h[:, b * width : (b + 1) * width] for b in range(groups)]
        g_parts = [g[:, b * width : (b + 1) * width] for b in range(groups)]
        acts, slopes, back = [], [], []
        for b in range(groups):
            a = dot(h_parts[b], up_ref[b], 1, 0)
            s = sigmoid(a)
            q = a * s
            acts.append(q.astype(BF))
            slopes.append(s + q * (1.0 - s))
            back.append(dot(g_parts[b], down_ref[b], 1, 1))
        grads = []
        for b in range(groups):
            lanes = slice(b * sub, (b + 1) * sub)
            perm = jnp.concatenate([acts[p][:, lanes] for p in range(groups)], axis=1)
            w_ref[groups + b] += dot(g_parts[b], perm, 0, 0)
            dq = jnp.concatenate([back[p][:, lanes] for p in range(groups)], axis=1)
            da = (dq * slopes[b]).astype(BF)
            w_ref[b] += dot(h_parts[b], da, 0, 0)
            grads.append(dot(da, up_ref[b], 1, 1))
        dh = (g.astype(F32) + jnp.concatenate(grads, axis=1)).astype(BF).astype(F32)
        dv_ref[...] = (dh * gate).astype(BF)
        r_ref[...] = (dh * (1.0 + v * (sx + gate * (1.0 - sx)))).astype(BF)

    block = pl.BlockSpec((step, plan.channels), lambda i: (i, 0))
    full = pl.BlockSpec((2 * groups, width, inner), lambda i: (0, 0, 0))
    in_specs = [
        plan.spec(step, plan.channels, piece),
        plan.spec(step, plan.channels, piece),
        block,
        pl.BlockSpec(up_blocks.shape, lambda i: (0, 0, 0)),
        pl.BlockSpec(down_blocks.shape, lambda i: (0, 0, 0)),
    ]
    operands = [plan.view(blocked), plan.view(incoming), mixed, in_hbm(up_blocks), in_hbm(down_blocks)]
    if before is not None:
        in_specs.append(full)
        operands.append(before)
    hidden = plan.rows * groups * inner
    return pl.pallas_call(
        body,
        grid=(plan.rows // step,),
        in_specs=in_specs,
        out_specs=[block, block, full],
        out_shape=[
            jax.ShapeDtypeStruct((plan.rows, plan.channels), BF),
            jax.ShapeDtypeStruct((plan.rows, plan.channels), BF),
            jax.ShapeDtypeStruct((2 * groups, width, inner), F32),
        ],
        compiler_params=params(),
        cost_estimate=cost(
            10 * hidden * width, 10 * plan.rows * plan.channels + 8 * groups * width * inner, hidden
        ),
        name="middle",
    )(*operands)


def finish(plan, factor, grad_firsts, blocked, gate_grads, piece, scale, rows_before, sum_before):
    last = piece == plan.pieces - 1
    step = min(256, plan.block)
    n_gates = plan.pieces if last else 0

    def body(*refs):
        factor_ref, d_ref, x_ref = refs[:3]
        one_ref, out_ref = refs[-2:]
        d = d_ref[...]
        one = dot(d, x_ref[...], 1, 1) * scale
        one_ref[...] = one.reshape(one_ref.shape)
        total = dot(rows_of(factor_ref), d, 0, 0)
        at = 3
        if piece > 0:
            total = total + refs[4][...]
            at = 5
        if last:
            if plan.pieces == 1:
                out_ref[...] = (total + refs[at][...].astype(F32)).astype(BF)
            else:
                total = total.reshape(step // plan.here, plan.pieces, plan.part, plan.channels)
                for q in range(plan.pieces):
                    got = (total[:, q] + refs[at + q][...].astype(F32)).astype(BF)
                    out_ref[:, q] = got
        else:
            out_ref[...] = total

    wide = pl.BlockSpec((step, plan.channels), lambda i: (i, 0))
    in_specs = [
        plan.spec(plan.rows, step, piece, lambda i: (0, i)),
        pl.BlockSpec((plan.rows, plan.channels), lambda i: (0, 0)),
        wide,
    ]
    operands = [plan.view(factor), grad_firsts, in_hbm(blocked)]
    aliases = {}
    if piece > 0:
        in_specs += [pl.BlockSpec(memory_space=pl.ANY), wide]
        operands += [rows_before, sum_before]
        aliases = {3: 0}
    if last:
        if plan.pieces == 1:
            in_specs.append(wide)
            operands += gate_grads
            out_spec = wide
            out_shape = (plan.block, plan.channels)
        else:
            in_specs += [
                pl.BlockSpec((step // plan.here, plan.part, plan.channels), lambda i: (i, 0, 0))
            ] * n_gates
            operands += [r.reshape(plan.count, plan.part, plan.channels) for r in gate_grads]
            out_spec = pl.BlockSpec(
                (step // plan.here, plan.pieces, plan.part, plan.channels), lambda i: (i, 0, 0, 0)
            )
            out_shape = (plan.count, plan.pieces, plan.part, plan.channels)
    else:
        out_spec = wide
        out_shape = (plan.block, plan.channels)
    one_shape = (plan.block, plan.block)
    if plan.pieces > 1:
        one_shape = (plan.count, plan.pieces, plan.part, plan.block)
    return pl.pallas_call(
        body,
        grid=(plan.block // step,),
        in_specs=in_specs,
        out_specs=[plan.spec(plan.rows, step, piece, lambda i: (0, i)), out_spec],
        out_shape=[
            jax.ShapeDtypeStruct(one_shape, F32),
            jax.ShapeDtypeStruct(out_shape, BF if last else F32),
        ],
        input_output_aliases=aliases,
        compiler_params=params(),
        cost_estimate=cost(
            4 * plan.rows * plan.block * plan.channels,
            6 * plan.rows * plan.block + 8 * plan.block * plan.channels,
        ),
        name="finish",
    )(*operands)


def radices(count):
    steps, stride = [], 1
    while stride < count:
        radix = 4 if stride >= 4 and count // stride == 4 else 2
        steps.append((stride, radix))
        stride *= radix
    return steps


def swap(values, count, stride, s):
    return lax.ppermute(values, "seq", [(i, i ^ (stride * s)) for i in range(count)])


def scatter_step(total, count, stride, radix):
    digit = (lax.axis_index("seq") // stride) % radix
    cut = total.reshape(radix, total.shape[0] // radix, total.shape[1])
    kept = lax.dynamic_index_in_dim(cut, digit, 0, keepdims=False)
    for s in range(1, radix):
        send = lax.dynamic_index_in_dim(cut, digit ^ s, 0, keepdims=False).astype(BF)
        kept = kept + swap(send, count, stride, s).astype(F32)
    return kept


def gather_step(share, count, stride, radix):
    digit = (lax.axis_index("seq") // stride) % radix
    got = [share] + [swap(share, count, stride, s) for s in range(1, radix)]
    if radix == 2:
        low = jnp.where(digit == 0, got[0], got[1])
        high = jnp.where(digit == 0, got[1], got[0])
        return jnp.concatenate([low, high], axis=0)
    whole = jnp.zeros((radix,) + share.shape, share.dtype)
    for s in range(radix):
        whole = lax.dynamic_update_index_in_dim(whole, got[s], digit ^ s, 0)
    return whole.reshape(radix * share.shape[0], share.shape[1])


def write_weights(total, up_shape, down_shape, scale):
    groups, width, inner = up_shape

    def body(up_in, down_in, up_ref, down_ref):
        up_ref[0] = up_in[...].astype(F32) * scale
        down_ref[0] = (down_in[...].astype(F32) * scale).T

    return pl.pallas_call(
        body,
        grid=(groups,),
        in_specs=[
            pl.BlockSpec((width, inner), lambda b: (b, 0)),
            pl.BlockSpec((width, inner), lambda b: (groups + b, 0)),
        ],
        out_specs=[
            pl.BlockSpec((1, width, inner), lambda b: (b, 0, 0)),
            pl.BlockSpec((1, inner, width), lambda b: (b, 0, 0)),
        ],
        out_shape=[
            jax.ShapeDtypeStruct(up_shape, F32),
            jax.ShapeDtypeStruct(down_shape, F32),
        ],
        compiler_params=params(),
        cost_estimate=cost(groups * width * inner, 12 * groups * width * inner),
        name="write_weights",
    )(total, total)


def on_device(tokens, cotangent, factor_one, factor_two, up_blocks, down_blocks):
    count = lax.axis_size("seq")
    outer = count // INNER
    block, channels = factor_one.shape[1], tokens.shape[1]
    plan = Plan(outer, block, channels)
    scale = float(count * tokens.shape[0]) ** (-0.5)
    factor = factor_one.reshape(block, block)
    pieces = range(plan.pieces)
    inner = lax.axis_index("seq").astype(jnp.int32) % INNER
    planes = [[z * INNER + i for z in range(outer)] for i in range(INNER)]

    def across(rows):
        cut = rows.reshape(outer, plan.part, channels)
        return lax.all_to_all(
            cut, "seq", split_axis=0, concat_axis=0, tiled=True, axis_index_groups=planes
        )

    def within(mine):
        far = swap(mine, count, 2, 1)
        return [mine, swap(mine, count, 1, 1), far, swap(far, count, 1, 1)]

    flat = factor_two.reshape(factor_two.shape[0], -1)
    plane_two = gather_step(gather_step(flat, count, 1, 2), count, 2, 2)
    spread = spread_factor(plan, inner, plane_two)

    def rows(value):
        return value.reshape(plan.rows, channels)

    firsts = [within(across(mix_first(plan, factor, tokens, q))) for q in pieces]
    mixed = [across(mix_second(plan, spread, firsts[q], q, False)) for q in pieces]
    weights = None
    own_grads, gate_grads = [], []
    for q in pieces:
        dv, r, weights = middle(
            plan, tokens, cotangent, rows(mixed[q]), up_blocks, down_blocks, q, weights
        )
        own_grads.append(across(dv))
        gate_grads.append(r)
    total = weights.reshape(-1, weights.shape[-1])
    steps = radices(count)
    for step in steps:
        total = scatter_step(total, count, *step)
    total = total.astype(BF)
    for step in reversed(steps):
        total = gather_step(total, count, *step)
    grad_firsts = [
        across(mix_second(plan, spread, within(own_grads[q]), q, True)) for q in pieces
    ]
    two = jnp.concatenate(
        [grad_second(plan, inner, own_grads[q], firsts[q], scale) for q in pieces], axis=0
    )
    here = factor_two.shape[0]
    two = two.reshape(INNER, here, outer, count)
    held = jnp.zeros_like(two)
    for s in range(INNER):
        part = lax.dynamic_index_in_dim(two, inner ^ s, 0, keepdims=False)
        got = part if s == 0 else swap(part, count, 1, s)
        held = lax.dynamic_update_index_in_dim(held, got, inner ^ s, 0)
    two = held.transpose(1, 2, 0, 3).reshape(here, count, count)
    grad_up, grad_down = write_weights(total, up_blocks.shape, down_blocks.shape, scale)
    one, tokens_sum = None, None
    for q in pieces:
        one, tokens_sum = finish(
            plan, factor, rows(grad_firsts[q]), tokens, gate_grads, q, scale, one, tokens_sum
        )
    return (
        tokens_sum.reshape(tokens.shape),
        one.reshape(1, block, block),
        two,
        grad_up,
        grad_down,
    )


def solution(mesh):
    return jax.shard_map(
        on_device,
        mesh=mesh,
        in_specs=(
            P(("grp", "seq"), None),
            P(("grp", "seq"), None),
            P("seq", None, None),
            P("seq", None, None),
            P(),
            P(),
        ),
        out_specs=(
            P(("grp", "seq"), None),
            P(("grp", "seq"), None, None),
            P(("grp", "seq"), None, None),
            P("grp", None, None),
            P("grp", None, None),
        ),
        check_vma=False,
    )
```

```python
import jax
import jax.numpy as jnp
from jax import lax
from jax.experimental import pallas as pl
from jax.experimental.pallas import tpu as pltpu
from jax.sharding import PartitionSpec as P

BF = jnp.bfloat16
F32 = jnp.float32
VMEM_BYTES = 40 * 1024 * 1024
ANY = pl.BlockSpec(memory_space=pl.ANY)
SCALAR = pl.BlockSpec(memory_space=pltpu.SMEM)


def in_hbm(array):
    return pltpu.with_memory_space_constraint(array, pltpu.HBM)


def sigmoid(z):
    return 0.5 + 0.5 * jnp.tanh(0.5 * z)


def dot(a, b, ca, cb, **kw):
    return lax.dot_general(a, b, (((ca,), (cb,)), ((), ())), preferred_element_type=F32, **kw)


def params(steps=1):
    return pltpu.CompilerParams(
        dimension_semantics=("arbitrary",) * steps, vmem_limit_bytes=VMEM_BYTES
    )


def cost(flops, moved, trans=0):
    return pl.CostEstimate(flops=int(flops), bytes_accessed=int(moved), transcendentals=int(trans))


def row_copies(src, dst, sems, first, parts):
    rows = src.shape[0] // parts
    return [
        pltpu.make_async_copy(
            src.at[pl.ds(i * rows, rows)], dst.at[pl.ds(i * rows, rows)], sems.at[first + i]
        )
        for i in range(parts)
    ]


def mix_first(factor, blocked):
    block, channels = factor.shape[0], blocked.shape[1]
    tiles = 4
    step = block // tiles

    def body(f_hbm, x_hbm, u_hbm, f_all, x_all, u_all, sems):
        xs = row_copies(x_hbm, x_all, sems, 0, tiles)
        fs = row_copies(f_hbm, f_all, sems, tiles, tiles)
        us = row_copies(u_all, u_hbm, sems, 2 * tiles, tiles)
        for c in xs + fs:
            c.start()
        for c in xs:
            c.wait()
        for t in range(tiles):
            fs[t].wait()
            at = slice(t * step, (t + 1) * step)
            u_all[at, :] = dot(f_all[at, :], x_all[...], 1, 0).astype(BF)
            us[t].start()
        for c in us:
            c.wait()

    return pl.pallas_call(
        body,
        in_specs=[ANY, ANY],
        out_specs=ANY,
        out_shape=pltpu.HBM((block, channels), BF),
        scratch_shapes=[
            pltpu.VMEM((block, block), BF),
            pltpu.VMEM((block, channels), BF),
            pltpu.VMEM((block, channels), BF),
            pltpu.SemaphoreType.DMA((3 * tiles,)),
        ],
        compiler_params=params(0),
        cost_estimate=cost(2 * block * block * channels, 2 * block * (block + 2 * channels)),
        name="mix_first",
    )(in_hbm(factor), in_hbm(blocked))


def spread_factor(factor_two):
    here, n, _ = factor_two.shape
    groups = here // 16
    wide = n * 16
    turned = factor_two.reshape(groups, 16, n, n).transpose(0, 2, 1, 3).reshape(groups, wide, n)

    def body(in_ref, out_ref):
        col = lax.broadcasted_iota(jnp.int32, (n, wide), 1)
        row = lax.broadcasted_iota(jnp.int32, (n, wide), 0)
        pick = jnp.where(col // 16 == row, 1.0, 0.0).astype(BF)
        r = lax.broadcasted_iota(jnp.int32, (wide, wide), 0)
        c = lax.broadcasted_iota(jnp.int32, (wide, wide), 1)
        same = r % 16 == c % 16
        full = dot(in_ref[0], pick, 1, 0)
        out_ref[0] = jnp.where(same, full, 0.0).astype(BF)

    return pl.pallas_call(
        body,
        grid=(groups,),
        in_specs=[pl.BlockSpec((1, wide, n), lambda g: (g, 0, 0))],
        out_specs=pl.BlockSpec((1, wide, wide), lambda g: (g, 0, 0)),
        out_shape=jax.ShapeDtypeStruct((groups, wide, wide), BF),
        compiler_params=params(),
        cost_estimate=cost(2 * groups * wide * wide * n, 2 * groups * wide * wide),
        name="spread_factor",
    )(turned)


def mix_second(spread, cols, back):
    n, here, channels = cols.shape
    wide = n * 16
    groups = here // 16

    def body(m_ref, in_ref, out_ref):
        rows = in_ref[...].reshape(wide, channels)
        got = dot(m_ref[0], rows, 0 if back else 1, 0).astype(BF)
        out_ref[...] = got.reshape(n, 16, channels)

    blocks = pl.BlockSpec((n, 16, channels), lambda g: (0, g, 0))
    return pl.pallas_call(
        body,
        grid=(groups,),
        in_specs=[pl.BlockSpec((1, wide, wide), lambda g: (g, 0, 0)), blocks],
        out_specs=blocks,
        out_shape=pltpu.HBM(cols.shape, BF) if back else jax.ShapeDtypeStruct(cols.shape, BF),
        compiler_params=params(),
        cost_estimate=cost(
            2 * groups * wide * wide * channels, 4 * cols.size + 2 * groups * wide * wide
        ),
        name="mix_second_back" if back else "mix_second",
    )(spread, cols)


def grad_second(grads, firsts, scale):
    n, here, channels = grads.shape
    wide = n * 16
    groups = here // 16

    def body(g_ref, u_ref, out_ref):
        g = g_ref[...].reshape(wide, channels)
        u = u_ref[...].reshape(wide, channels)
        full = dot(g, u, 1, 1)
        r = lax.broadcasted_iota(jnp.int32, (wide, wide), 0)
        c = lax.broadcasted_iota(jnp.int32, (wide, wide), 1)
        kept = jnp.where(r % 16 == c % 16, full, 0.0)
        row = lax.broadcasted_iota(jnp.int32, (wide, n), 0)
        col = lax.broadcasted_iota(jnp.int32, (wide, n), 1)
        pick = jnp.where(row // 16 == col, 1.0, 0.0)
        out_ref[0] = dot(kept, pick, 1, 0, precision=lax.Precision.HIGHEST) * scale

    out = pl.pallas_call(
        body,
        grid=(groups,),
        in_specs=[pl.BlockSpec((n, 16, channels), lambda g: (0, g, 0))] * 2,
        out_specs=pl.BlockSpec((1, wide, n), lambda g: (g, 0, 0)),
        out_shape=jax.ShapeDtypeStruct((groups, wide, n), F32),
        compiler_params=params(),
        cost_estimate=cost(2 * groups * wide * wide * channels, 4 * grads.size),
        name="grad_second",
    )(grads, firsts)
    return out.reshape(groups, n, 16, n).transpose(0, 2, 1, 3).reshape(here, n, n)


def middle(half, blocked, incoming, mixed, up_blocks, down_blocks):
    groups, width, inner = up_blocks.shape
    sub = inner // groups
    rows, channels = blocked.shape
    step = min(256, rows)
    last = rows // step - 1

    def body(half_ref, x_ref, g_ref, v_ref, up_ref, down_ref, dv_ref, r_ref, kept_ref, sent_ref, w):
        i = pl.program_id(0)

        @pl.when(i == 0)
        def _():
            w[...] = jnp.zeros_like(w)

        x = x_ref[...].astype(F32)
        g = g_ref[...]
        v = v_ref[...].astype(F32)
        sx = sigmoid(x)
        gate = x * sx
        h = (x + v * gate).astype(BF)
        h_parts = [h[:, b * width : (b + 1) * width] for b in range(groups)]
        g_parts = [g[:, b * width : (b + 1) * width] for b in range(groups)]
        acts, slopes, back = [], [], []
        for b in range(groups):
            a = dot(h_parts[b], up_ref[b], 1, 0)
            s = sigmoid(a)
            q = a * s
            acts.append(q.astype(BF))
            slopes.append(s + q * (1.0 - s))
            back.append(dot(g_parts[b], down_ref[b], 1, 1))
        grads = []
        for b in range(groups):
            lanes = slice(b * sub, (b + 1) * sub)
            perm = jnp.concatenate([acts[p][:, lanes] for p in range(groups)], axis=1)
            w[1, b] += dot(g_parts[b], perm, 0, 0)
            dq = jnp.concatenate([back[p][:, lanes] for p in range(groups)], axis=1)
            da = (dq * slopes[b]).astype(BF)
            w[0, b] += dot(h_parts[b], da, 0, 0)
            grads.append(dot(da, up_ref[b], 1, 1))
        dh = (g.astype(F32) + jnp.concatenate(grads, axis=1)).astype(BF).astype(F32)
        dv_ref[...] = (dh * gate).astype(BF)
        r_ref[...] = (dh * (1.0 + v * (sx + gate * (1.0 - sx)))).astype(BF)

        @pl.when(i == last)
        def _():
            kept_ref[...] = w[half_ref[0]].astype(BF)
            sent_ref[...] = w[1 - half_ref[0]].astype(BF)

    block = pl.BlockSpec((step, channels), lambda i: (i, 0))
    full = pl.BlockSpec(up_blocks.shape, lambda i: (0, 0, 0))
    hidden = rows * groups * inner
    return pl.pallas_call(
        body,
        grid=(last + 1,),
        in_specs=[
            SCALAR,
            block,
            block,
            block,
            full,
            pl.BlockSpec(down_blocks.shape, lambda i: (0, 0, 0)),
        ],
        out_specs=[block, block, full, full],
        out_shape=[
            pltpu.HBM((rows, channels), BF),
            pltpu.HBM((rows, channels), BF),
            pltpu.HBM(up_blocks.shape, BF),
            pltpu.HBM(up_blocks.shape, BF),
        ],
        scratch_shapes=[pltpu.VMEM((2, groups, width, inner), F32)],
        compiler_params=params(),
        cost_estimate=cost(
            10 * hidden * width, 10 * rows * channels + 8 * groups * width * inner, hidden
        ),
        name="middle",
    )(half, in_hbm(blocked), in_hbm(incoming), mixed, in_hbm(up_blocks), in_hbm(down_blocks))


def finish(factor, grad_first, blocked, gate_grad, scale):
    block, channels = blocked.shape
    tiles = 4
    step = block // tiles

    def body(f_hbm, d_hbm, x_hbm, r_hbm, one_hbm, out_hbm, f, d, x, r, one, out, sems):
        ds = row_copies(d_hbm, d, sems, 0, tiles)
        xs = row_copies(x_hbm, x, sems, tiles, tiles)
        fs = row_copies(f_hbm, f, sems, 2 * tiles, tiles)
        rs = row_copies(r_hbm, r, sems, 3 * tiles, tiles)
        ones = row_copies(one, one_hbm, sems, 4 * tiles, tiles)
        outs = row_copies(out, out_hbm, sems, 5 * tiles, tiles)
        for c in ds + xs + fs + rs:
            c.start()
        for c in xs:
            c.wait()
        for t in range(tiles):
            at = slice(t * step, (t + 1) * step)
            ds[t].wait()
            one[at, :] = dot(d[at, :], x[...], 1, 1) * scale
            ones[t].start()
        for c in fs + rs:
            c.wait()
        for t in range(tiles):
            at = slice(t * step, (t + 1) * step)
            total = dot(f[:, at], d[...], 0, 0) + r[at, :].astype(F32)
            out[at, :] = total.astype(BF)
            outs[t].start()
        for c in ones + outs:
            c.wait()

    return pl.pallas_call(
        body,
        in_specs=[ANY] * 4,
        out_specs=[ANY] * 2,
        out_shape=[pltpu.HBM((block, block), F32), pltpu.HBM((block, channels), BF)],
        scratch_shapes=[
            pltpu.VMEM((block, block), BF),
            pltpu.VMEM((block, channels), BF),
            pltpu.VMEM((block, channels), BF),
            pltpu.VMEM((block, channels), BF),
            pltpu.VMEM((block, block), F32),
            pltpu.VMEM((block, channels), BF),
            pltpu.SemaphoreType.DMA((6 * tiles,)),
        ],
        compiler_params=params(0),
        cost_estimate=cost(4 * block * block * channels, 6 * block * block + 8 * block * channels),
        name="finish",
    )(in_hbm(factor), grad_first, in_hbm(blocked), in_hbm(gate_grad))


def radices(count):
    steps, stride = [], 1
    while stride < count:
        radix = 4 if stride >= 4 and count // stride == 4 else 2
        steps.append((stride, radix))
        stride *= radix
    return steps


def swap(values, count, stride, s):
    return lax.ppermute(values, "seq", [(i, i ^ (stride * s)) for i in range(count)])


def scatter_step(total, count, stride, radix, after=None):
    digit = (lax.axis_index("seq") // stride) % radix
    cut = total.reshape(radix, total.shape[0] // radix, total.shape[1])
    kept = lax.dynamic_index_in_dim(cut, digit, 0, keepdims=False)
    got = []
    for s in range(1, radix):
        send = lax.dynamic_index_in_dim(cut, digit ^ s, 0, keepdims=False).astype(BF)
        got.append(swap(send, count, stride, s))
    if after is not None:
        got, after = lax.optimization_barrier((got, after))
    for g in got:
        kept = kept + g.astype(F32)
    return kept


def gather_step(share, count, stride, radix):
    digit = (lax.axis_index("seq") // stride) % radix
    got = [share] + [swap(share, count, stride, s) for s in range(1, radix)]
    if radix == 2:
        low = jnp.where(digit == 0, got[0], got[1])
        high = jnp.where(digit == 0, got[1], got[0])
        return jnp.concatenate([low, high], axis=0)
    whole = jnp.zeros((radix,) + share.shape, share.dtype)
    for s in range(radix):
        whole = lax.dynamic_update_index_in_dim(whole, got[s], digit ^ s, 0)
    return whole.reshape(radix * share.shape[0], share.shape[1])


def write_weights(total, up_shape, down_shape, scale):
    groups, width, inner = up_shape

    def body(up_in, down_in, up_ref, down_ref):
        up_ref[0] = up_in[...].astype(F32) * scale
        down_ref[0] = (down_in[...].astype(F32) * scale).T

    return pl.pallas_call(
        body,
        grid=(groups,),
        in_specs=[
            pl.BlockSpec((width, inner), lambda b: (b, 0)),
            pl.BlockSpec((width, inner), lambda b: (groups + b, 0)),
        ],
        out_specs=[
            pl.BlockSpec((1, width, inner), lambda b: (b, 0, 0)),
            pl.BlockSpec((1, inner, width), lambda b: (b, 0, 0)),
        ],
        out_shape=[
            jax.ShapeDtypeStruct(up_shape, F32),
            jax.ShapeDtypeStruct(down_shape, F32),
        ],
        compiler_params=params(),
        cost_estimate=cost(groups * width * inner, 12 * groups * width * inner),
        name="write_weights",
    )(total, total)


def on_device(tokens, cotangent, factor_one, factor_two, up_blocks, down_blocks):
    count = lax.axis_size("seq")
    block, channels = factor_one.shape[1], tokens.shape[1]
    here = block // count
    scale = float(count * tokens.shape[0]) ** (-0.5)
    factor = factor_one.reshape(block, block)
    grouped = here % 16 == 0

    def exchange(values):
        cut = values.reshape(count, here, channels)
        return lax.all_to_all(cut, "seq", split_axis=0, concat_axis=0, tiled=True)

    if grouped:
        spread = spread_factor(factor_two)

    def second(cols, back):
        if grouped:
            return mix_second(spread, cols, back)
        names = "kmj,mkc->jkc" if back else "kmj,jkc->mkc"
        return jnp.einsum(names, factor_two, cols, preferred_element_type=F32).astype(BF)

    def second_grad(grads, firsts):
        if grouped:
            return grad_second(grads, firsts, scale)
        return jnp.einsum("mkc,jkc->kmj", grads, firsts, preferred_element_type=F32) * scale

    half = (lax.axis_index("seq") % 2).astype(jnp.int32).reshape(1)
    firsts = exchange(mix_first(factor, tokens))
    mixed = exchange(second(firsts, False)).reshape(block, channels)
    dv, gate_grad, kept, sent = middle(half, tokens, cotangent, mixed, up_blocks, down_blocks)
    grad_mixed = exchange(dv)
    back = second(grad_mixed, True)
    grad_first = exchange(back).reshape(block, channels)
    inner = kept.shape[-1]
    total = kept.astype(F32) + swap(sent, count, 1, 1).astype(F32)
    total = total.reshape(-1, inner)
    steps = radices(count)
    for step in steps[1:-1]:
        total = scatter_step(total, count, *step)
    total = scatter_step(total, count, *steps[-1], after=back).astype(BF)
    for step in reversed(steps):
        total = gather_step(total, count, *step)
    grad_up, grad_down = write_weights(total, up_blocks.shape, down_blocks.shape, scale)
    two = second_grad(grad_mixed, firsts)
    one, grad_tokens = finish(factor, grad_first, tokens, gate_grad, scale)
    return (grad_tokens, one.reshape(1, block, block), two, grad_up, grad_down)


def solution(mesh):
    return jax.shard_map(
        on_device,
        mesh=mesh,
        in_specs=(
            P(("grp", "seq"), None),
            P(("grp", "seq"), None),
            P("seq", None, None),
            P("seq", None, None),
            P(),
            P(),
        ),
        out_specs=(
            P(("grp", "seq"), None),
            P(("grp", "seq"), None, None),
            P(("grp", "seq"), None, None),
            P("grp", None, None),
            P("grp", None, None),
        ),
        check_vma=False,
    )
```

```python
import jax
import jax.numpy as jnp
from jax import lax
from jax.experimental import pallas as pl
from jax.experimental.pallas import tpu as pltpu
from jax.sharding import PartitionSpec as P

BF = jnp.bfloat16
F32 = jnp.float32
VMEM_BYTES = 40 * 1024 * 1024
ANY = pl.BlockSpec(memory_space=pl.ANY)
SCALAR = pl.BlockSpec(memory_space=pltpu.SMEM)


def in_hbm(array):
    return pltpu.with_memory_space_constraint(array, pltpu.HBM)


def sigmoid(z):
    return 0.5 + 0.5 * jnp.tanh(0.5 * z)


def dot(a, b, ca, cb, **kw):
    return lax.dot_general(a, b, (((ca,), (cb,)), ((), ())), preferred_element_type=F32, **kw)


def params(steps=1):
    return pltpu.CompilerParams(
        dimension_semantics=("arbitrary",) * steps, vmem_limit_bytes=VMEM_BYTES
    )


def cost(flops, moved, trans=0):
    return pl.CostEstimate(flops=int(flops), bytes_accessed=int(moved), transcendentals=int(trans))


def row_copies(src, dst, sems, first, parts):
    rows = src.shape[0] // parts
    return [
        pltpu.make_async_copy(
            src.at[pl.ds(i * rows, rows)], dst.at[pl.ds(i * rows, rows)], sems.at[first + i]
        )
        for i in range(parts)
    ]


def mix_first(factor, blocked):
    block, channels = factor.shape[0], blocked.shape[1]
    tiles = 4
    step = block // tiles

    def body(f_hbm, x_hbm, u_hbm, f_all, x_all, u_all, sems):
        xs = row_copies(x_hbm, x_all, sems, 0, tiles)
        fs = row_copies(f_hbm, f_all, sems, tiles, tiles)
        us = row_copies(u_all, u_hbm, sems, 2 * tiles, tiles)
        for c in xs + fs:
            c.start()
        for c in xs:
            c.wait()
        for t in range(tiles):
            fs[t].wait()
            at = slice(t * step, (t + 1) * step)
            u_all[at, :] = dot(f_all[at, :], x_all[...], 1, 0).astype(BF)
            us[t].start()
        for c in us:
            c.wait()

    return pl.pallas_call(
        body,
        in_specs=[ANY, ANY],
        out_specs=ANY,
        out_shape=pltpu.HBM((block, channels), BF),
        scratch_shapes=[
            pltpu.VMEM((block, block), BF),
            pltpu.VMEM((block, channels), BF),
            pltpu.VMEM((block, channels), BF),
            pltpu.SemaphoreType.DMA((3 * tiles,)),
        ],
        compiler_params=params(0),
        cost_estimate=cost(2 * block * block * channels, 2 * block * (block + 2 * channels)),
        name="mix_first",
    )(in_hbm(factor), in_hbm(blocked))


def spread_factor(factor_two):
    here, n, _ = factor_two.shape
    groups = here // 16
    wide = n * 16
    turned = factor_two.reshape(groups, 16, n, n).transpose(0, 2, 1, 3).reshape(groups, wide, n)

    def body(in_ref, out_ref):
        col = lax.broadcasted_iota(jnp.int32, (n, wide), 1)
        row = lax.broadcasted_iota(jnp.int32, (n, wide), 0)
        pick = jnp.where(col // 16 == row, 1.0, 0.0).astype(BF)
        r = lax.broadcasted_iota(jnp.int32, (wide, wide), 0)
        c = lax.broadcasted_iota(jnp.int32, (wide, wide), 1)
        same = r % 16 == c % 16
        full = dot(in_ref[0], pick, 1, 0)
        out_ref[0] = jnp.where(same, full, 0.0).astype(BF)

    return pl.pallas_call(
        body,
        grid=(groups,),
        in_specs=[pl.BlockSpec((1, wide, n), lambda g: (g, 0, 0))],
        out_specs=pl.BlockSpec((1, wide, wide), lambda g: (g, 0, 0)),
        out_shape=jax.ShapeDtypeStruct((groups, wide, wide), BF),
        compiler_params=params(),
        cost_estimate=cost(2 * groups * wide * wide * n, 2 * groups * wide * wide),
        name="spread_factor",
    )(turned)


def mix_second(spread, cols, back):
    n, here, channels = cols.shape
    wide = n * 16
    groups = here // 16

    def body(m_ref, in_ref, out_ref):
        rows = in_ref[...].reshape(wide, channels)
        got = dot(m_ref[0], rows, 0 if back else 1, 0).astype(BF)
        out_ref[...] = got.reshape(n, 16, channels)

    blocks = pl.BlockSpec((n, 16, channels), lambda g: (0, g, 0))
    return pl.pallas_call(
        body,
        grid=(groups,),
        in_specs=[pl.BlockSpec((1, wide, wide), lambda g: (g, 0, 0)), blocks],
        out_specs=blocks,
        out_shape=pltpu.HBM(cols.shape, BF) if back else jax.ShapeDtypeStruct(cols.shape, BF),
        compiler_params=params(),
        cost_estimate=cost(
            2 * groups * wide * wide * channels, 4 * cols.size + 2 * groups * wide * wide
        ),
        name="mix_second_back" if back else "mix_second",
    )(spread, cols)


def grad_second(grads, firsts, scale):
    n, here, channels = grads.shape
    wide = n * 16
    groups = here // 16

    def body(g_ref, u_ref, out_ref):
        g = g_ref[...].reshape(wide, channels)
        u = u_ref[...].reshape(wide, channels)
        full = dot(g, u, 1, 1)
        r = lax.broadcasted_iota(jnp.int32, (wide, wide), 0)
        c = lax.broadcasted_iota(jnp.int32, (wide, wide), 1)
        kept = jnp.where(r % 16 == c % 16, full, 0.0)
        row = lax.broadcasted_iota(jnp.int32, (wide, n), 0)
        col = lax.broadcasted_iota(jnp.int32, (wide, n), 1)
        pick = jnp.where(row // 16 == col, 1.0, 0.0)
        out_ref[0] = dot(kept, pick, 1, 0, precision=lax.Precision.HIGHEST) * scale

    out = pl.pallas_call(
        body,
        grid=(groups,),
        in_specs=[pl.BlockSpec((n, 16, channels), lambda g: (0, g, 0))] * 2,
        out_specs=pl.BlockSpec((1, wide, n), lambda g: (g, 0, 0)),
        out_shape=jax.ShapeDtypeStruct((groups, wide, n), F32),
        compiler_params=params(),
        cost_estimate=cost(2 * groups * wide * wide * channels, 4 * grads.size),
        name="grad_second",
    )(grads, firsts)
    return out.reshape(groups, n, 16, n).transpose(0, 2, 1, 3).reshape(here, n, n)


def middle(half, blocked, incoming, mixed, up_blocks, down_blocks):
    groups, width, inner = up_blocks.shape
    sub = inner // groups
    rows, channels = blocked.shape
    step = min(256, rows)
    last = rows // step - 1

    def body(half_ref, x_ref, g_ref, v_ref, up_ref, down_ref, dv_ref, r_ref, kept_ref, sent_ref, w):
        i = pl.program_id(0)

        @pl.when(i == 0)
        def _():
            w[...] = jnp.zeros_like(w)

        x = x_ref[...].astype(F32)
        g = g_ref[...]
        v = v_ref[...].astype(F32)
        sx = sigmoid(x)
        gate = x * sx
        h = (x + v * gate).astype(BF)
        h_parts = [h[:, b * width : (b + 1) * width] for b in range(groups)]
        g_parts = [g[:, b * width : (b + 1) * width] for b in range(groups)]
        acts, slopes, back = [], [], []
        for b in range(groups):
            a = dot(h_parts[b], up_ref[b], 1, 0)
            s = sigmoid(a)
            q = a * s
            acts.append(q.astype(BF))
            slopes.append(s + q * (1.0 - s))
            back.append(dot(g_parts[b], down_ref[b], 1, 1))
        grads = []
        for b in range(groups):
            lanes = slice(b * sub, (b + 1) * sub)
            perm = jnp.concatenate([acts[p][:, lanes] for p in range(groups)], axis=1)
            w[1, b] += dot(g_parts[b], perm, 0, 0)
            dq = jnp.concatenate([back[p][:, lanes] for p in range(groups)], axis=1)
            da = (dq * slopes[b]).astype(BF)
            w[0, b] += dot(h_parts[b], da, 0, 0)
            grads.append(dot(da, up_ref[b], 1, 1))
        dh = (g.astype(F32) + jnp.concatenate(grads, axis=1)).astype(BF).astype(F32)
        dv_ref[...] = (dh * gate).astype(BF)
        r_ref[...] = (dh * (1.0 + v * (sx + gate * (1.0 - sx)))).astype(BF)

        @pl.when(i == last)
        def _():
            kept_ref[...] = w[half_ref[0]].astype(BF)
            sent_ref[...] = w[1 - half_ref[0]].astype(BF)

    block = pl.BlockSpec((step, channels), lambda i: (i, 0))
    full = pl.BlockSpec(up_blocks.shape, lambda i: (0, 0, 0))
    hidden = rows * groups * inner
    return pl.pallas_call(
        body,
        grid=(last + 1,),
        in_specs=[
            SCALAR,
            block,
            block,
            block,
            full,
            pl.BlockSpec(down_blocks.shape, lambda i: (0, 0, 0)),
        ],
        out_specs=[block, block, full, full],
        out_shape=[
            pltpu.HBM((rows, channels), BF),
            pltpu.HBM((rows, channels), BF),
            pltpu.HBM(up_blocks.shape, BF),
            pltpu.HBM(up_blocks.shape, BF),
        ],
        scratch_shapes=[pltpu.VMEM((2, groups, width, inner), F32)],
        compiler_params=params(),
        cost_estimate=cost(
            10 * hidden * width, 10 * rows * channels + 8 * groups * width * inner, hidden
        ),
        name="middle",
    )(half, in_hbm(blocked), in_hbm(incoming), mixed, in_hbm(up_blocks), in_hbm(down_blocks))


def bring(arrays, name):
    number = len(arrays)

    def body(*refs):
        sems = refs[-1]
        copies = [
            pltpu.make_async_copy(refs[i], refs[number + i], sems.at[i]) for i in range(number)
        ]
        for c in copies:
            c.start()
        for c in copies:
            c.wait()

    return pl.pallas_call(
        body,
        in_specs=[ANY] * number,
        out_specs=[pl.BlockSpec(memory_space=pltpu.VMEM)] * number,
        out_shape=[pltpu.VMEM(a.shape, a.dtype) for a in arrays],
        scratch_shapes=[pltpu.SemaphoreType.DMA((number,))],
        compiler_params=pltpu.CompilerParams(vmem_limit_bytes=16 * 1024 * 1024),
        cost_estimate=cost(0, sum(2 * a.size * a.dtype.itemsize for a in arrays)),
        name=name,
    )(*[in_hbm(a) for a in arrays])


def finish(factor, grad_first, blocked, gate_grad, scale):
    block, channels = blocked.shape
    tiles = 4
    step = block // tiles

    def body(f, x, r, d_hbm, one_hbm, out_hbm, d, one, out, sems):
        ds = row_copies(d_hbm, d, sems, 0, tiles)
        ones = row_copies(one, one_hbm, sems, tiles, tiles)
        outs = row_copies(out, out_hbm, sems, 2 * tiles, tiles)
        for c in ds:
            c.start()
        for t in range(tiles):
            at = slice(t * step, (t + 1) * step)
            ds[t].wait()
            one[at, :] = dot(d[at, :], x[...], 1, 1) * scale
            ones[t].start()
        for t in range(tiles):
            at = slice(t * step, (t + 1) * step)
            total = dot(f[:, at], d[...], 0, 0) + r[at, :].astype(F32)
            out[at, :] = total.astype(BF)
            outs[t].start()
        for c in ones + outs:
            c.wait()

    vmem = pl.BlockSpec(memory_space=pltpu.VMEM)
    return pl.pallas_call(
        body,
        in_specs=[vmem, vmem, vmem, ANY],
        out_specs=[ANY] * 2,
        out_shape=[pltpu.HBM((block, block), F32), pltpu.HBM((block, channels), BF)],
        scratch_shapes=[
            pltpu.VMEM((block, channels), BF),
            pltpu.VMEM((block, block), F32),
            pltpu.VMEM((block, channels), BF),
            pltpu.SemaphoreType.DMA((3 * tiles,)),
        ],
        compiler_params=params(0),
        cost_estimate=cost(4 * block * block * channels, 6 * block * block + 8 * block * channels),
        name="finish",
    )(
        *[pltpu.with_memory_space_constraint(a, pltpu.VMEM) for a in (factor, blocked, gate_grad)],
        grad_first,
    )


def radices(count):
    steps, stride = [], 1
    while stride < count:
        radix = 4 if stride >= 4 and count // stride == 4 else 2
        steps.append((stride, radix))
        stride *= radix
    return steps


def swap(values, count, stride, s):
    return lax.ppermute(values, "seq", [(i, i ^ (stride * s)) for i in range(count)])


def scatter_step(total, count, stride, radix, after=None):
    digit = (lax.axis_index("seq") // stride) % radix
    cut = total.reshape(radix, total.shape[0] // radix, total.shape[1])
    kept = lax.dynamic_index_in_dim(cut, digit, 0, keepdims=False)
    got = []
    for s in range(1, radix):
        send = lax.dynamic_index_in_dim(cut, digit ^ s, 0, keepdims=False).astype(BF)
        got.append(swap(send, count, stride, s))
    if after is not None:
        got, after = lax.optimization_barrier((got, after))
    for g in got:
        kept = kept + g.astype(F32)
    return kept


def gather_step(share, count, stride, radix):
    digit = (lax.axis_index("seq") // stride) % radix
    got = [share] + [swap(share, count, stride, s) for s in range(1, radix)]
    if radix == 2:
        low = jnp.where(digit == 0, got[0], got[1])
        high = jnp.where(digit == 0, got[1], got[0])
        return jnp.concatenate([low, high], axis=0)
    whole = jnp.zeros((radix,) + share.shape, share.dtype)
    for s in range(radix):
        whole = lax.dynamic_update_index_in_dim(whole, got[s], digit ^ s, 0)
    return whole.reshape(radix * share.shape[0], share.shape[1])


def write_weights(total, up_shape, down_shape, scale):
    groups, width, inner = up_shape

    def body(up_in, down_in, up_ref, down_ref):
        up_ref[0] = up_in[...].astype(F32) * scale
        down_ref[0] = (down_in[...].astype(F32) * scale).T

    return pl.pallas_call(
        body,
        grid=(groups,),
        in_specs=[
            pl.BlockSpec((width, inner), lambda b: (b, 0)),
            pl.BlockSpec((width, inner), lambda b: (groups + b, 0)),
        ],
        out_specs=[
            pl.BlockSpec((1, width, inner), lambda b: (b, 0, 0)),
            pl.BlockSpec((1, inner, width), lambda b: (b, 0, 0)),
        ],
        out_shape=[
            jax.ShapeDtypeStruct(up_shape, F32),
            jax.ShapeDtypeStruct(down_shape, F32),
        ],
        compiler_params=params(),
        cost_estimate=cost(groups * width * inner, 12 * groups * width * inner),
        name="write_weights",
    )(total, total)


def on_device(tokens, cotangent, factor_one, factor_two, up_blocks, down_blocks):
    count = lax.axis_size("seq")
    block, channels = factor_one.shape[1], tokens.shape[1]
    here = block // count
    scale = float(count * tokens.shape[0]) ** (-0.5)
    factor = factor_one.reshape(block, block)
    grouped = here % 16 == 0

    def exchange(values):
        cut = values.reshape(count, here, channels)
        return lax.all_to_all(cut, "seq", split_axis=0, concat_axis=0, tiled=True)

    if grouped:
        spread = spread_factor(factor_two)

    def second(cols, back):
        if grouped:
            return mix_second(spread, cols, back)
        names = "kmj,mkc->jkc" if back else "kmj,jkc->mkc"
        return jnp.einsum(names, factor_two, cols, preferred_element_type=F32).astype(BF)

    def second_grad(grads, firsts):
        if grouped:
            return grad_second(grads, firsts, scale)
        return jnp.einsum("mkc,jkc->kmj", grads, firsts, preferred_element_type=F32) * scale

    half = (lax.axis_index("seq") % 2).astype(jnp.int32).reshape(1)
    firsts = exchange(mix_first(factor, tokens))
    mixed = exchange(second(firsts, False)).reshape(block, channels)
    dv, gate_grad, kept, sent = middle(half, tokens, cotangent, mixed, up_blocks, down_blocks)
    grad_mixed = exchange(dv)
    back = second(grad_mixed, True)
    inner = kept.shape[-1]
    total = kept.astype(F32) + swap(sent, count, 1, 1).astype(F32)
    total = total.reshape(-1, inner)
    steps = radices(count)
    for step in steps[1:-1]:
        total = scatter_step(total, count, *step)
    total = scatter_step(total, count, *steps[-1], after=back).astype(BF)
    back, total, factor_late, tokens_late, gate_late = lax.optimization_barrier(
        (back, total, factor, tokens, gate_grad)
    )
    for step in reversed(steps):
        total = gather_step(total, count, *step)
    grad_first = exchange(back).reshape(block, channels)
    grad_up, grad_down = write_weights(total, up_blocks.shape, down_blocks.shape, scale)
    two = second_grad(grad_mixed, firsts)
    held = bring([factor_late, tokens_late, gate_late], "bring_last")
    one, grad_tokens = finish(held[0], grad_first, held[1], held[2], scale)
    return (grad_tokens, one.reshape(1, block, block), two, grad_up, grad_down)


def solution(mesh):
    return jax.shard_map(
        on_device,
        mesh=mesh,
        in_specs=(
            P(("grp", "seq"), None),
            P(("grp", "seq"), None),
            P("seq", None, None),
            P("seq", None, None),
            P(),
            P(),
        ),
        out_specs=(
            P(("grp", "seq"), None),
            P(("grp", "seq"), None, None),
            P(("grp", "seq"), None, None),
            P("grp", None, None),
            P("grp", None, None),
        ),
        check_vma=False,
    )
```

```python
import jax
import jax.numpy as jnp
from jax import lax
from jax.experimental import pallas as pl
from jax.experimental.pallas import tpu as pltpu
from jax.sharding import PartitionSpec as P

BF = jnp.bfloat16
F32 = jnp.float32
VMEM_BYTES = 40 * 1024 * 1024
ANY = pl.BlockSpec(memory_space=pl.ANY)
VMEM = pl.BlockSpec(memory_space=pltpu.VMEM)
SCALAR = pl.BlockSpec(memory_space=pltpu.SMEM)


def in_hbm(array):
    return pltpu.with_memory_space_constraint(array, pltpu.HBM)


def in_vmem(array):
    return pltpu.with_memory_space_constraint(array, pltpu.VMEM)


def sigmoid(z):
    return 0.5 + 0.5 * jnp.tanh(0.5 * z)


def dot(a, b, ca, cb, **kw):
    return lax.dot_general(a, b, (((ca,), (cb,)), ((), ())), preferred_element_type=F32, **kw)


def params(steps=1):
    return pltpu.CompilerParams(
        dimension_semantics=("arbitrary",) * steps, vmem_limit_bytes=VMEM_BYTES
    )


def cost(flops, moved, trans=0):
    return pl.CostEstimate(flops=int(flops), bytes_accessed=int(moved), transcendentals=int(trans))


def row_copies(src, dst, sems, first, parts):
    rows = src.shape[0] // parts
    return [
        pltpu.make_async_copy(
            src.at[pl.ds(i * rows, rows)], dst.at[pl.ds(i * rows, rows)], sems.at[first + i]
        )
        for i in range(parts)
    ]


def mix_first(factor, blocked):
    block, channels = factor.shape[0], blocked.shape[1]
    tiles = 4
    step = block // tiles

    def body(f_hbm, x_hbm, u_hbm, f_all, x_all, u_all, sems):
        xs = row_copies(x_hbm, x_all, sems, 0, tiles)
        fs = row_copies(f_hbm, f_all, sems, tiles, tiles)
        us = row_copies(u_all, u_hbm, sems, 2 * tiles, tiles)
        for c in xs + fs:
            c.start()
        for c in xs:
            c.wait()
        for t in range(tiles):
            fs[t].wait()
            at = slice(t * step, (t + 1) * step)
            u_all[at, :] = dot(f_all[at, :], x_all[...], 1, 0).astype(BF)
            us[t].start()
        for c in us:
            c.wait()

    return pl.pallas_call(
        body,
        in_specs=[ANY, ANY],
        out_specs=ANY,
        out_shape=pltpu.HBM((block, channels), BF),
        scratch_shapes=[
            pltpu.VMEM((block, block), BF),
            pltpu.VMEM((block, channels), BF),
            pltpu.VMEM((block, channels), BF),
            pltpu.SemaphoreType.DMA((3 * tiles,)),
        ],
        compiler_params=params(0),
        cost_estimate=cost(2 * block * block * channels, 2 * block * (block + 2 * channels)),
        name="mix_first",
    )(in_hbm(factor), in_hbm(blocked))


def spread_factor(factor_two):
    here, n, _ = factor_two.shape
    groups = here // 16
    wide = n * 16
    turned = factor_two.reshape(groups, 16, n, n).transpose(0, 2, 1, 3).reshape(groups, wide, n)

    def body(in_ref, out_ref):
        col = lax.broadcasted_iota(jnp.int32, (n, wide), 1)
        row = lax.broadcasted_iota(jnp.int32, (n, wide), 0)
        pick = jnp.where(col // 16 == row, 1.0, 0.0).astype(BF)
        r = lax.broadcasted_iota(jnp.int32, (wide, wide), 0)
        c = lax.broadcasted_iota(jnp.int32, (wide, wide), 1)
        same = r % 16 == c % 16
        full = dot(in_ref[0], pick, 1, 0)
        out_ref[0] = jnp.where(same, full, 0.0).astype(BF)

    return pl.pallas_call(
        body,
        grid=(groups,),
        in_specs=[pl.BlockSpec((1, wide, n), lambda g: (g, 0, 0))],
        out_specs=pl.BlockSpec((1, wide, wide), lambda g: (g, 0, 0)),
        out_shape=jax.ShapeDtypeStruct((groups, wide, wide), BF),
        compiler_params=params(),
        cost_estimate=cost(2 * groups * wide * wide * n, 2 * groups * wide * wide),
        name="spread_factor",
    )(turned)


def mix_second(spread, cols, back):
    n, here, channels = cols.shape
    wide = n * 16
    groups = here // 16

    def body(m_ref, in_ref, out_hbm, out, sems):
        copies = []
        for g in range(groups):
            at = pl.ds(g * 16, 16)
            rows = in_ref[:, at, :].reshape(wide, channels)
            got = dot(m_ref[g], rows, 0 if back else 1, 0).astype(BF)
            out[:, at, :] = got.reshape(n, 16, channels)
            copies.append(
                pltpu.make_async_copy(out.at[:, at, :], out_hbm.at[:, at, :], sems.at[g])
            )
            copies[-1].start()
        for c in copies:
            c.wait()

    return pl.pallas_call(
        body,
        in_specs=[VMEM, VMEM],
        out_specs=ANY,
        out_shape=pltpu.HBM(cols.shape, BF),
        scratch_shapes=[pltpu.VMEM(cols.shape, BF), pltpu.SemaphoreType.DMA((groups,))],
        compiler_params=params(0),
        cost_estimate=cost(
            2 * groups * wide * wide * channels, 4 * cols.size + 2 * groups * wide * wide
        ),
        name="mix_second_back" if back else "mix_second",
    )(in_vmem(spread), in_vmem(cols))


def grad_second(grads, firsts, scale):
    n, here, channels = grads.shape
    wide = n * 16
    groups = here // 16

    def body(g_ref, u_ref, out_ref):
        r = lax.broadcasted_iota(jnp.int32, (wide, wide), 0)
        c = lax.broadcasted_iota(jnp.int32, (wide, wide), 1)
        same = r % 16 == c % 16
        row = lax.broadcasted_iota(jnp.int32, (wide, n), 0)
        col = lax.broadcasted_iota(jnp.int32, (wide, n), 1)
        pick = jnp.where(row // 16 == col, 1.0, 0.0)
        for k in range(groups):
            at = pl.ds(k * 16, 16)
            g = g_ref[:, at, :].reshape(wide, channels)
            u = u_ref[:, at, :].reshape(wide, channels)
            kept = jnp.where(same, dot(g, u, 1, 1), 0.0)
            out_ref[k] = dot(kept, pick, 1, 0, precision=lax.Precision.HIGHEST) * scale

    out = pl.pallas_call(
        body,
        in_specs=[VMEM, VMEM],
        out_specs=VMEM,
        out_shape=jax.ShapeDtypeStruct((groups, wide, n), F32),
        compiler_params=params(0),
        cost_estimate=cost(2 * groups * wide * wide * channels, 4 * grads.size),
        name="grad_second",
    )(in_vmem(grads), in_vmem(firsts))
    return out.reshape(groups, n, 16, n).transpose(0, 2, 1, 3).reshape(here, n, n)


def middle(half, blocked, incoming, mixed, up_blocks, down_blocks):
    groups, width, inner = up_blocks.shape
    sub = inner // groups
    rows, channels = blocked.shape
    step = min(256, rows)
    tiles = rows // step

    def body(half_ref, x_ref, g_ref, v_ref, up_ref, down_ref, dv_hbm, r_ref, kept_ref, sent_ref, *tmp):
        dv, w, sems = tmp
        w[...] = jnp.zeros_like(w)

        def send(t):
            at = pl.ds(t * step, step)
            return pltpu.make_async_copy(dv.at[at], dv_hbm.at[at], sems.at[t])

        def tile(t, carry):
            at = pl.ds(pl.multiple_of(t * step, step), step)
            x = x_ref[at, :].astype(F32)
            g = g_ref[at, :]
            v = v_ref[at, :].astype(F32)
            sx = sigmoid(x)
            gate = x * sx
            h = (x + v * gate).astype(BF)
            h_parts = [h[:, b * width : (b + 1) * width] for b in range(groups)]
            g_parts = [g[:, b * width : (b + 1) * width] for b in range(groups)]
            acts, slopes, back = [], [], []
            for b in range(groups):
                a = dot(h_parts[b], up_ref[b], 1, 0)
                s = sigmoid(a)
                q = a * s
                acts.append(q.astype(BF))
                slopes.append(s + q * (1.0 - s))
                back.append(dot(g_parts[b], down_ref[b], 1, 1))
            grads = []
            for b in range(groups):
                lanes = slice(b * sub, (b + 1) * sub)
                perm = jnp.concatenate([acts[p][:, lanes] for p in range(groups)], axis=1)
                w[1, b] += dot(g_parts[b], perm, 0, 0)
                dq = jnp.concatenate([back[p][:, lanes] for p in range(groups)], axis=1)
                da = (dq * slopes[b]).astype(BF)
                w[0, b] += dot(h_parts[b], da, 0, 0)
                grads.append(dot(da, up_ref[b], 1, 1))
            dh = (g.astype(F32) + jnp.concatenate(grads, axis=1)).astype(BF).astype(F32)
            dv[at, :] = (dh * gate).astype(BF)
            send(t).start()
            r_ref[at, :] = (dh * (1.0 + v * (sx + gate * (1.0 - sx)))).astype(BF)
            return carry

        lax.fori_loop(0, tiles, tile, 0)
        kept_ref[...] = w[half_ref[0]].astype(BF)
        sent_ref[...] = w[1 - half_ref[0]].astype(BF)
        for t in range(tiles):
            send(t).wait()

    hidden = rows * groups * inner
    return pl.pallas_call(
        body,
        in_specs=[SCALAR] + [VMEM] * 5,
        out_specs=[ANY, VMEM, VMEM, VMEM],
        out_shape=[
            pltpu.HBM((rows, channels), BF),
            pltpu.VMEM((rows, channels), BF),
            pltpu.VMEM(up_blocks.shape, BF),
            pltpu.VMEM(up_blocks.shape, BF),
        ],
        scratch_shapes=[
            pltpu.VMEM((rows, channels), BF),
            pltpu.VMEM((2, groups, width, inner), F32),
            pltpu.SemaphoreType.DMA((tiles,)),
        ],
        compiler_params=params(0),
        cost_estimate=cost(
            10 * hidden * width, 10 * rows * channels + 8 * groups * width * inner, hidden
        ),
        name="middle",
    )(half, *[in_vmem(a) for a in (blocked, incoming, mixed, up_blocks, down_blocks)])


def bring(arrays, name):
    number = len(arrays)

    def body(*refs):
        sems = refs[-1]
        copies = [
            pltpu.make_async_copy(refs[i], refs[number + i], sems.at[i]) for i in range(number)
        ]
        for c in copies:
            c.start()
        for c in copies:
            c.wait()

    return pl.pallas_call(
        body,
        in_specs=[ANY] * number,
        out_specs=[pl.BlockSpec(memory_space=pltpu.VMEM)] * number,
        out_shape=[pltpu.VMEM(a.shape, a.dtype) for a in arrays],
        scratch_shapes=[pltpu.SemaphoreType.DMA((number,))],
        compiler_params=pltpu.CompilerParams(vmem_limit_bytes=16 * 1024 * 1024),
        cost_estimate=cost(0, sum(2 * a.size * a.dtype.itemsize for a in arrays)),
        name=name,
    )(*[in_hbm(a) for a in arrays])


def finish(factor, grad_first, blocked, gate_grad, scale):
    block, channels = blocked.shape
    tiles = 4
    step = block // tiles

    def body(f, x, r, d, one_hbm, out_hbm, one, out, sems):
        ones = row_copies(one, one_hbm, sems, 0, tiles)
        outs = row_copies(out, out_hbm, sems, tiles, tiles)
        for t in range(tiles):
            at = slice(t * step, (t + 1) * step)
            one[at, :] = dot(d[at, :], x[...], 1, 1) * scale
            ones[t].start()
        for t in range(tiles):
            at = slice(t * step, (t + 1) * step)
            total = dot(f[:, at], d[...], 0, 0) + r[at, :].astype(F32)
            out[at, :] = total.astype(BF)
            outs[t].start()
        for c in ones + outs:
            c.wait()

    return pl.pallas_call(
        body,
        in_specs=[VMEM] * 4,
        out_specs=[ANY] * 2,
        out_shape=[pltpu.HBM((block, block), F32), pltpu.HBM((block, channels), BF)],
        scratch_shapes=[
            pltpu.VMEM((block, block), F32),
            pltpu.VMEM((block, channels), BF),
            pltpu.SemaphoreType.DMA((2 * tiles,)),
        ],
        compiler_params=params(0),
        cost_estimate=cost(4 * block * block * channels, 6 * block * block + 8 * block * channels),
        name="finish",
    )(*[in_vmem(a) for a in (factor, blocked, gate_grad, grad_first)])


def radices(count):
    steps, stride = [], 1
    while stride < count:
        radix = 4 if stride >= 4 and count // stride == 4 else 2
        steps.append((stride, radix))
        stride *= radix
    return steps


def swap(values, count, stride, s):
    return lax.ppermute(values, "seq", [(i, i ^ (stride * s)) for i in range(count)])


def add_and_cut(terms, digit, radix):
    rows, columns = terms[0].shape
    share = rows // radix

    def body(digit_ref, *refs):
        ins, kept_ref, outs = refs[: len(terms)], refs[len(terms)], refs[len(terms) + 1 :]

        def part(s):
            at = pl.ds(pl.multiple_of((digit_ref[0] ^ s) * share, share), share)
            total = ins[0][at, :].astype(F32)
            for ref in ins[1:]:
                total = total + ref[at, :].astype(F32)
            return total

        kept_ref[...] = part(0)
        for s, ref in enumerate(outs):
            ref[...] = part(s + 1).astype(BF)

    return pl.pallas_call(
        body,
        in_specs=[SCALAR] + [VMEM] * len(terms),
        out_specs=[VMEM] * radix,
        out_shape=[jax.ShapeDtypeStruct((share, columns), F32)]
        + [jax.ShapeDtypeStruct((share, columns), BF)] * (radix - 1),
        compiler_params=pltpu.CompilerParams(vmem_limit_bytes=16 * 1024 * 1024),
        cost_estimate=cost(rows * columns, 8 * rows * columns),
        name="add_and_cut",
    )(digit.reshape(1), *terms)


def scatter_step(terms, count, stride, radix):
    digit = (lax.axis_index("seq").astype(jnp.int32) // stride) % radix
    kept, *send = add_and_cut(terms, digit, radix)
    return [kept] + [swap(a, count, stride, s + 1) for s, a in enumerate(send)]


def gather_step(share, count, stride, radix, after=()):
    digit = (lax.axis_index("seq") // stride) % radix
    got = [share] + [swap(share, count, stride, s) for s in range(1, radix)]
    got, after = lax.optimization_barrier((got, after))
    if radix == 2:
        low = jnp.where(digit == 0, got[0], got[1])
        high = jnp.where(digit == 0, got[1], got[0])
        return jnp.concatenate([low, high], axis=0)
    whole = jnp.zeros((radix,) + share.shape, share.dtype)
    for s in range(radix):
        whole = lax.dynamic_update_index_in_dim(whole, got[s], digit ^ s, 0)
    return whole.reshape(radix * share.shape[0], share.shape[1])


def write_weights(total, up_shape, down_shape, scale):
    groups, width, inner = up_shape

    def body(up_in, down_in, up_ref, down_ref):
        up_ref[0] = up_in[...].astype(F32) * scale
        down_ref[0] = (down_in[...].astype(F32) * scale).T

    return pl.pallas_call(
        body,
        grid=(groups,),
        in_specs=[
            pl.BlockSpec((width, inner), lambda b: (b, 0)),
            pl.BlockSpec((width, inner), lambda b: (groups + b, 0)),
        ],
        out_specs=[
            pl.BlockSpec((1, width, inner), lambda b: (b, 0, 0)),
            pl.BlockSpec((1, inner, width), lambda b: (b, 0, 0)),
        ],
        out_shape=[
            jax.ShapeDtypeStruct(up_shape, F32),
            jax.ShapeDtypeStruct(down_shape, F32),
        ],
        compiler_params=params(),
        cost_estimate=cost(groups * width * inner, 12 * groups * width * inner),
        name="write_weights",
    )(total, total)


def on_device(tokens, cotangent, factor_one, factor_two, up_blocks, down_blocks):
    count = lax.axis_size("seq")
    block, channels = factor_one.shape[1], tokens.shape[1]
    here = block // count
    scale = float(count * tokens.shape[0]) ** (-0.5)
    factor = factor_one.reshape(block, block)
    grouped = here % 16 == 0

    def exchange(values):
        cut = values.reshape(count, here, channels)
        return lax.all_to_all(cut, "seq", split_axis=0, concat_axis=0, tiled=True)

    if grouped:
        spread = spread_factor(factor_two)

    def second(cols, back):
        if grouped:
            return mix_second(spread, cols, back)
        names = "kmj,mkc->jkc" if back else "kmj,jkc->mkc"
        return jnp.einsum(names, factor_two, cols, preferred_element_type=F32).astype(BF)

    def second_grad(grads, firsts):
        if grouped:
            return grad_second(grads, firsts, scale)
        return jnp.einsum("mkc,jkc->kmj", grads, firsts, preferred_element_type=F32) * scale

    half = (lax.axis_index("seq") % 2).astype(jnp.int32).reshape(1)
    firsts = exchange(mix_first(factor, tokens))
    late = (tokens, cotangent, factor, up_blocks, down_blocks)
    firsts, late = lax.optimization_barrier((firsts, late))
    tokens_v, cotangent_v, factor_v, up_v, down_v = bring(late, "bring")
    mixed = exchange(second(firsts, False)).reshape(block, channels)
    dv, gate_grad, kept, sent = middle(half, tokens_v, cotangent_v, mixed, up_v, down_v)
    grad_mixed = exchange(dv)
    back = second(grad_mixed, True)
    terms = [kept, swap(sent, count, 1, 1)]
    terms = [t.reshape(-1, t.shape[-1]) for t in terms]
    steps = radices(count)
    for step in steps[1:]:
        terms = scatter_step(terms, count, *step)
    terms, back = lax.optimization_barrier((terms, back))
    total = sum(t.astype(F32) for t in terms).astype(BF)
    back, total = lax.optimization_barrier((back, total))
    grad_first = exchange(back).reshape(block, channels)
    two = second_grad(grad_mixed, firsts)
    for step in reversed(steps):
        total = gather_step(total, count, *step, after=two if step == steps[1] else ())
    grad_up, grad_down = write_weights(total, up_blocks.shape, down_blocks.shape, scale)
    one, grad_tokens = finish(factor_v, grad_first, tokens_v, gate_grad, scale)
    return (grad_tokens, one.reshape(1, block, block), two, grad_up, grad_down)


def solution(mesh):
    return jax.shard_map(
        on_device,
        mesh=mesh,
        in_specs=(
            P(("grp", "seq"), None),
            P(("grp", "seq"), None),
            P("seq", None, None),
            P("seq", None, None),
            P(),
            P(),
        ),
        out_specs=(
            P(("grp", "seq"), None),
            P(("grp", "seq"), None, None),
            P(("grp", "seq"), None, None),
            P("grp", None, None),
            P("grp", None, None),
        ),
        check_vma=False,
    )
```

```python
import jax
import jax.numpy as jnp
from jax import lax
from jax.experimental import pallas as pl
from jax.experimental.pallas import tpu as pltpu
from jax.sharding import PartitionSpec as P

BF = jnp.bfloat16
F32 = jnp.float32
VMEM_BYTES = 40 * 1024 * 1024
ANY = pl.BlockSpec(memory_space=pl.ANY)
VMEM = pl.BlockSpec(memory_space=pltpu.VMEM)
SCALAR = pl.BlockSpec(memory_space=pltpu.SMEM)


def in_hbm(array):
    return pltpu.with_memory_space_constraint(array, pltpu.HBM)


def in_vmem(array):
    return pltpu.with_memory_space_constraint(array, pltpu.VMEM)


def sigmoid(z):
    return 0.5 + 0.5 * jnp.tanh(0.5 * z)


def dot(a, b, ca, cb, **kw):
    return lax.dot_general(a, b, (((ca,), (cb,)), ((), ())), preferred_element_type=F32, **kw)


def params(steps=1):
    return pltpu.CompilerParams(
        dimension_semantics=("arbitrary",) * steps, vmem_limit_bytes=VMEM_BYTES
    )


def cost(flops, moved, trans=0):
    return pl.CostEstimate(flops=int(flops), bytes_accessed=int(moved), transcendentals=int(trans))


def row_copies(src, dst, sems, first, parts):
    rows = src.shape[0] // parts
    return [
        pltpu.make_async_copy(
            src.at[pl.ds(i * rows, rows)], dst.at[pl.ds(i * rows, rows)], sems.at[first + i]
        )
        for i in range(parts)
    ]


def mix_first(factor, blocked):
    block, channels = factor.shape[0], blocked.shape[1]
    tiles = 4
    step = block // tiles

    def body(f_hbm, x_hbm, u_hbm, f_all, x_all, u_all, sems):
        xs = row_copies(x_hbm, x_all, sems, 0, tiles)
        fs = row_copies(f_hbm, f_all, sems, tiles, tiles)
        us = row_copies(u_all, u_hbm, sems, 2 * tiles, tiles)
        for c in xs + fs[:1]:
            c.start()
        for c in xs:
            c.wait()
        for c in fs[1:]:
            c.start()
        for t in range(tiles):
            fs[t].wait()
            at = slice(t * step, (t + 1) * step)
            u_all[at, :] = dot(f_all[at, :], x_all[...], 1, 0).astype(BF)
            us[t].start()
        for c in us:
            c.wait()

    return pl.pallas_call(
        body,
        in_specs=[ANY, ANY],
        out_specs=ANY,
        out_shape=pltpu.HBM((block, channels), BF),
        scratch_shapes=[
            pltpu.VMEM((block, block), BF),
            pltpu.VMEM((block, channels), BF),
            pltpu.VMEM((block, channels), BF),
            pltpu.SemaphoreType.DMA((3 * tiles,)),
        ],
        compiler_params=params(0),
        cost_estimate=cost(2 * block * block * channels, 2 * block * (block + 2 * channels)),
        name="mix_first",
    )(in_hbm(factor), in_hbm(blocked))


def spread_factor(factor_two):
    here, n, _ = factor_two.shape
    groups = here // 16
    wide = n * 16
    turned = factor_two.reshape(groups, 16, n, n).transpose(0, 2, 1, 3).reshape(groups, wide, n)

    def body(in_ref, out_ref):
        col = lax.broadcasted_iota(jnp.int32, (n, wide), 1)
        row = lax.broadcasted_iota(jnp.int32, (n, wide), 0)
        pick = jnp.where(col // 16 == row, 1.0, 0.0).astype(BF)
        r = lax.broadcasted_iota(jnp.int32, (wide, wide), 0)
        c = lax.broadcasted_iota(jnp.int32, (wide, wide), 1)
        same = r % 16 == c % 16
        full = dot(in_ref[0], pick, 1, 0)
        out_ref[0] = jnp.where(same, full, 0.0).astype(BF)

    return pl.pallas_call(
        body,
        grid=(groups,),
        in_specs=[pl.BlockSpec((1, wide, n), lambda g: (g, 0, 0))],
        out_specs=pl.BlockSpec((1, wide, wide), lambda g: (g, 0, 0)),
        out_shape=jax.ShapeDtypeStruct((groups, wide, wide), BF),
        compiler_params=params(),
        cost_estimate=cost(2 * groups * wide * wide * n, 2 * groups * wide * wide),
        name="spread_factor",
    )(turned)


def mix_second(spread, cols, back):
    n, here, channels = cols.shape
    wide = n * 16
    groups = here // 16

    def body(m_ref, in_ref, out_hbm, out, sems):
        copies = []
        for g in range(groups):
            at = pl.ds(g * 16, 16)
            rows = in_ref[:, at, :].reshape(wide, channels)
            got = dot(m_ref[g], rows, 0 if back else 1, 0).astype(BF)
            out[:, at, :] = got.reshape(n, 16, channels)
            copies.append(
                pltpu.make_async_copy(out.at[:, at, :], out_hbm.at[:, at, :], sems.at[g])
            )
            copies[-1].start()
        for c in copies:
            c.wait()

    return pl.pallas_call(
        body,
        in_specs=[VMEM, VMEM],
        out_specs=ANY,
        out_shape=pltpu.HBM(cols.shape, BF),
        scratch_shapes=[pltpu.VMEM(cols.shape, BF), pltpu.SemaphoreType.DMA((groups,))],
        compiler_params=params(0),
        cost_estimate=cost(
            2 * groups * wide * wide * channels, 4 * cols.size + 2 * groups * wide * wide
        ),
        name="mix_second_back" if back else "mix_second",
    )(in_vmem(spread), in_vmem(cols))


def grad_second(grads, firsts, scale):
    n, here, channels = grads.shape
    wide = n * 16
    groups = here // 16

    def body(g_ref, u_ref, out_ref):
        r = lax.broadcasted_iota(jnp.int32, (wide, wide), 0)
        c = lax.broadcasted_iota(jnp.int32, (wide, wide), 1)
        same = r % 16 == c % 16
        row = lax.broadcasted_iota(jnp.int32, (wide, n), 0)
        col = lax.broadcasted_iota(jnp.int32, (wide, n), 1)
        pick = jnp.where(row // 16 == col, 1.0, 0.0)
        for k in range(groups):
            at = pl.ds(k * 16, 16)
            g = g_ref[:, at, :].reshape(wide, channels)
            u = u_ref[:, at, :].reshape(wide, channels)
            kept = jnp.where(same, dot(g, u, 1, 1), 0.0)
            out_ref[k] = dot(kept, pick, 1, 0, precision=lax.Precision.HIGHEST) * scale

    out = pl.pallas_call(
        body,
        in_specs=[VMEM, VMEM],
        out_specs=VMEM,
        out_shape=jax.ShapeDtypeStruct((groups, wide, n), F32),
        compiler_params=params(0),
        cost_estimate=cost(2 * groups * wide * wide * channels, 4 * grads.size),
        name="grad_second",
    )(in_vmem(grads), in_vmem(firsts))
    return out.reshape(groups, n, 16, n).transpose(0, 2, 1, 3).reshape(here, n, n)


def middle(half, blocked, incoming, mixed, up_blocks, down_blocks):
    groups, width, inner = up_blocks.shape
    sub = inner // groups
    rows, channels = blocked.shape
    step = min(256, rows)
    tiles = rows // step

    def body(half_ref, x_hbm, g_hbm, v_ref, up_hbm, down_hbm, *refs):
        dv_hbm, r_hbm, kept_hbm, sent_hbm = refs[:4]
        x_ref, g_ref, up_ref, down_ref, dv, r_ref, w, halves, sems = refs[4:]

        def rows_copy(src, dst, kind, t):
            at = pl.ds(t * step, step)
            return pltpu.make_async_copy(src.at[at], dst.at[at], sems.at[kind * tiles + t])

        def whole_copy(src, dst, number):
            return pltpu.make_async_copy(src, dst, sems.at[4 * tiles + number])

        fetch_up = whole_copy(up_hbm, up_ref, 0)
        fetch_down = whole_copy(down_hbm, down_ref, 1)
        rows_copy(x_hbm, x_ref, 0, 0).start()
        fetch_up.start()
        rows_copy(g_hbm, g_ref, 1, 0).start()
        fetch_down.start()
        for t in range(1, tiles):
            rows_copy(x_hbm, x_ref, 0, t).start()
            rows_copy(g_hbm, g_ref, 1, t).start()
        w[...] = jnp.zeros_like(w)
        fetch_up.wait()
        fetch_down.wait()

        def tile(t, carry):
            rows_copy(x_hbm, x_ref, 0, t).wait()
            rows_copy(g_hbm, g_ref, 1, t).wait()
            at = pl.ds(pl.multiple_of(t * step, step), step)
            x = x_ref[at, :].astype(F32)
            g = g_ref[at, :]
            v = v_ref[at, :].astype(F32)
            sx = sigmoid(x)
            gate = x * sx
            h = (x + v * gate).astype(BF)
            h_parts = [h[:, b * width : (b + 1) * width] for b in range(groups)]
            g_parts = [g[:, b * width : (b + 1) * width] for b in range(groups)]
            acts, slopes, back = [], [], []
            for b in range(groups):
                a = dot(h_parts[b], up_ref[b], 1, 0)
                s = sigmoid(a)
                q = a * s
                acts.append(q.astype(BF))
                slopes.append(s + q * (1.0 - s))
                back.append(dot(g_parts[b], down_ref[b], 1, 1))
            grads = []
            for b in range(groups):
                lanes = slice(b * sub, (b + 1) * sub)
                perm = jnp.concatenate([acts[p][:, lanes] for p in range(groups)], axis=1)
                w[1, b] += dot(g_parts[b], perm, 0, 0)
                dq = jnp.concatenate([back[p][:, lanes] for p in range(groups)], axis=1)
                da = (dq * slopes[b]).astype(BF)
                w[0, b] += dot(h_parts[b], da, 0, 0)
                grads.append(dot(da, up_ref[b], 1, 1))
            dh = (g.astype(F32) + jnp.concatenate(grads, axis=1)).astype(BF).astype(F32)
            dv[at, :] = (dh * gate).astype(BF)
            rows_copy(dv, dv_hbm, 2, t).start()
            r_ref[at, :] = (dh * (1.0 + v * (sx + gate * (1.0 - sx)))).astype(BF)
            rows_copy(r_ref, r_hbm, 3, t).start()
            return carry

        lax.fori_loop(0, tiles, tile, 0)
        halves[1] = w[1 - half_ref[0]].astype(BF)
        send = whole_copy(halves.at[1], sent_hbm, 2)
        send.start()
        halves[0] = w[half_ref[0]].astype(BF)
        keep = whole_copy(halves.at[0], kept_hbm, 3)
        keep.start()
        for t in range(tiles):
            rows_copy(dv, dv_hbm, 2, t).wait()
            rows_copy(r_ref, r_hbm, 3, t).wait()
        send.wait()
        keep.wait()

    hidden = rows * groups * inner
    return pl.pallas_call(
        body,
        in_specs=[SCALAR, ANY, ANY, VMEM, ANY, ANY],
        out_specs=[ANY] * 4,
        out_shape=[
            pltpu.HBM((rows, channels), BF),
            pltpu.HBM((rows, channels), BF),
            pltpu.HBM(up_blocks.shape, BF),
            pltpu.HBM(up_blocks.shape, BF),
        ],
        scratch_shapes=[
            pltpu.VMEM((rows, channels), BF),
            pltpu.VMEM((rows, channels), BF),
            pltpu.VMEM(up_blocks.shape, BF),
            pltpu.VMEM(down_blocks.shape, BF),
            pltpu.VMEM((rows, channels), BF),
            pltpu.VMEM((rows, channels), BF),
            pltpu.VMEM((2, groups, width, inner), F32),
            pltpu.VMEM((2, groups, width, inner), BF),
            pltpu.SemaphoreType.DMA((4 * tiles + 4,)),
        ],
        compiler_params=params(0),
        cost_estimate=cost(
            10 * hidden * width, 10 * rows * channels + 8 * groups * width * inner, hidden
        ),
        name="middle",
    )(half, in_hbm(blocked), in_hbm(incoming), in_vmem(mixed), in_hbm(up_blocks), in_hbm(down_blocks))


def finish(factor, grad_first, blocked, gate_grad, scale):
    block, channels = blocked.shape
    tiles = 4
    step = block // tiles

    def body(f_hbm, d_hbm, x_hbm, r_hbm, one_hbm, out_hbm, f, d, x, r, one, out, sems):
        ds = row_copies(d_hbm, d, sems, 0, tiles)
        xs = row_copies(x_hbm, x, sems, tiles, tiles)
        fs = row_copies(f_hbm, f, sems, 2 * tiles, tiles)
        rs = row_copies(r_hbm, r, sems, 3 * tiles, tiles)
        ones = row_copies(one, one_hbm, sems, 4 * tiles, tiles)
        outs = row_copies(out, out_hbm, sems, 5 * tiles, tiles)
        for c in xs + ds:
            c.start()
        for c in xs:
            c.wait()
        for t in range(tiles):
            at = slice(t * step, (t + 1) * step)
            ds[t].wait()
            fs[t].start()
            rs[t].start()
            one[at, :] = dot(d[at, :], x[...], 1, 1) * scale
            ones[t].start()
        for c in fs:
            c.wait()
        for t in range(tiles):
            at = slice(t * step, (t + 1) * step)
            rs[t].wait()
            total = dot(f[:, at], d[...], 0, 0) + r[at, :].astype(F32)
            out[at, :] = total.astype(BF)
            outs[t].start()
        for c in ones + outs:
            c.wait()

    return pl.pallas_call(
        body,
        in_specs=[ANY] * 4,
        out_specs=[ANY] * 2,
        out_shape=[pltpu.HBM((block, block), F32), pltpu.HBM((block, channels), BF)],
        scratch_shapes=[
            pltpu.VMEM((block, block), BF),
            pltpu.VMEM((block, channels), BF),
            pltpu.VMEM((block, channels), BF),
            pltpu.VMEM((block, channels), BF),
            pltpu.VMEM((block, block), F32),
            pltpu.VMEM((block, channels), BF),
            pltpu.SemaphoreType.DMA((6 * tiles,)),
        ],
        compiler_params=params(0),
        cost_estimate=cost(4 * block * block * channels, 6 * block * block + 8 * block * channels),
        name="finish",
    )(in_hbm(factor), in_hbm(grad_first), in_hbm(blocked), in_hbm(gate_grad))


def radices(count):
    steps, stride = [], 1
    while stride < count:
        radix = 4 if stride >= 4 and count // stride == 4 else 2
        steps.append((stride, radix))
        stride *= radix
    return steps


def swap(values, count, stride, s):
    return lax.ppermute(values, "seq", [(i, i ^ (stride * s)) for i in range(count)])


def add_and_cut(terms, digit, radix):
    rows, columns = terms[0].shape
    share = rows // radix

    def body(digit_ref, *refs):
        ins, kept_ref, outs = refs[: len(terms)], refs[len(terms)], refs[len(terms) + 1 :]

        def part(s):
            at = pl.ds(pl.multiple_of((digit_ref[0] ^ s) * share, share), share)
            total = ins[0][at, :].astype(F32)
            for ref in ins[1:]:
                total = total + ref[at, :].astype(F32)
            return total

        kept_ref[...] = part(0)
        for s, ref in enumerate(outs):
            ref[...] = part(s + 1).astype(BF)

    return pl.pallas_call(
        body,
        in_specs=[SCALAR] + [VMEM] * len(terms),
        out_specs=[VMEM] * radix,
        out_shape=[jax.ShapeDtypeStruct((share, columns), F32)]
        + [jax.ShapeDtypeStruct((share, columns), BF)] * (radix - 1),
        compiler_params=pltpu.CompilerParams(vmem_limit_bytes=16 * 1024 * 1024),
        cost_estimate=cost(rows * columns, 8 * rows * columns),
        name="add_and_cut",
    )(digit.reshape(1), *terms)


def scatter_step(terms, count, stride, radix):
    digit = (lax.axis_index("seq").astype(jnp.int32) // stride) % radix
    kept, *send = add_and_cut(terms, digit, radix)
    return [kept] + [swap(a, count, stride, s + 1) for s, a in enumerate(send)]


def gather_step(share, count, stride, radix, after=()):
    digit = (lax.axis_index("seq") // stride) % radix
    got = [share] + [swap(share, count, stride, s) for s in range(1, radix)]
    got, after = lax.optimization_barrier((got, after))
    if radix == 2:
        low = jnp.where(digit == 0, got[0], got[1])
        high = jnp.where(digit == 0, got[1], got[0])
        return jnp.concatenate([low, high], axis=0)
    whole = jnp.zeros((radix,) + share.shape, share.dtype)
    for s in range(radix):
        whole = lax.dynamic_update_index_in_dim(whole, got[s], digit ^ s, 0)
    return whole.reshape(radix * share.shape[0], share.shape[1])


def write_weights(total, up_shape, down_shape, scale):
    groups, width, inner = up_shape

    def body(up_in, down_in, up_ref, down_ref):
        up_ref[0] = up_in[...].astype(F32) * scale
        down_ref[0] = (down_in[...].astype(F32) * scale).T

    return pl.pallas_call(
        body,
        grid=(groups,),
        in_specs=[
            pl.BlockSpec((width, inner), lambda b: (b, 0)),
            pl.BlockSpec((width, inner), lambda b: (groups + b, 0)),
        ],
        out_specs=[
            pl.BlockSpec((1, width, inner), lambda b: (b, 0, 0)),
            pl.BlockSpec((1, inner, width), lambda b: (b, 0, 0)),
        ],
        out_shape=[
            jax.ShapeDtypeStruct(up_shape, F32),
            jax.ShapeDtypeStruct(down_shape, F32),
        ],
        compiler_params=params(),
        cost_estimate=cost(groups * width * inner, 12 * groups * width * inner),
        name="write_weights",
    )(total, total)


def on_device(tokens, cotangent, factor_one, factor_two, up_blocks, down_blocks):
    count = lax.axis_size("seq")
    block, channels = factor_one.shape[1], tokens.shape[1]
    here = block // count
    scale = float(count * tokens.shape[0]) ** (-0.5)
    factor = factor_one.reshape(block, block)
    grouped = here % 16 == 0

    def exchange(values):
        cut = values.reshape(count, here, channels)
        return lax.all_to_all(cut, "seq", split_axis=0, concat_axis=0, tiled=True)

    if grouped:
        spread = spread_factor(factor_two)

    def second(cols, back):
        if grouped:
            return mix_second(spread, cols, back)
        names = "kmj,mkc->jkc" if back else "kmj,jkc->mkc"
        return jnp.einsum(names, factor_two, cols, preferred_element_type=F32).astype(BF)

    def second_grad(grads, firsts):
        if grouped:
            return grad_second(grads, firsts, scale)
        return jnp.einsum("mkc,jkc->kmj", grads, firsts, preferred_element_type=F32) * scale

    half = (lax.axis_index("seq") % 2).astype(jnp.int32).reshape(1)
    firsts = exchange(mix_first(factor, tokens))
    mixed = exchange(second(firsts, False)).reshape(block, channels)
    dv, gate_grad, kept, sent = middle(half, tokens, cotangent, mixed, up_blocks, down_blocks)
    grad_mixed = exchange(dv)
    back = second(grad_mixed, True)
    terms = [kept, swap(sent, count, 1, 1)]
    terms = [t.reshape(-1, t.shape[-1]) for t in terms]
    steps = radices(count)
    for step in steps[1:]:
        terms = scatter_step(terms, count, *step)
    terms, back = lax.optimization_barrier((terms, back))
    total = sum(t.astype(F32) for t in terms).astype(BF)
    back, total = lax.optimization_barrier((back, total))
    grad_first = exchange(back).reshape(block, channels)
    two = second_grad(grad_mixed, firsts)
    for step in reversed(steps):
        total = gather_step(total, count, *step, after=two if step == steps[1] else ())
    grad_up, grad_down = write_weights(total, up_blocks.shape, down_blocks.shape, scale)
    one, grad_tokens = finish(factor, grad_first, tokens, gate_grad, scale)
    return (grad_tokens, one.reshape(1, block, block), two, grad_up, grad_down)


def solution(mesh):
    return jax.shard_map(
        on_device,
        mesh=mesh,
        in_specs=(
            P(("grp", "seq"), None),
            P(("grp", "seq"), None),
            P("seq", None, None),
            P("seq", None, None),
            P(),
            P(),
        ),
        out_specs=(
            P(("grp", "seq"), None),
            P(("grp", "seq"), None, None),
            P(("grp", "seq"), None, None),
            P("grp", None, None),
            P("grp", None, None),
        ),
        check_vma=False,
    )
```

```python
import jax
import jax.numpy as jnp
from jax import lax
from jax.experimental import pallas as pl
from jax.experimental.pallas import tpu as pltpu
from jax.sharding import PartitionSpec as P

BF = jnp.bfloat16
F32 = jnp.float32
VMEM_BYTES = 40 * 1024 * 1024
ANY = pl.BlockSpec(memory_space=pl.ANY)
VMEM = pl.BlockSpec(memory_space=pltpu.VMEM)
SCALAR = pl.BlockSpec(memory_space=pltpu.SMEM)


def in_hbm(array):
    return pltpu.with_memory_space_constraint(array, pltpu.HBM)


def in_vmem(array):
    return pltpu.with_memory_space_constraint(array, pltpu.VMEM)


def sigmoid(z):
    return 0.5 + 0.5 * jnp.tanh(0.5 * z)


def dot(a, b, ca, cb, **kw):
    return lax.dot_general(a, b, (((ca,), (cb,)), ((), ())), preferred_element_type=F32, **kw)


def params(steps=1):
    return pltpu.CompilerParams(
        dimension_semantics=("arbitrary",) * steps, vmem_limit_bytes=VMEM_BYTES
    )


def cost(flops, moved, trans=0):
    return pl.CostEstimate(flops=int(flops), bytes_accessed=int(moved), transcendentals=int(trans))


def row_copies(src, dst, sems, first, parts):
    rows = src.shape[0] // parts
    return [
        pltpu.make_async_copy(
            src.at[pl.ds(i * rows, rows)], dst.at[pl.ds(i * rows, rows)], sems.at[first + i]
        )
        for i in range(parts)
    ]


def mix_first(factor, blocked):
    block, channels = factor.shape[0], blocked.shape[1]
    tiles = 4
    step = block // tiles

    def body(f_hbm, x_hbm, u_hbm, f_all, x_all, u_all, sems):
        xs = row_copies(x_hbm, x_all, sems, 0, tiles)
        fs = row_copies(f_hbm, f_all, sems, tiles, tiles)
        us = row_copies(u_all, u_hbm, sems, 2 * tiles, tiles)
        for c in xs + fs:
            c.start()
        for c in xs:
            c.wait()
        for t in range(tiles):
            fs[t].wait()
            at = slice(t * step, (t + 1) * step)
            u_all[at, :] = dot(f_all[at, :], x_all[...], 1, 0).astype(BF)
            us[t].start()
        for c in us:
            c.wait()

    return pl.pallas_call(
        body,
        in_specs=[ANY, ANY],
        out_specs=ANY,
        out_shape=pltpu.HBM((block, channels), BF),
        scratch_shapes=[
            pltpu.VMEM((block, block), BF),
            pltpu.VMEM((block, channels), BF),
            pltpu.VMEM((block, channels), BF),
            pltpu.SemaphoreType.DMA((3 * tiles,)),
        ],
        compiler_params=params(0),
        cost_estimate=cost(2 * block * block * channels, 2 * block * (block + 2 * channels)),
        name="mix_first",
    )(in_hbm(factor), in_hbm(blocked))


def spread_factor(factor_two):
    here, n, _ = factor_two.shape
    groups = here // 16
    wide = n * 16
    turned = factor_two.reshape(groups, 16, n, n).transpose(0, 2, 1, 3).reshape(groups, wide, n)

    def body(in_ref, out_ref):
        col = lax.broadcasted_iota(jnp.int32, (n, wide), 1)
        row = lax.broadcasted_iota(jnp.int32, (n, wide), 0)
        pick = jnp.where(col // 16 == row, 1.0, 0.0).astype(BF)
        r = lax.broadcasted_iota(jnp.int32, (wide, wide), 0)
        c = lax.broadcasted_iota(jnp.int32, (wide, wide), 1)
        same = r % 16 == c % 16
        full = dot(in_ref[0], pick, 1, 0)
        out_ref[0] = jnp.where(same, full, 0.0).astype(BF)

    return pl.pallas_call(
        body,
        grid=(groups,),
        in_specs=[pl.BlockSpec((1, wide, n), lambda g: (g, 0, 0))],
        out_specs=pl.BlockSpec((1, wide, wide), lambda g: (g, 0, 0)),
        out_shape=jax.ShapeDtypeStruct((groups, wide, wide), BF),
        compiler_params=params(),
        cost_estimate=cost(2 * groups * wide * wide * n, 2 * groups * wide * wide),
        name="spread_factor",
    )(turned)


def mix_second(spread, cols, back):
    n, here, channels = cols.shape
    wide = n * 16
    groups = here // 16

    def body(m_ref, in_ref, out_hbm, out, sems):
        copies = []
        for g in range(groups):
            at = pl.ds(g * 16, 16)
            rows = in_ref[:, at, :].reshape(wide, channels)
            got = dot(m_ref[g], rows, 0 if back else 1, 0).astype(BF)
            out[:, at, :] = got.reshape(n, 16, channels)
            copies.append(
                pltpu.make_async_copy(out.at[:, at, :], out_hbm.at[:, at, :], sems.at[g])
            )
            copies[-1].start()
        for c in copies:
            c.wait()

    return pl.pallas_call(
        body,
        in_specs=[VMEM, VMEM],
        out_specs=ANY,
        out_shape=pltpu.HBM(cols.shape, BF),
        scratch_shapes=[pltpu.VMEM(cols.shape, BF), pltpu.SemaphoreType.DMA((groups,))],
        compiler_params=params(0),
        cost_estimate=cost(
            2 * groups * wide * wide * channels, 4 * cols.size + 2 * groups * wide * wide
        ),
        name="mix_second_back" if back else "mix_second",
    )(in_vmem(spread), in_vmem(cols))


def grad_second(grads, firsts, scale):
    n, here, channels = grads.shape
    wide = n * 16
    groups = here // 16

    def body(g_ref, u_ref, out_ref):
        r = lax.broadcasted_iota(jnp.int32, (wide, wide), 0)
        c = lax.broadcasted_iota(jnp.int32, (wide, wide), 1)
        same = r % 16 == c % 16
        row = lax.broadcasted_iota(jnp.int32, (wide, n), 0)
        col = lax.broadcasted_iota(jnp.int32, (wide, n), 1)
        pick = jnp.where(row // 16 == col, 1.0, 0.0)
        for k in range(groups):
            at = pl.ds(k * 16, 16)
            g = g_ref[:, at, :].reshape(wide, channels)
            u = u_ref[:, at, :].reshape(wide, channels)
            kept = jnp.where(same, dot(g, u, 1, 1), 0.0)
            out_ref[k] = dot(kept, pick, 1, 0, precision=lax.Precision.HIGHEST) * scale

    out = pl.pallas_call(
        body,
        in_specs=[VMEM, VMEM],
        out_specs=VMEM,
        out_shape=jax.ShapeDtypeStruct((groups, wide, n), F32),
        compiler_params=params(0),
        cost_estimate=cost(2 * groups * wide * wide * channels, 4 * grads.size),
        name="grad_second",
    )(in_vmem(grads), in_vmem(firsts))
    return out.reshape(groups, n, 16, n).transpose(0, 2, 1, 3).reshape(here, n, n)


def middle(half, blocked, incoming, mixed, up_blocks, down_blocks):
    groups, width, inner = up_blocks.shape
    sub = inner // groups
    rows, channels = blocked.shape
    step = min(256, rows)
    tiles = rows // step

    def body(half_ref, x_hbm, g_hbm, v_ref, up_hbm, down_hbm, *refs):
        dv_hbm, r_hbm, kept_hbm, sent_hbm = refs[:4]
        x_ref, g_ref, up_ref, down_ref, dv, r_ref, w, halves, sems = refs[4:]

        def rows_copy(src, dst, kind, t):
            at = pl.ds(t * step, step)
            return pltpu.make_async_copy(src.at[at], dst.at[at], sems.at[kind * tiles + t])

        def whole_copy(src, dst, number):
            return pltpu.make_async_copy(src, dst, sems.at[4 * tiles + number])

        fetch_up = whole_copy(up_hbm, up_ref, 0)
        fetch_down = whole_copy(down_hbm, down_ref, 1)
        rows_copy(x_hbm, x_ref, 0, 0).start()
        fetch_up.start()
        rows_copy(g_hbm, g_ref, 1, 0).start()
        fetch_down.start()
        for t in range(1, tiles):
            rows_copy(x_hbm, x_ref, 0, t).start()
            rows_copy(g_hbm, g_ref, 1, t).start()
        w[...] = jnp.zeros_like(w)
        fetch_up.wait()
        fetch_down.wait()

        def tile(t, carry):
            rows_copy(x_hbm, x_ref, 0, t).wait()
            rows_copy(g_hbm, g_ref, 1, t).wait()
            at = pl.ds(pl.multiple_of(t * step, step), step)
            x = x_ref[at, :].astype(F32)
            g = g_ref[at, :]
            v = v_ref[at, :].astype(F32)
            sx = sigmoid(x)
            gate = x * sx
            h = (x + v * gate).astype(BF)
            h_parts = [h[:, b * width : (b + 1) * width] for b in range(groups)]
            g_parts = [g[:, b * width : (b + 1) * width] for b in range(groups)]
            acts, slopes, back = [], [], []
            for b in range(groups):
                a = dot(h_parts[b], up_ref[b], 1, 0).astype(BF)
                s = sigmoid(a)
                q = a * s
                acts.append(q)
                slopes.append(s + q * (1 - s))
                back.append(dot(g_parts[b], down_ref[b], 1, 1).astype(BF))
            grads = []
            for b in range(groups):
                lanes = slice(b * sub, (b + 1) * sub)
                perm = jnp.concatenate([acts[p][:, lanes] for p in range(groups)], axis=1)
                w[1, b] += dot(g_parts[b], perm, 0, 0)
                dq = jnp.concatenate([back[p][:, lanes] for p in range(groups)], axis=1)
                da = dq * slopes[b]
                w[0, b] += dot(h_parts[b], da, 0, 0)
                grads.append(dot(da, up_ref[b], 1, 1))
            dh = (g.astype(F32) + jnp.concatenate(grads, axis=1)).astype(BF).astype(F32)
            dv[at, :] = (dh * gate).astype(BF)
            rows_copy(dv, dv_hbm, 2, t).start()
            r_ref[at, :] = (dh * (1.0 + v * (sx + gate * (1.0 - sx)))).astype(BF)
            rows_copy(r_ref, r_hbm, 3, t).start()
            return carry

        lax.fori_loop(0, tiles, tile, 0)
        halves[1] = w[1 - half_ref[0]].astype(BF)
        send = whole_copy(halves.at[1], sent_hbm, 2)
        send.start()
        halves[0] = w[half_ref[0]].astype(BF)
        keep = whole_copy(halves.at[0], kept_hbm, 3)
        keep.start()
        for t in range(tiles):
            rows_copy(dv, dv_hbm, 2, t).wait()
            rows_copy(r_ref, r_hbm, 3, t).wait()
        send.wait()
        keep.wait()

    hidden = rows * groups * inner
    return pl.pallas_call(
        body,
        in_specs=[SCALAR, ANY, ANY, VMEM, ANY, ANY],
        out_specs=[ANY] * 4,
        out_shape=[
            pltpu.HBM((rows, channels), BF),
            pltpu.HBM((rows, channels), BF),
            pltpu.HBM(up_blocks.shape, BF),
            pltpu.HBM(up_blocks.shape, BF),
        ],
        scratch_shapes=[
            pltpu.VMEM((rows, channels), BF),
            pltpu.VMEM((rows, channels), BF),
            pltpu.VMEM(up_blocks.shape, BF),
            pltpu.VMEM(down_blocks.shape, BF),
            pltpu.VMEM((rows, channels), BF),
            pltpu.VMEM((rows, channels), BF),
            pltpu.VMEM((2, groups, width, inner), F32),
            pltpu.VMEM((2, groups, width, inner), BF),
            pltpu.SemaphoreType.DMA((4 * tiles + 4,)),
        ],
        compiler_params=params(0),
        cost_estimate=cost(
            10 * hidden * width, 10 * rows * channels + 8 * groups * width * inner, hidden
        ),
        name="middle",
    )(half, in_hbm(blocked), in_hbm(incoming), in_vmem(mixed), in_hbm(up_blocks), in_hbm(down_blocks))


def finish(factor, grad_first, blocked, gate_grad, scale):
    block, channels = blocked.shape
    tiles = 4
    step = block // tiles

    def body(f_hbm, d_hbm, x_hbm, r_hbm, one_hbm, out_hbm, f, d, x, r, one, out, sems):
        ds = row_copies(d_hbm, d, sems, 0, tiles)
        xs = row_copies(x_hbm, x, sems, tiles, tiles)
        fs = row_copies(f_hbm, f, sems, 2 * tiles, tiles)
        rs = row_copies(r_hbm, r, sems, 3 * tiles, tiles)
        ones = row_copies(one, one_hbm, sems, 4 * tiles, tiles)
        outs = row_copies(out, out_hbm, sems, 5 * tiles, tiles)
        for c in xs + ds + fs + rs:
            c.start()
        for c in xs:
            c.wait()
        for t in range(tiles):
            at = slice(t * step, (t + 1) * step)
            ds[t].wait()
            one[at, :] = dot(d[at, :], x[...], 1, 1) * scale
            ones[t].start()
        for c in fs:
            c.wait()
        for t in range(tiles):
            at = slice(t * step, (t + 1) * step)
            rs[t].wait()
            total = dot(f[:, at], d[...], 0, 0) + r[at, :].astype(F32)
            out[at, :] = total.astype(BF)
            outs[t].start()
        for c in ones + outs:
            c.wait()

    return pl.pallas_call(
        body,
        in_specs=[ANY] * 4,
        out_specs=[ANY] * 2,
        out_shape=[pltpu.HBM((block, block), F32), pltpu.HBM((block, channels), BF)],
        scratch_shapes=[
            pltpu.VMEM((block, block), BF),
            pltpu.VMEM((block, channels), BF),
            pltpu.VMEM((block, channels), BF),
            pltpu.VMEM((block, channels), BF),
            pltpu.VMEM((block, block), F32),
            pltpu.VMEM((block, channels), BF),
            pltpu.SemaphoreType.DMA((6 * tiles,)),
        ],
        compiler_params=params(0),
        cost_estimate=cost(4 * block * block * channels, 6 * block * block + 8 * block * channels),
        name="finish",
    )(in_hbm(factor), in_hbm(grad_first), in_hbm(blocked), in_hbm(gate_grad))


def radices(count):
    steps, stride = [], 1
    while stride < count:
        radix = 4 if stride >= 4 and count // stride == 4 else 2
        steps.append((stride, radix))
        stride *= radix
    return steps


def swap(values, count, stride, s):
    return lax.ppermute(values, "seq", [(i, i ^ (stride * s)) for i in range(count)])


def add_and_cut(terms, digit, radix):
    rows, columns = terms[0].shape
    share = rows // radix

    number = len(terms)

    number = len(terms)
    shape = (radix, share, columns)

    def body(digit_ref, *refs):
        ins, outs = refs[:number], refs[number : number + radix]
        held, made, sems = refs[number + radix : -radix - 1], refs[-radix - 1 : -1], refs[-1]
        copies = [pltpu.make_async_copy(ins[i], held[i], sems.at[i]) for i in range(number)]
        for c in copies:
            c.start()
        for c in copies:
            c.wait()
        copies = []
        for s, ref in enumerate(made):
            total = held[0][digit_ref[0] ^ s].astype(F32)
            for term in held[1:]:
                total = total + term[digit_ref[0] ^ s].astype(F32)
            ref[...] = total.astype(ref.dtype)
            copies.append(pltpu.make_async_copy(ref, outs[s], sems.at[number + s]))
            copies[-1].start()
        for c in copies:
            c.wait()

    types = [F32] + [BF] * (radix - 1)
    return pl.pallas_call(
        body,
        in_specs=[SCALAR] + [ANY] * number,
        out_specs=[ANY] * radix,
        out_shape=[pltpu.HBM((share, columns), t) for t in types],
        scratch_shapes=[pltpu.VMEM(shape, t.dtype) for t in terms]
        + [pltpu.VMEM((share, columns), t) for t in types]
        + [pltpu.SemaphoreType.DMA((number + radix,))],
        compiler_params=params(0),
        cost_estimate=cost(rows * columns, 8 * rows * columns),
        name="add_and_cut",
    )(digit.reshape(1), *[t.reshape(shape) for t in terms])


def scatter_step(terms, count, stride, radix):
    digit = (lax.axis_index("seq").astype(jnp.int32) // stride) % radix
    kept, *send = add_and_cut(terms, digit, radix)
    return [kept] + [swap(a, count, stride, s + 1) for s, a in enumerate(send)]


def gather_step(share, count, stride, radix, after=()):
    digit = (lax.axis_index("seq") // stride) % radix
    got = [share] + [swap(share, count, stride, s) for s in range(1, radix)]
    got, after = lax.optimization_barrier((got, after))
    if radix == 2:
        low = jnp.where(digit == 0, got[0], got[1])
        high = jnp.where(digit == 0, got[1], got[0])
        return jnp.concatenate([low, high], axis=0)
    whole = jnp.zeros((radix,) + share.shape, share.dtype)
    for s in range(radix):
        whole = lax.dynamic_update_index_in_dim(whole, got[s], digit ^ s, 0)
    return whole.reshape(radix * share.shape[0], share.shape[1])


def write_weights(total, up_shape, down_shape, scale):
    groups, width, inner = up_shape

    def body(up_in, down_in, up_ref, down_ref):
        up_ref[0] = up_in[...].astype(F32) * scale
        down_ref[0] = (down_in[...].astype(F32) * scale).T

    return pl.pallas_call(
        body,
        grid=(groups,),
        in_specs=[
            pl.BlockSpec((width, inner), lambda b: (b, 0)),
            pl.BlockSpec((width, inner), lambda b: (groups + b, 0)),
        ],
        out_specs=[
            pl.BlockSpec((1, width, inner), lambda b: (b, 0, 0)),
            pl.BlockSpec((1, inner, width), lambda b: (b, 0, 0)),
        ],
        out_shape=[
            jax.ShapeDtypeStruct(up_shape, F32),
            jax.ShapeDtypeStruct(down_shape, F32),
        ],
        compiler_params=params(),
        cost_estimate=cost(groups * width * inner, 12 * groups * width * inner),
        name="write_weights",
    )(total, total)


def on_device(tokens, cotangent, factor_one, factor_two, up_blocks, down_blocks):
    count = lax.axis_size("seq")
    block, channels = factor_one.shape[1], tokens.shape[1]
    here = block // count
    scale = float(count * tokens.shape[0]) ** (-0.5)
    factor = factor_one.reshape(block, block)
    grouped = here % 16 == 0

    def exchange(values):
        cut = values.reshape(count, here, channels)
        return lax.all_to_all(cut, "seq", split_axis=0, concat_axis=0, tiled=True)

    if grouped:
        spread = spread_factor(factor_two)

    def second(cols, back):
        if grouped:
            return mix_second(spread, cols, back)
        names = "kmj,mkc->jkc" if back else "kmj,jkc->mkc"
        return jnp.einsum(names, factor_two, cols, preferred_element_type=F32).astype(BF)

    def second_grad(grads, firsts):
        if grouped:
            return grad_second(grads, firsts, scale)
        return jnp.einsum("mkc,jkc->kmj", grads, firsts, preferred_element_type=F32) * scale

    half = (lax.axis_index("seq") % 2).astype(jnp.int32).reshape(1)
    firsts = exchange(mix_first(factor, tokens))
    mixed = exchange(second(firsts, False)).reshape(block, channels)
    dv, gate_grad, kept, sent = middle(half, tokens, cotangent, mixed, up_blocks, down_blocks)
    grad_mixed = exchange(dv)
    back = second(grad_mixed, True)
    terms = [kept, swap(sent, count, 1, 1)]
    terms = [t.reshape(-1, t.shape[-1]) for t in terms]
    steps = radices(count)
    for step in steps[1:]:
        terms = scatter_step(terms, count, *step)
    terms, back = lax.optimization_barrier((terms, back))
    total = sum(t.astype(F32) for t in terms).astype(BF)
    back, total = lax.optimization_barrier((back, total))
    grad_first = exchange(back).reshape(block, channels)
    two = second_grad(grad_mixed, firsts)
    for step in reversed(steps):
        total = gather_step(total, count, *step, after=two if step == steps[1] else ())
    grad_up, grad_down = write_weights(total, up_blocks.shape, down_blocks.shape, scale)
    one, grad_tokens = finish(factor, grad_first, tokens, gate_grad, scale)
    return (grad_tokens, one.reshape(1, block, block), two, grad_up, grad_down)


def solution(mesh):
    return jax.shard_map(
        on_device,
        mesh=mesh,
        in_specs=(
            P(("grp", "seq"), None),
            P(("grp", "seq"), None),
            P("seq", None, None),
            P("seq", None, None),
            P(),
            P(),
        ),
        out_specs=(
            P(("grp", "seq"), None),
            P(("grp", "seq"), None, None),
            P(("grp", "seq"), None, None),
            P("grp", None, None),
            P("grp", None, None),
        ),
        check_vma=False,
    )
```

```python
import jax
import jax.numpy as jnp
from jax import lax
from jax.experimental import pallas as pl
from jax.experimental.pallas import tpu as pltpu
from jax.sharding import PartitionSpec as P

BF = jnp.bfloat16
F32 = jnp.float32
VMEM_BYTES = 40 * 1024 * 1024
ANY = pl.BlockSpec(memory_space=pl.ANY)
VMEM = pl.BlockSpec(memory_space=pltpu.VMEM)
SCALAR = pl.BlockSpec(memory_space=pltpu.SMEM)


def in_hbm(array):
    return pltpu.with_memory_space_constraint(array, pltpu.HBM)


def in_vmem(array):
    return pltpu.with_memory_space_constraint(array, pltpu.VMEM)


def sigmoid(z):
    return 0.5 + 0.5 * jnp.tanh(0.5 * z)


def dot(a, b, ca, cb, **kw):
    return lax.dot_general(a, b, (((ca,), (cb,)), ((), ())), preferred_element_type=F32, **kw)


def params(steps=1):
    return pltpu.CompilerParams(
        dimension_semantics=("arbitrary",) * steps, vmem_limit_bytes=VMEM_BYTES
    )


def cost(flops, moved, trans=0):
    return pl.CostEstimate(flops=int(flops), bytes_accessed=int(moved), transcendentals=int(trans))


def row_copies(src, dst, sems, first, parts):
    rows = src.shape[0] // parts
    return [
        pltpu.make_async_copy(
            src.at[pl.ds(i * rows, rows)], dst.at[pl.ds(i * rows, rows)], sems.at[first + i]
        )
        for i in range(parts)
    ]


def mix_first(factor, blocked):
    block, channels = factor.shape[0], blocked.shape[1]
    tiles = 4
    step = block // tiles

    def body(f_hbm, x_hbm, u_hbm, f_all, x_all, u_all, sems):
        xs = row_copies(x_hbm, x_all, sems, 0, tiles)
        fs = row_copies(f_hbm, f_all, sems, tiles, tiles)
        us = row_copies(u_all, u_hbm, sems, 2 * tiles, tiles)
        for c in xs + fs:
            c.start()
        for c in xs:
            c.wait()
        for t in range(tiles):
            fs[t].wait()
            at = slice(t * step, (t + 1) * step)
            u_all[at, :] = dot(f_all[at, :], x_all[...], 1, 0).astype(BF)
            us[t].start()
        for c in us:
            c.wait()

    return pl.pallas_call(
        body,
        in_specs=[ANY, ANY],
        out_specs=ANY,
        out_shape=pltpu.HBM((block, channels), BF),
        scratch_shapes=[
            pltpu.VMEM((block, block), BF),
            pltpu.VMEM((block, channels), BF),
            pltpu.VMEM((block, channels), BF),
            pltpu.SemaphoreType.DMA((3 * tiles,)),
        ],
        compiler_params=params(0),
        cost_estimate=cost(2 * block * block * channels, 2 * block * (block + 2 * channels)),
        name="mix_first",
    )(in_hbm(factor), in_hbm(blocked))


def spread_factor(factor_two):
    here, n, _ = factor_two.shape
    groups = here // 16
    wide = n * 16
    turned = factor_two.reshape(groups, 16, n, n).transpose(0, 2, 1, 3).reshape(groups, wide, n)

    def body(in_ref, out_ref):
        col = lax.broadcasted_iota(jnp.int32, (n, wide), 1)
        row = lax.broadcasted_iota(jnp.int32, (n, wide), 0)
        pick = jnp.where(col // 16 == row, 1.0, 0.0).astype(BF)
        r = lax.broadcasted_iota(jnp.int32, (wide, wide), 0)
        c = lax.broadcasted_iota(jnp.int32, (wide, wide), 1)
        same = r % 16 == c % 16
        full = dot(in_ref[0], pick, 1, 0)
        out_ref[0] = jnp.where(same, full, 0.0).astype(BF)

    return pl.pallas_call(
        body,
        grid=(groups,),
        in_specs=[pl.BlockSpec((1, wide, n), lambda g: (g, 0, 0))],
        out_specs=pl.BlockSpec((1, wide, wide), lambda g: (g, 0, 0)),
        out_shape=jax.ShapeDtypeStruct((groups, wide, wide), BF),
        compiler_params=params(),
        cost_estimate=cost(2 * groups * wide * wide * n, 2 * groups * wide * wide),
        name="spread_factor",
    )(turned)


def mix_second(spread, cols, back):
    n, here, channels = cols.shape
    wide = n * 16
    groups = here // 16

    def body(m_ref, in_ref, out_hbm, out, sems):
        copies = []
        for g in range(groups):
            at = pl.ds(g * 16, 16)
            rows = in_ref[:, at, :].reshape(wide, channels)
            got = dot(m_ref[g], rows, 0 if back else 1, 0).astype(BF)
            out[:, at, :] = got.reshape(n, 16, channels)
            copies.append(
                pltpu.make_async_copy(out.at[:, at, :], out_hbm.at[:, at, :], sems.at[g])
            )
            copies[-1].start()
        for c in copies:
            c.wait()

    return pl.pallas_call(
        body,
        in_specs=[VMEM, VMEM],
        out_specs=ANY,
        out_shape=pltpu.HBM(cols.shape, BF),
        scratch_shapes=[pltpu.VMEM(cols.shape, BF), pltpu.SemaphoreType.DMA((groups,))],
        compiler_params=params(0),
        cost_estimate=cost(
            2 * groups * wide * wide * channels, 4 * cols.size + 2 * groups * wide * wide
        ),
        name="mix_second_back" if back else "mix_second",
    )(in_vmem(spread), in_vmem(cols))


def grad_second(grads, firsts, scale):
    n, here, channels = grads.shape
    wide = n * 16
    groups = here // 16

    def body(g_ref, u_ref, out_ref):
        r = lax.broadcasted_iota(jnp.int32, (wide, wide), 0)
        c = lax.broadcasted_iota(jnp.int32, (wide, wide), 1)
        same = r % 16 == c % 16
        row = lax.broadcasted_iota(jnp.int32, (wide, n), 0)
        col = lax.broadcasted_iota(jnp.int32, (wide, n), 1)
        pick = jnp.where(row // 16 == col, 1.0, 0.0)
        for k in range(groups):
            at = pl.ds(k * 16, 16)
            g = g_ref[:, at, :].reshape(wide, channels)
            u = u_ref[:, at, :].reshape(wide, channels)
            kept = jnp.where(same, dot(g, u, 1, 1), 0.0)
            out_ref[k] = dot(kept, pick, 1, 0, precision=lax.Precision.HIGHEST) * scale

    out = pl.pallas_call(
        body,
        in_specs=[VMEM, VMEM],
        out_specs=VMEM,
        out_shape=jax.ShapeDtypeStruct((groups, wide, n), F32),
        compiler_params=params(0),
        cost_estimate=cost(2 * groups * wide * wide * channels, 4 * grads.size),
        name="grad_second",
    )(in_vmem(grads), in_vmem(firsts))
    return out.reshape(groups, n, 16, n).transpose(0, 2, 1, 3).reshape(here, n, n)


def middle(half, blocked, incoming, mixed, up_blocks, down_blocks):
    groups, width, inner = up_blocks.shape
    sub = inner // groups
    rows, channels = blocked.shape
    step = min(512, rows)
    tiles = rows // step

    def body(half_ref, x_hbm, g_hbm, v_ref, up_hbm, down_hbm, *refs):
        dv_hbm, r_hbm, kept_hbm, sent_hbm = refs[:4]
        x_ref, g_ref, up_ref, down_ref, dv, r_ref, w, halves, sems = refs[4:]

        def rows_copy(src, dst, kind, t):
            at = pl.ds(t * step, step)
            return pltpu.make_async_copy(src.at[at], dst.at[at], sems.at[kind * tiles + t])

        def whole_copy(src, dst, number):
            return pltpu.make_async_copy(src, dst, sems.at[4 * tiles + number])

        fetch_up = whole_copy(up_hbm, up_ref, 0)
        fetch_down = whole_copy(down_hbm, down_ref, 1)
        rows_copy(x_hbm, x_ref, 0, 0).start()
        fetch_up.start()
        rows_copy(g_hbm, g_ref, 1, 0).start()
        fetch_down.start()
        for t in range(1, tiles):
            rows_copy(x_hbm, x_ref, 0, t).start()
            rows_copy(g_hbm, g_ref, 1, t).start()
        w[...] = jnp.zeros_like(w)

        def tile(t, carry):
            rows_copy(x_hbm, x_ref, 0, t).wait()
            rows_copy(g_hbm, g_ref, 1, t).wait()
            at = pl.ds(pl.multiple_of(t * step, step), step)
            x = x_ref[at, :].astype(F32)
            g = g_ref[at, :]
            v = v_ref[at, :].astype(F32)
            sx = sigmoid(x)
            gate = x * sx
            h = (x + v * gate).astype(BF)
            h_parts = [h[:, b * width : (b + 1) * width] for b in range(groups)]
            g_parts = [g[:, b * width : (b + 1) * width] for b in range(groups)]

            @pl.when(t == 0)
            def _():
                fetch_up.wait()
                fetch_down.wait()

            acts, slopes, back = [], [], []
            for b in range(groups):
                a = dot(h_parts[b], up_ref[b], 1, 0).astype(BF)
                s = sigmoid(a)
                q = a * s
                acts.append(q)
                slopes.append(s + q * (1 - s))
                back.append(dot(g_parts[b], down_ref[b], 1, 1).astype(BF))
            grads = []
            for b in range(groups):
                lanes = slice(b * sub, (b + 1) * sub)
                perm = jnp.concatenate([acts[p][:, lanes] for p in range(groups)], axis=1)
                w[1, b] += dot(g_parts[b], perm, 0, 0)
                dq = jnp.concatenate([back[p][:, lanes] for p in range(groups)], axis=1)
                da = dq * slopes[b]
                w[0, b] += dot(h_parts[b], da, 0, 0)
                grads.append(dot(da, up_ref[b], 1, 1))
            dh = (g.astype(F32) + jnp.concatenate(grads, axis=1)).astype(BF).astype(F32)
            dv[at, :] = (dh * gate).astype(BF)
            rows_copy(dv, dv_hbm, 2, t).start()
            r_ref[at, :] = (dh * (1.0 + v * (sx + gate * (1.0 - sx)))).astype(BF)
            rows_copy(r_ref, r_hbm, 3, t).start()
            return carry

        lax.fori_loop(0, tiles, tile, 0)
        halves[1] = w[1 - half_ref[0]].astype(BF)
        send = whole_copy(halves.at[1], sent_hbm, 2)
        send.start()
        halves[0] = w[half_ref[0]].astype(BF)
        keep = whole_copy(halves.at[0], kept_hbm, 3)
        keep.start()
        for t in range(tiles):
            rows_copy(dv, dv_hbm, 2, t).wait()
            rows_copy(r_ref, r_hbm, 3, t).wait()
        send.wait()
        keep.wait()

    hidden = rows * groups * inner
    return pl.pallas_call(
        body,
        in_specs=[SCALAR, ANY, ANY, VMEM, ANY, ANY],
        out_specs=[ANY] * 4,
        out_shape=[
            pltpu.HBM((rows, channels), BF),
            pltpu.HBM((rows, channels), BF),
            pltpu.HBM(up_blocks.shape, BF),
            pltpu.HBM(up_blocks.shape, BF),
        ],
        scratch_shapes=[
            pltpu.VMEM((rows, channels), BF),
            pltpu.VMEM((rows, channels), BF),
            pltpu.VMEM(up_blocks.shape, BF),
            pltpu.VMEM(down_blocks.shape, BF),
            pltpu.VMEM((rows, channels), BF),
            pltpu.VMEM((rows, channels), BF),
            pltpu.VMEM((2, groups, width, inner), F32),
            pltpu.VMEM((2, groups, width, inner), BF),
            pltpu.SemaphoreType.DMA((4 * tiles + 4,)),
        ],
        compiler_params=params(0),
        cost_estimate=cost(
            10 * hidden * width, 10 * rows * channels + 8 * groups * width * inner, hidden
        ),
        name="middle",
    )(half, in_hbm(blocked), in_hbm(incoming), in_vmem(mixed), in_hbm(up_blocks), in_hbm(down_blocks))


def bring(arrays, name):
    number = len(arrays)

    def body(*refs):
        sems = refs[-1]
        copies = [
            pltpu.make_async_copy(refs[i], refs[number + i], sems.at[i]) for i in range(number)
        ]
        for c in copies:
            c.start()
        for c in copies:
            c.wait()

    return pl.pallas_call(
        body,
        in_specs=[ANY] * number,
        out_specs=[pl.BlockSpec(memory_space=pltpu.VMEM)] * number,
        out_shape=[pltpu.VMEM(a.shape, a.dtype) for a in arrays],
        scratch_shapes=[pltpu.SemaphoreType.DMA((number,))],
        compiler_params=pltpu.CompilerParams(vmem_limit_bytes=16 * 1024 * 1024),
        cost_estimate=cost(0, sum(2 * a.size * a.dtype.itemsize for a in arrays)),
        name=name,
    )(*[in_hbm(a) for a in arrays])


def finish(factor, grad_first, blocked, gate_grad, scale):
    block, channels = blocked.shape
    tiles = 4
    step = block // tiles

    def body(f, x, d_hbm, r_hbm, one_hbm, out_hbm, d, r, one, out, sems):
        ds = row_copies(d_hbm, d, sems, 0, tiles)
        rs = row_copies(r_hbm, r, sems, tiles, tiles)
        ones = row_copies(one, one_hbm, sems, 2 * tiles, tiles)
        outs = row_copies(out, out_hbm, sems, 3 * tiles, tiles)
        for c in ds + rs:
            c.start()
        for t in range(tiles):
            at = slice(t * step, (t + 1) * step)
            ds[t].wait()
            one[at, :] = dot(d[at, :], x[...], 1, 1) * scale
            ones[t].start()
        for t in range(tiles):
            at = slice(t * step, (t + 1) * step)
            rs[t].wait()
            total = dot(f[:, at], d[...], 0, 0) + r[at, :].astype(F32)
            out[at, :] = total.astype(BF)
            outs[t].start()
        for c in ones + outs:
            c.wait()

    return pl.pallas_call(
        body,
        in_specs=[VMEM, VMEM, ANY, ANY],
        out_specs=[ANY] * 2,
        out_shape=[pltpu.HBM((block, block), F32), pltpu.HBM((block, channels), BF)],
        scratch_shapes=[
            pltpu.VMEM((block, channels), BF),
            pltpu.VMEM((block, channels), BF),
            pltpu.VMEM((block, block), F32),
            pltpu.VMEM((block, channels), BF),
            pltpu.SemaphoreType.DMA((4 * tiles,)),
        ],
        compiler_params=params(0),
        cost_estimate=cost(4 * block * block * channels, 6 * block * block + 8 * block * channels),
        name="finish",
    )(in_vmem(factor), in_vmem(blocked), in_hbm(grad_first), in_hbm(gate_grad))


def radices(count):
    steps, stride = [], 1
    while stride < count:
        radix = 4 if stride >= 4 and count // stride == 4 else 2
        steps.append((stride, radix))
        stride *= radix
    return steps


def swap(values, count, stride, s):
    return lax.ppermute(values, "seq", [(i, i ^ (stride * s)) for i in range(count)])


def add_and_cut(terms, digit, radix):
    rows, columns = terms[0].shape
    share = rows // radix

    number = len(terms)

    number = len(terms)
    shape = (radix, share, columns)

    def body(digit_ref, *refs):
        ins, outs = refs[:number], refs[number : number + radix]
        held, made, sems = refs[number + radix : -radix - 1], refs[-radix - 1 : -1], refs[-1]
        copies = [pltpu.make_async_copy(ins[i], held[i], sems.at[i]) for i in range(number)]
        for c in copies:
            c.start()
        for c in copies:
            c.wait()
        copies = []
        for s, ref in enumerate(made):
            total = held[0][digit_ref[0] ^ s].astype(F32)
            for term in held[1:]:
                total = total + term[digit_ref[0] ^ s].astype(F32)
            ref[...] = total.astype(ref.dtype)
            copies.append(pltpu.make_async_copy(ref, outs[s], sems.at[number + s]))
            copies[-1].start()
        for c in copies:
            c.wait()

    types = [F32] + [BF] * (radix - 1)
    return pl.pallas_call(
        body,
        in_specs=[SCALAR] + [ANY] * number,
        out_specs=[ANY] * radix,
        out_shape=[pltpu.HBM((share, columns), t) for t in types],
        scratch_shapes=[pltpu.VMEM(shape, t.dtype) for t in terms]
        + [pltpu.VMEM((share, columns), t) for t in types]
        + [pltpu.SemaphoreType.DMA((number + radix,))],
        compiler_params=params(0),
        cost_estimate=cost(rows * columns, 8 * rows * columns),
        name="add_and_cut",
    )(digit.reshape(1), *[t.reshape(shape) for t in terms])


def scatter_step(terms, count, stride, radix):
    digit = (lax.axis_index("seq").astype(jnp.int32) // stride) % radix
    kept, *send = add_and_cut(terms, digit, radix)
    return [kept] + [swap(a, count, stride, s + 1) for s, a in enumerate(send)]


def gather_step(share, count, stride, radix, after=()):
    digit = (lax.axis_index("seq") // stride) % radix
    got = [share] + [swap(share, count, stride, s) for s in range(1, radix)]
    got, after = lax.optimization_barrier((got, after))
    if radix == 2:
        low = jnp.where(digit == 0, got[0], got[1])
        high = jnp.where(digit == 0, got[1], got[0])
        return jnp.concatenate([low, high], axis=0)
    whole = jnp.zeros((radix,) + share.shape, share.dtype)
    for s in range(radix):
        whole = lax.dynamic_update_index_in_dim(whole, got[s], digit ^ s, 0)
    return whole.reshape(radix * share.shape[0], share.shape[1])


def write_weights(total, up_shape, down_shape, scale):
    groups, width, inner = up_shape

    def body(up_in, down_in, up_ref, down_ref):
        up_ref[0] = up_in[...].astype(F32) * scale
        down_ref[0] = (down_in[...].astype(F32) * scale).T

    return pl.pallas_call(
        body,
        grid=(groups,),
        in_specs=[
            pl.BlockSpec((width, inner), lambda b: (b, 0)),
            pl.BlockSpec((width, inner), lambda b: (groups + b, 0)),
        ],
        out_specs=[
            pl.BlockSpec((1, width, inner), lambda b: (b, 0, 0)),
            pl.BlockSpec((1, inner, width), lambda b: (b, 0, 0)),
        ],
        out_shape=[
            jax.ShapeDtypeStruct(up_shape, F32),
            jax.ShapeDtypeStruct(down_shape, F32),
        ],
        compiler_params=params(),
        cost_estimate=cost(groups * width * inner, 12 * groups * width * inner),
        name="write_weights",
    )(total, total)


def on_device(tokens, cotangent, factor_one, factor_two, up_blocks, down_blocks):
    count = lax.axis_size("seq")
    block, channels = factor_one.shape[1], tokens.shape[1]
    here = block // count
    scale = float(count * tokens.shape[0]) ** (-0.5)
    factor = factor_one.reshape(block, block)
    grouped = here % 16 == 0

    def exchange(values):
        cut = values.reshape(count, here, channels)
        return lax.all_to_all(cut, "seq", split_axis=0, concat_axis=0, tiled=True)

    if grouped:
        spread = spread_factor(factor_two)

    def second(cols, back):
        if grouped:
            return mix_second(spread, cols, back)
        names = "kmj,mkc->jkc" if back else "kmj,jkc->mkc"
        return jnp.einsum(names, factor_two, cols, preferred_element_type=F32).astype(BF)

    def second_grad(grads, firsts):
        if grouped:
            return grad_second(grads, firsts, scale)
        return jnp.einsum("mkc,jkc->kmj", grads, firsts, preferred_element_type=F32) * scale

    half = (lax.axis_index("seq") % 2).astype(jnp.int32).reshape(1)
    firsts = exchange(mix_first(factor, tokens))
    mixed = exchange(second(firsts, False)).reshape(block, channels)
    dv, gate_grad, kept, sent = middle(half, tokens, cotangent, mixed, up_blocks, down_blocks)
    grad_mixed = exchange(dv)
    back = second(grad_mixed, True)
    terms = [kept, swap(sent, count, 1, 1)]
    terms = [t.reshape(-1, t.shape[-1]) for t in terms]
    steps = radices(count)
    for step in steps[1:]:
        terms = scatter_step(terms, count, *step)
    terms, back = lax.optimization_barrier((terms, back))
    total = sum(t.astype(F32) for t in terms).astype(BF)
    back, total = lax.optimization_barrier((back, total))
    grad_first = exchange(back).reshape(block, channels)
    two = second_grad(grad_mixed, firsts)
    for step in reversed(steps):
        total = gather_step(total, count, *step, after=two if step == steps[1] else ())
    grad_up, grad_down = write_weights(total, up_blocks.shape, down_blocks.shape, scale)
    late = (factor, tokens)
    late, grad_up, grad_down = lax.optimization_barrier((late, grad_up, grad_down))
    factor, tokens = bring(late, "bring")
    one, grad_tokens = finish(factor, grad_first, tokens, gate_grad, scale)
    return (grad_tokens, one.reshape(1, block, block), two, grad_up, grad_down)


def solution(mesh):
    return jax.shard_map(
        on_device,
        mesh=mesh,
        in_specs=(
            P(("grp", "seq"), None),
            P(("grp", "seq"), None),
            P("seq", None, None),
            P("seq", None, None),
            P(),
            P(),
        ),
        out_specs=(
            P(("grp", "seq"), None),
            P(("grp", "seq"), None, None),
            P(("grp", "seq"), None, None),
            P("grp", None, None),
            P("grp", None, None),
        ),
        check_vma=False,
    )
```

```python
import jax
import jax.numpy as jnp
from jax import lax
from jax.experimental import pallas as pl
from jax.experimental.pallas import tpu as pltpu
from jax.sharding import PartitionSpec as P

BF = jnp.bfloat16
F32 = jnp.float32
VMEM_BYTES = 40 * 1024 * 1024
ANY = pl.BlockSpec(memory_space=pl.ANY)
VMEM = pl.BlockSpec(memory_space=pltpu.VMEM)
SCALAR = pl.BlockSpec(memory_space=pltpu.SMEM)


def in_hbm(array):
    return pltpu.with_memory_space_constraint(array, pltpu.HBM)


def in_vmem(array):
    return pltpu.with_memory_space_constraint(array, pltpu.VMEM)


def sigmoid(z):
    return 0.5 + 0.5 * jnp.tanh(0.5 * z)


def dot(a, b, ca, cb, **kw):
    return lax.dot_general(a, b, (((ca,), (cb,)), ((), ())), preferred_element_type=F32, **kw)


def params(steps=1):
    return pltpu.CompilerParams(
        dimension_semantics=("arbitrary",) * steps, vmem_limit_bytes=VMEM_BYTES
    )


def cost(flops, moved, trans=0):
    return pl.CostEstimate(flops=int(flops), bytes_accessed=int(moved), transcendentals=int(trans))


def row_copies(src, dst, sems, first, parts):
    rows = src.shape[0] // parts
    return [
        pltpu.make_async_copy(
            src.at[pl.ds(i * rows, rows)], dst.at[pl.ds(i * rows, rows)], sems.at[first + i]
        )
        for i in range(parts)
    ]


def mix_first(factor, blocked):
    block, channels = factor.shape[0], blocked.shape[1]
    tiles = 4
    step = block // tiles

    def body(f_hbm, x_hbm, u_hbm, f_all, x_all, u_all, sems):
        xs = row_copies(x_hbm, x_all, sems, 0, tiles)
        fs = row_copies(f_hbm, f_all, sems, tiles, tiles)
        us = row_copies(u_all, u_hbm, sems, 2 * tiles, tiles)
        for c in xs + fs:
            c.start()
        for c in xs:
            c.wait()
        for t in range(tiles):
            fs[t].wait()
            at = slice(t * step, (t + 1) * step)
            u_all[at, :] = dot(f_all[at, :], x_all[...], 1, 0).astype(BF)
            us[t].start()
        for c in us:
            c.wait()

    return pl.pallas_call(
        body,
        in_specs=[ANY, ANY],
        out_specs=ANY,
        out_shape=pltpu.HBM((block, channels), BF),
        scratch_shapes=[
            pltpu.VMEM((block, block), BF),
            pltpu.VMEM((block, channels), BF),
            pltpu.VMEM((block, channels), BF),
            pltpu.SemaphoreType.DMA((3 * tiles,)),
        ],
        compiler_params=params(0),
        cost_estimate=cost(2 * block * block * channels, 2 * block * (block + 2 * channels)),
        name="mix_first",
    )(in_hbm(factor), in_hbm(blocked))


def spread_factor(factor_two):
    here, n, _ = factor_two.shape
    groups = here // 16
    wide = n * 16
    turned = factor_two.reshape(groups, 16, n, n).transpose(0, 2, 1, 3).reshape(groups, wide, n)

    def body(in_ref, out_ref):
        col = lax.broadcasted_iota(jnp.int32, (n, wide), 1)
        row = lax.broadcasted_iota(jnp.int32, (n, wide), 0)
        pick = jnp.where(col // 16 == row, 1.0, 0.0).astype(BF)
        r = lax.broadcasted_iota(jnp.int32, (wide, wide), 0)
        c = lax.broadcasted_iota(jnp.int32, (wide, wide), 1)
        same = r % 16 == c % 16
        full = dot(in_ref[0], pick, 1, 0)
        out_ref[0] = jnp.where(same, full, 0.0).astype(BF)

    return pl.pallas_call(
        body,
        grid=(groups,),
        in_specs=[pl.BlockSpec((1, wide, n), lambda g: (g, 0, 0))],
        out_specs=pl.BlockSpec((1, wide, wide), lambda g: (g, 0, 0)),
        out_shape=jax.ShapeDtypeStruct((groups, wide, wide), BF),
        compiler_params=params(),
        cost_estimate=cost(2 * groups * wide * wide * n, 2 * groups * wide * wide),
        name="spread_factor",
    )(turned)


def mix_second(spread, cols, back):
    n, here, channels = cols.shape
    wide = n * 16
    groups = here // 16

    def body(m_ref, in_ref, out_hbm, out, sems):
        copies = []
        for g in range(groups):
            at = pl.ds(g * 16, 16)
            rows = in_ref[:, at, :].reshape(wide, channels)
            got = dot(m_ref[g], rows, 0 if back else 1, 0).astype(BF)
            out[:, at, :] = got.reshape(n, 16, channels)
            copies.append(
                pltpu.make_async_copy(out.at[:, at, :], out_hbm.at[:, at, :], sems.at[g])
            )
            copies[-1].start()
        for c in copies:
            c.wait()

    return pl.pallas_call(
        body,
        in_specs=[VMEM, VMEM],
        out_specs=ANY,
        out_shape=pltpu.HBM(cols.shape, BF),
        scratch_shapes=[pltpu.VMEM(cols.shape, BF), pltpu.SemaphoreType.DMA((groups,))],
        compiler_params=params(0),
        cost_estimate=cost(
            2 * groups * wide * wide * channels, 4 * cols.size + 2 * groups * wide * wide
        ),
        name="mix_second_back" if back else "mix_second",
    )(in_vmem(spread), in_vmem(cols))


def grad_second(grads, firsts, scale):
    n, here, channels = grads.shape
    wide = n * 16
    groups = here // 16

    def body(g_ref, u_ref, out_ref):
        r = lax.broadcasted_iota(jnp.int32, (wide, wide), 0)
        c = lax.broadcasted_iota(jnp.int32, (wide, wide), 1)
        same = r % 16 == c % 16
        row = lax.broadcasted_iota(jnp.int32, (wide, n), 0)
        col = lax.broadcasted_iota(jnp.int32, (wide, n), 1)
        pick = jnp.where(row // 16 == col, 1.0, 0.0)
        for k in range(groups):
            at = pl.ds(k * 16, 16)
            g = g_ref[:, at, :].reshape(wide, channels)
            u = u_ref[:, at, :].reshape(wide, channels)
            kept = jnp.where(same, dot(g, u, 1, 1), 0.0)
            out_ref[k] = dot(kept, pick, 1, 0, precision=lax.Precision.HIGHEST) * scale

    out = pl.pallas_call(
        body,
        in_specs=[VMEM, VMEM],
        out_specs=VMEM,
        out_shape=jax.ShapeDtypeStruct((groups, wide, n), F32),
        compiler_params=params(0),
        cost_estimate=cost(2 * groups * wide * wide * channels, 4 * grads.size),
        name="grad_second",
    )(in_vmem(grads), in_vmem(firsts))
    return out.reshape(groups, n, 16, n).transpose(0, 2, 1, 3).reshape(here, n, n)


def turn(factor, incoming, up_blocks, down_blocks):
    block = factor.shape[0]
    rows, channels = incoming.shape
    groups, width, inner = up_blocks.shape

    def body(f_ref, g_ref, up_ref, down_ref, f_out, g_out, up_out, down_out):
        f_out[...] = f_ref[...].T
        g_out[...] = g_ref[...].T
        up_out[0] = up_ref[0].T
        down_out[0] = down_ref[0].T

    step, part = rows // groups, block // groups
    return pl.pallas_call(
        body,
        grid=(groups,),
        in_specs=[
            pl.BlockSpec((block, part), lambda i: (0, i)),
            pl.BlockSpec((step, channels), lambda i: (i, 0)),
            pl.BlockSpec((1, width, inner), lambda i: (i, 0, 0)),
            pl.BlockSpec((1, inner, width), lambda i: (i, 0, 0)),
        ],
        out_specs=[
            pl.BlockSpec((part, block), lambda i: (i, 0)),
            pl.BlockSpec((channels, step), lambda i: (0, i)),
            pl.BlockSpec((1, inner, width), lambda i: (i, 0, 0)),
            pl.BlockSpec((1, width, inner), lambda i: (i, 0, 0)),
        ],
        out_shape=[
            pltpu.HBM((block, block), BF),
            pltpu.HBM((channels, rows), BF),
            pltpu.HBM((groups, inner, width), BF),
            pltpu.HBM((groups, width, inner), BF),
        ],
        compiler_params=params(),
        cost_estimate=cost(0, 4 * (block * block + rows * channels)),
        name="turn",
    )(in_hbm(factor), in_hbm(incoming), in_hbm(up_blocks), in_hbm(down_blocks))


def middle(half, blocked, incoming, mixed, up_blocks, turned):
    groups, width, inner = up_blocks.shape
    sub = inner // groups
    rows, channels = blocked.shape
    step = min(256, rows)
    tiles = rows // step
    incoming_t, up_t, down_t = turned

    def body(half_ref, x_hbm, g_hbm, gt_hbm, v_ref, up_hbm, upt_hbm, downt_hbm, *refs):
        dv_hbm, r_hbm, kept_hbm, sent_hbm = refs[:4]
        x_ref, g_ref, gt_ref, up_ref, upt_ref, downt_ref, dv, r_ref, w, halves, sems = refs[4:]

        def rows_copy(src, dst, kind, t):
            at = pl.ds(t * step, step)
            return pltpu.make_async_copy(src.at[at], dst.at[at], sems.at[kind * tiles + t])

        def whole_copy(src, dst, number):
            return pltpu.make_async_copy(src, dst, sems.at[4 * tiles + number])

        fetch_up = whole_copy(up_hbm, up_ref, 0)
        fetch_downt = whole_copy(downt_hbm, downt_ref, 1)
        fetch_upt = whole_copy(upt_hbm, upt_ref, 2)
        fetch_gt = whole_copy(gt_hbm, gt_ref, 3)
        rows_copy(x_hbm, x_ref, 0, 0).start()
        fetch_up.start()
        rows_copy(g_hbm, g_ref, 1, 0).start()
        fetch_downt.start()
        fetch_gt.start()
        fetch_upt.start()
        for t in range(1, tiles):
            rows_copy(x_hbm, x_ref, 0, t).start()
            rows_copy(g_hbm, g_ref, 1, t).start()
        w[...] = jnp.zeros_like(w)
        for t in range(tiles):
            at = slice(t * step, (t + 1) * step)
            rows_copy(x_hbm, x_ref, 0, t).wait()
            x = x_ref[at, :].astype(F32)
            v = v_ref[at, :].astype(F32)
            sx = sigmoid(x)
            gate = x * sx
            h = (x + v * gate).astype(BF)
            ht = h.T
            rows_copy(g_hbm, g_ref, 1, t).wait()
            if t == 0:
                fetch_up.wait()
                fetch_downt.wait()
            acts, slopes, back = [], [], []
            for b in range(groups):
                part = slice(b * width, (b + 1) * width)
                a = dot(h[:, part], up_ref[b], 1, 0).astype(BF)
                s = sigmoid(a)
                q = a * s
                acts.append(q)
                slopes.append(s + q * (1 - s))
                back.append(dot(g_ref[at, part], downt_ref[b], 1, 0).astype(BF))
            if t == 0:
                fetch_gt.wait()
                fetch_upt.wait()
            grads = []
            for b in range(groups):
                part = slice(b * width, (b + 1) * width)
                lanes = slice(b * sub, (b + 1) * sub)
                perm = jnp.concatenate([acts[p][:, lanes] for p in range(groups)], axis=1)
                w[1, b] += dot(gt_ref[part, at], perm, 1, 0)
                dq = jnp.concatenate([back[p][:, lanes] for p in range(groups)], axis=1)
                da = dq * slopes[b]
                w[0, b] += dot(ht[part, :], da, 1, 0)
                grads.append(dot(da, upt_ref[b], 1, 0))
            g = g_ref[at, :].astype(F32)
            dh = (g + jnp.concatenate(grads, axis=1)).astype(BF).astype(F32)
            dv[at, :] = (dh * gate).astype(BF)
            rows_copy(dv, dv_hbm, 2, t).start()
            r_ref[at, :] = (dh * (1.0 + v * (sx + gate * (1.0 - sx)))).astype(BF)
            rows_copy(r_ref, r_hbm, 3, t).start()
        halves[1] = w[1 - half_ref[0]].astype(BF)
        send = whole_copy(halves.at[1], sent_hbm, 4)
        send.start()
        halves[0] = w[half_ref[0]].astype(BF)
        keep = whole_copy(halves.at[0], kept_hbm, 5)
        keep.start()
        for t in range(tiles):
            rows_copy(dv, dv_hbm, 2, t).wait()
            rows_copy(r_ref, r_hbm, 3, t).wait()
        send.wait()
        keep.wait()

    hidden = rows * groups * inner
    return pl.pallas_call(
        body,
        in_specs=[SCALAR, ANY, ANY, ANY, VMEM, ANY, ANY, ANY],
        out_specs=[ANY] * 4,
        out_shape=[
            pltpu.HBM((rows, channels), BF),
            pltpu.HBM((rows, channels), BF),
            pltpu.HBM(up_blocks.shape, BF),
            pltpu.HBM(up_blocks.shape, BF),
        ],
        scratch_shapes=[
            pltpu.VMEM((rows, channels), BF),
            pltpu.VMEM((rows, channels), BF),
            pltpu.VMEM(incoming_t.shape, BF),
            pltpu.VMEM(up_blocks.shape, BF),
            pltpu.VMEM(up_t.shape, BF),
            pltpu.VMEM(down_t.shape, BF),
            pltpu.VMEM((rows, channels), BF),
            pltpu.VMEM((rows, channels), BF),
            pltpu.VMEM((2, groups, width, inner), F32),
            pltpu.VMEM((2, groups, width, inner), BF),
            pltpu.SemaphoreType.DMA((4 * tiles + 6,)),
        ],
        compiler_params=params(0),
        cost_estimate=cost(
            10 * hidden * width, 10 * rows * channels + 8 * groups * width * inner, hidden
        ),
        name="middle",
    )(
        half,
        in_hbm(blocked),
        in_hbm(incoming),
        in_hbm(incoming_t),
        in_vmem(mixed),
        in_hbm(up_blocks),
        in_hbm(up_t),
        in_hbm(down_t),
    )


def finish(factor_t, grad_first, blocked, gate_grad, scale):
    block, channels = blocked.shape
    tiles = 4
    step = block // tiles

    def body(f_hbm, d_hbm, x_hbm, r_hbm, one_hbm, out_hbm, f, d, x, r, one, out, sems):
        ds = row_copies(d_hbm, d, sems, 0, tiles)
        xs = row_copies(x_hbm, x, sems, tiles, tiles)
        fs = row_copies(f_hbm, f, sems, 2 * tiles, tiles)
        rs = row_copies(r_hbm, r, sems, 3 * tiles, tiles)
        ones = row_copies(one, one_hbm, sems, 4 * tiles, tiles)
        outs = row_copies(out, out_hbm, sems, 5 * tiles, tiles)
        for c in xs + ds + fs + rs:
            c.start()
        for c in xs:
            c.wait()
        for t in range(tiles):
            at = slice(t * step, (t + 1) * step)
            ds[t].wait()
            one[at, :] = dot(d[at, :], x[...], 1, 1) * scale
            ones[t].start()
        for t in range(tiles):
            at = slice(t * step, (t + 1) * step)
            fs[t].wait()
            rs[t].wait()
            total = dot(f[at, :], d[...], 1, 0) + r[at, :].astype(F32)
            out[at, :] = total.astype(BF)
            outs[t].start()
        for c in ones + outs:
            c.wait()

    return pl.pallas_call(
        body,
        in_specs=[ANY] * 4,
        out_specs=[ANY] * 2,
        out_shape=[pltpu.HBM((block, block), F32), pltpu.HBM((block, channels), BF)],
        scratch_shapes=[
            pltpu.VMEM((block, block), BF),
            pltpu.VMEM((block, channels), BF),
            pltpu.VMEM((block, channels), BF),
            pltpu.VMEM((block, channels), BF),
            pltpu.VMEM((block, block), F32),
            pltpu.VMEM((block, channels), BF),
            pltpu.SemaphoreType.DMA((6 * tiles,)),
        ],
        compiler_params=params(0),
        cost_estimate=cost(4 * block * block * channels, 6 * block * block + 8 * block * channels),
        name="finish",
    )(in_hbm(factor_t), in_hbm(grad_first), in_hbm(blocked), in_hbm(gate_grad))


def radices(count):
    steps, stride = [], 1
    while stride < count:
        radix = 4 if stride >= 4 and count // stride == 4 else 2
        steps.append((stride, radix))
        stride *= radix
    return steps


def swap(values, count, stride, s):
    return lax.ppermute(values, "seq", [(i, i ^ (stride * s)) for i in range(count)])


def add_and_cut(terms, digit, radix):
    rows, columns = terms[0].shape
    share = rows // radix

    number = len(terms)

    number = len(terms)
    shape = (radix, share, columns)

    def body(digit_ref, *refs):
        ins, outs = refs[:number], refs[number : number + radix]
        held, made, sems = refs[number + radix : -radix - 1], refs[-radix - 1 : -1], refs[-1]
        copies = [pltpu.make_async_copy(ins[i], held[i], sems.at[i]) for i in range(number)]
        for c in copies:
            c.start()
        for c in copies:
            c.wait()
        copies = []
        for s, ref in enumerate(made):
            total = held[0][digit_ref[0] ^ s].astype(F32)
            for term in held[1:]:
                total = total + term[digit_ref[0] ^ s].astype(F32)
            ref[...] = total.astype(ref.dtype)
            copies.append(pltpu.make_async_copy(ref, outs[s], sems.at[number + s]))
            copies[-1].start()
        for c in copies:
            c.wait()

    types = [F32] + [BF] * (radix - 1)
    return pl.pallas_call(
        body,
        in_specs=[SCALAR] + [ANY] * number,
        out_specs=[ANY] * radix,
        out_shape=[pltpu.HBM((share, columns), t) for t in types],
        scratch_shapes=[pltpu.VMEM(shape, t.dtype) for t in terms]
        + [pltpu.VMEM((share, columns), t) for t in types]
        + [pltpu.SemaphoreType.DMA((number + radix,))],
        compiler_params=params(0),
        cost_estimate=cost(rows * columns, 8 * rows * columns),
        name="add_and_cut",
    )(digit.reshape(1), *[t.reshape(shape) for t in terms])


def scatter_step(terms, count, stride, radix):
    digit = (lax.axis_index("seq").astype(jnp.int32) // stride) % radix
    kept, *send = add_and_cut(terms, digit, radix)
    return [kept] + [swap(a, count, stride, s + 1) for s, a in enumerate(send)]


def gather_step(share, count, stride, radix, after=()):
    digit = (lax.axis_index("seq") // stride) % radix
    got = [share] + [swap(share, count, stride, s) for s in range(1, radix)]
    got, after = lax.optimization_barrier((got, after))
    if radix == 2:
        low = jnp.where(digit == 0, got[0], got[1])
        high = jnp.where(digit == 0, got[1], got[0])
        return jnp.concatenate([low, high], axis=0)
    whole = jnp.zeros((radix,) + share.shape, share.dtype)
    for s in range(radix):
        whole = lax.dynamic_update_index_in_dim(whole, got[s], digit ^ s, 0)
    return whole.reshape(radix * share.shape[0], share.shape[1])


def write_weights(total, up_shape, down_shape, scale):
    groups, width, inner = up_shape

    def body(up_in, down_in, up_ref, down_ref):
        up_ref[0] = up_in[...].astype(F32) * scale
        down_ref[0] = (down_in[...].astype(F32) * scale).T

    return pl.pallas_call(
        body,
        grid=(groups,),
        in_specs=[
            pl.BlockSpec((width, inner), lambda b: (b, 0)),
            pl.BlockSpec((width, inner), lambda b: (groups + b, 0)),
        ],
        out_specs=[
            pl.BlockSpec((1, width, inner), lambda b: (b, 0, 0)),
            pl.BlockSpec((1, inner, width), lambda b: (b, 0, 0)),
        ],
        out_shape=[
            jax.ShapeDtypeStruct(up_shape, F32),
            jax.ShapeDtypeStruct(down_shape, F32),
        ],
        compiler_params=params(),
        cost_estimate=cost(groups * width * inner, 12 * groups * width * inner),
        name="write_weights",
    )(total, total)


def on_device(tokens, cotangent, factor_one, factor_two, up_blocks, down_blocks):
    count = lax.axis_size("seq")
    block, channels = factor_one.shape[1], tokens.shape[1]
    here = block // count
    scale = float(count * tokens.shape[0]) ** (-0.5)
    factor = factor_one.reshape(block, block)
    grouped = here % 16 == 0

    def exchange(values):
        cut = values.reshape(count, here, channels)
        return lax.all_to_all(cut, "seq", split_axis=0, concat_axis=0, tiled=True)

    if grouped:
        spread = spread_factor(factor_two)

    def second(cols, back):
        if grouped:
            return mix_second(spread, cols, back)
        names = "kmj,mkc->jkc" if back else "kmj,jkc->mkc"
        return jnp.einsum(names, factor_two, cols, preferred_element_type=F32).astype(BF)

    def second_grad(grads, firsts):
        if grouped:
            return grad_second(grads, firsts, scale)
        return jnp.einsum("mkc,jkc->kmj", grads, firsts, preferred_element_type=F32) * scale

    half = (lax.axis_index("seq") % 2).astype(jnp.int32).reshape(1)
    firsts = exchange(mix_first(factor, tokens))
    mixed = exchange(second(firsts, False)).reshape(block, channels)
    late = (factor, cotangent, up_blocks, down_blocks)
    firsts, late = lax.optimization_barrier((firsts, late))
    factor_t, *turned = turn(*late)
    dv, gate_grad, kept, sent = middle(half, tokens, cotangent, mixed, up_blocks, turned)
    grad_mixed = exchange(dv)
    back = second(grad_mixed, True)
    terms = [kept, swap(sent, count, 1, 1)]
    terms = [t.reshape(-1, t.shape[-1]) for t in terms]
    steps = radices(count)
    for step in steps[1:]:
        terms = scatter_step(terms, count, *step)
    terms, back = lax.optimization_barrier((terms, back))
    total = sum(t.astype(F32) for t in terms).astype(BF)
    back, total = lax.optimization_barrier((back, total))
    grad_first = exchange(back).reshape(block, channels)
    two = second_grad(grad_mixed, firsts)
    for step in reversed(steps):
        total = gather_step(total, count, *step, after=two if step == steps[1] else ())
    grad_up, grad_down = write_weights(total, up_blocks.shape, down_blocks.shape, scale)
    one, grad_tokens = finish(factor_t, grad_first, tokens, gate_grad, scale)
    return (grad_tokens, one.reshape(1, block, block), two, grad_up, grad_down)


def solution(mesh):
    return jax.shard_map(
        on_device,
        mesh=mesh,
        in_specs=(
            P(("grp", "seq"), None),
            P(("grp", "seq"), None),
            P("seq", None, None),
            P("seq", None, None),
            P(),
            P(),
        ),
        out_specs=(
            P(("grp", "seq"), None),
            P(("grp", "seq"), None, None),
            P(("grp", "seq"), None, None),
            P("grp", None, None),
            P("grp", None, None),
        ),
        check_vma=False,
    )
```

```python
import jax
import jax.numpy as jnp
from jax import lax
from jax.experimental import pallas as pl
from jax.experimental.pallas import tpu as pltpu
from jax.sharding import PartitionSpec as P

BF = jnp.bfloat16
F32 = jnp.float32
VMEM_BYTES = 40 * 1024 * 1024
ANY = pl.BlockSpec(memory_space=pl.ANY)
VMEM = pl.BlockSpec(memory_space=pltpu.VMEM)
SCALAR = pl.BlockSpec(memory_space=pltpu.SMEM)


def in_hbm(array):
    return pltpu.with_memory_space_constraint(array, pltpu.HBM)


def in_vmem(array):
    return pltpu.with_memory_space_constraint(array, pltpu.VMEM)


def sigmoid(z):
    return 0.5 + 0.5 * jnp.tanh(0.5 * z)


def dot(a, b, ca, cb, **kw):
    return lax.dot_general(a, b, (((ca,), (cb,)), ((), ())), preferred_element_type=F32, **kw)


def params(steps=1):
    return pltpu.CompilerParams(
        dimension_semantics=("arbitrary",) * steps, vmem_limit_bytes=VMEM_BYTES
    )


def cost(flops, moved, trans=0):
    return pl.CostEstimate(flops=int(flops), bytes_accessed=int(moved), transcendentals=int(trans))


def row_copies(src, dst, sems, first, parts):
    rows = src.shape[0] // parts
    return [
        pltpu.make_async_copy(
            src.at[pl.ds(i * rows, rows)], dst.at[pl.ds(i * rows, rows)], sems.at[first + i]
        )
        for i in range(parts)
    ]


def mix_first(factor, blocked):
    block, channels = factor.shape[0], blocked.shape[1]
    tiles = 2
    step = block // tiles

    def body(f_hbm, x_hbm, u_hbm, f_all, x_all, u_all, sems):
        xs = row_copies(x_hbm, x_all, sems, 0, tiles)
        fs = row_copies(f_hbm, f_all, sems, tiles, tiles)
        us = row_copies(u_all, u_hbm, sems, 2 * tiles, tiles)
        for c in xs + fs:
            c.start()
        for c in xs:
            c.wait()
        for t in range(tiles):
            fs[t].wait()
            at = slice(t * step, (t + 1) * step)
            u_all[at, :] = dot(f_all[at, :], x_all[...], 1, 0).astype(BF)
            us[t].start()
        for c in us:
            c.wait()

    return pl.pallas_call(
        body,
        in_specs=[ANY, ANY],
        out_specs=ANY,
        out_shape=pltpu.HBM((block, channels), BF),
        scratch_shapes=[
            pltpu.VMEM((block, block), BF),
            pltpu.VMEM((block, channels), BF),
            pltpu.VMEM((block, channels), BF),
            pltpu.SemaphoreType.DMA((3 * tiles,)),
        ],
        compiler_params=params(0),
        cost_estimate=cost(2 * block * block * channels, 2 * block * (block + 2 * channels)),
        name="mix_first",
    )(in_hbm(factor), in_hbm(blocked))


def spread_factor(factor_two):
    here, n, _ = factor_two.shape
    groups = here // 16
    wide = n * 16
    turned = factor_two.reshape(groups, 16, n, n).transpose(0, 2, 1, 3).reshape(groups, wide, n)

    def body(in_ref, out_ref):
        col = lax.broadcasted_iota(jnp.int32, (n, wide), 1)
        row = lax.broadcasted_iota(jnp.int32, (n, wide), 0)
        pick = jnp.where(col // 16 == row, 1.0, 0.0).astype(BF)
        r = lax.broadcasted_iota(jnp.int32, (wide, wide), 0)
        c = lax.broadcasted_iota(jnp.int32, (wide, wide), 1)
        same = r % 16 == c % 16
        full = dot(in_ref[0], pick, 1, 0)
        out_ref[0] = jnp.where(same, full, 0.0).astype(BF)

    return pl.pallas_call(
        body,
        grid=(groups,),
        in_specs=[pl.BlockSpec((1, wide, n), lambda g: (g, 0, 0))],
        out_specs=pl.BlockSpec((1, wide, wide), lambda g: (g, 0, 0)),
        out_shape=jax.ShapeDtypeStruct((groups, wide, wide), BF),
        compiler_params=params(),
        cost_estimate=cost(2 * groups * wide * wide * n, 2 * groups * wide * wide),
        name="spread_factor",
    )(turned)


def mix_second(spread, cols, back):
    n, here, channels = cols.shape
    wide = n * 16
    groups = here // 16

    def body(m_ref, in_ref, out_hbm, out, sems):
        copies = []
        for g in range(groups):
            at = pl.ds(g * 16, 16)
            rows = in_ref[:, at, :].reshape(wide, channels)
            got = dot(m_ref[g], rows, 0 if back else 1, 0).astype(BF)
            out[:, at, :] = got.reshape(n, 16, channels)
            copies.append(
                pltpu.make_async_copy(out.at[:, at, :], out_hbm.at[:, at, :], sems.at[g])
            )
            copies[-1].start()
        for c in copies:
            c.wait()

    return pl.pallas_call(
        body,
        in_specs=[VMEM, VMEM],
        out_specs=ANY,
        out_shape=pltpu.HBM(cols.shape, BF),
        scratch_shapes=[pltpu.VMEM(cols.shape, BF), pltpu.SemaphoreType.DMA((groups,))],
        compiler_params=params(0),
        cost_estimate=cost(
            2 * groups * wide * wide * channels, 4 * cols.size + 2 * groups * wide * wide
        ),
        name="mix_second_back" if back else "mix_second",
    )(in_vmem(spread), in_vmem(cols))


def grad_second(grads, firsts, scale):
    n, here, channels = grads.shape
    wide = n * 16
    groups = here // 16

    def body(g_ref, u_ref, out_ref):
        r = lax.broadcasted_iota(jnp.int32, (wide, wide), 0)
        c = lax.broadcasted_iota(jnp.int32, (wide, wide), 1)
        same = r % 16 == c % 16
        row = lax.broadcasted_iota(jnp.int32, (wide, n), 0)
        col = lax.broadcasted_iota(jnp.int32, (wide, n), 1)
        pick = jnp.where(row // 16 == col, 1.0, 0.0)
        for k in range(groups):
            at = pl.ds(k * 16, 16)
            g = g_ref[:, at, :].reshape(wide, channels)
            u = u_ref[:, at, :].reshape(wide, channels)
            kept = jnp.where(same, dot(g, u, 1, 1), 0.0)
            out_ref[k] = dot(kept, pick, 1, 0, precision=lax.Precision.HIGHEST) * scale

    out = pl.pallas_call(
        body,
        in_specs=[VMEM, VMEM],
        out_specs=VMEM,
        out_shape=jax.ShapeDtypeStruct((groups, wide, n), F32),
        compiler_params=params(0),
        cost_estimate=cost(2 * groups * wide * wide * channels, 4 * grads.size),
        name="grad_second",
    )(in_vmem(grads), in_vmem(firsts))
    return out.reshape(groups, n, 16, n).transpose(0, 2, 1, 3).reshape(here, n, n)


def middle(half, blocked, incoming, mixed, up_blocks, down_blocks):
    groups, width, inner = up_blocks.shape
    sub = inner // groups
    rows, channels = blocked.shape
    step = min(256, rows)
    tiles = rows // step

    def body(half_ref, x_hbm, g_hbm, v_ref, up_hbm, down_hbm, *refs):
        dv_hbm, r_hbm, kept_hbm, sent_hbm = refs[:4]
        x_ref, g_ref, up_ref, down_ref, dv, r_ref, w, halves, sems = refs[4:]

        def rows_copy(src, dst, kind, t):
            at = pl.ds(t * step, step)
            return pltpu.make_async_copy(src.at[at], dst.at[at], sems.at[kind * tiles + t])

        def whole_copy(src, dst, number):
            return pltpu.make_async_copy(src, dst, sems.at[4 * tiles + number])

        fetch_up = whole_copy(up_hbm, up_ref, 0)
        fetch_down = whole_copy(down_hbm, down_ref, 1)
        rows_copy(x_hbm, x_ref, 0, 0).start()
        fetch_up.start()
        rows_copy(g_hbm, g_ref, 1, 0).start()
        fetch_down.start()
        for t in range(1, tiles):
            rows_copy(x_hbm, x_ref, 0, t).start()
            rows_copy(g_hbm, g_ref, 1, t).start()
        w[...] = jnp.zeros_like(w)
        fetch_up.wait()
        fetch_down.wait()

        def tile(t, carry):
            rows_copy(x_hbm, x_ref, 0, t).wait()
            rows_copy(g_hbm, g_ref, 1, t).wait()
            at = pl.ds(pl.multiple_of(t * step, step), step)
            x = x_ref[at, :].astype(F32)
            g = g_ref[at, :]
            v = v_ref[at, :].astype(F32)
            sx = sigmoid(x)
            gate = x * sx
            h = (x + v * gate).astype(BF)
            h_parts = [h[:, b * width : (b + 1) * width] for b in range(groups)]
            g_parts = [g[:, b * width : (b + 1) * width] for b in range(groups)]
            acts, slopes, back = [], [], []
            for b in range(groups):
                a = dot(h_parts[b], up_ref[b], 1, 0).astype(BF)
                s = sigmoid(a)
                q = a * s
                acts.append(q)
                slopes.append(s + q * (1 - s))
                back.append(dot(g_parts[b], down_ref[b], 1, 1).astype(BF))
            grads = []
            for b in range(groups):
                lanes = slice(b * sub, (b + 1) * sub)
                perm = jnp.concatenate([acts[p][:, lanes] for p in range(groups)], axis=1)
                w[1, b] += dot(g_parts[b], perm, 0, 0)
                dq = jnp.concatenate([back[p][:, lanes] for p in range(groups)], axis=1)
                da = dq * slopes[b]
                w[0, b] += dot(h_parts[b], da, 0, 0)
                grads.append(dot(da, up_ref[b], 1, 1))
            dh = (g.astype(F32) + jnp.concatenate(grads, axis=1)).astype(BF).astype(F32)
            dv[at, :] = (dh * gate).astype(BF)
            rows_copy(dv, dv_hbm, 2, t).start()
            r_ref[at, :] = (dh * (1.0 + v * (sx + gate * (1.0 - sx)))).astype(BF)
            rows_copy(r_ref, r_hbm, 3, t).start()
            return carry

        lax.fori_loop(0, tiles, tile, 0)
        halves[1] = w[1 - half_ref[0]].astype(BF)
        send = whole_copy(halves.at[1], sent_hbm, 2)
        send.start()
        halves[0] = w[half_ref[0]].astype(BF)
        keep = whole_copy(halves.at[0], kept_hbm, 3)
        keep.start()
        for t in range(tiles):
            rows_copy(dv, dv_hbm, 2, t).wait()
            rows_copy(r_ref, r_hbm, 3, t).wait()
        send.wait()
        keep.wait()

    hidden = rows * groups * inner
    return pl.pallas_call(
        body,
        in_specs=[SCALAR, ANY, ANY, VMEM, ANY, ANY],
        out_specs=[ANY] * 4,
        out_shape=[
            pltpu.HBM((rows, channels), BF),
            pltpu.HBM((rows, channels), BF),
            pltpu.HBM(up_blocks.shape, BF),
            pltpu.HBM(up_blocks.shape, BF),
        ],
        scratch_shapes=[
            pltpu.VMEM((rows, channels), BF),
            pltpu.VMEM((rows, channels), BF),
            pltpu.VMEM(up_blocks.shape, BF),
            pltpu.VMEM(down_blocks.shape, BF),
            pltpu.VMEM((rows, channels), BF),
            pltpu.VMEM((rows, channels), BF),
            pltpu.VMEM((2, groups, width, inner), F32),
            pltpu.VMEM((2, groups, width, inner), BF),
            pltpu.SemaphoreType.DMA((4 * tiles + 4,)),
        ],
        compiler_params=params(0),
        cost_estimate=cost(
            10 * hidden * width, 10 * rows * channels + 8 * groups * width * inner, hidden
        ),
        name="middle",
    )(half, in_hbm(blocked), in_hbm(incoming), in_vmem(mixed), in_hbm(up_blocks), in_hbm(down_blocks))


def finish(factor, grad_first, blocked, gate_grad, scale):
    block, channels = blocked.shape
    tiles = 4
    step = block // tiles

    def body(f_hbm, d_hbm, x_hbm, r_hbm, one_hbm, out_hbm, f, d, x, r, one, out, sems):
        ds = row_copies(d_hbm, d, sems, 0, tiles)
        xs = row_copies(x_hbm, x, sems, tiles, tiles)
        fs = row_copies(f_hbm, f, sems, 2 * tiles, tiles)
        rs = row_copies(r_hbm, r, sems, 3 * tiles, tiles)
        outs = row_copies(out, out_hbm, sems, 4 * tiles, 1)
        ones = []
        for c in ds + xs + fs + rs:
            c.start()
        for c in ds:
            c.wait()
        for t in range(tiles):
            at = slice(t * step, (t + 1) * step)
            xs[t].wait()
            one[t] = dot(d[...], x[at, :], 1, 1) * scale
            ones.append(
                pltpu.make_async_copy(
                    one.at[t], one_hbm.at[:, pl.ds(t * step, step)], sems.at[4 * tiles + 1 + t]
                )
            )
            ones[t].start()
        for c in fs + rs:
            c.wait()
        out[...] = (dot(f[...], d[...], 0, 0) + r[...].astype(F32)).astype(BF)
        outs[0].start()
        for c in ones + outs:
            c.wait()

    return pl.pallas_call(
        body,
        in_specs=[ANY] * 4,
        out_specs=[ANY] * 2,
        out_shape=[pltpu.HBM((block, block), F32), pltpu.HBM((block, channels), BF)],
        scratch_shapes=[
            pltpu.VMEM((block, block), BF),
            pltpu.VMEM((block, channels), BF),
            pltpu.VMEM((block, channels), BF),
            pltpu.VMEM((block, channels), BF),
            pltpu.VMEM((tiles, block, step), F32),
            pltpu.VMEM((block, channels), BF),
            pltpu.SemaphoreType.DMA((5 * tiles + 1,)),
        ],
        compiler_params=params(0),
        cost_estimate=cost(4 * block * block * channels, 6 * block * block + 8 * block * channels),
        name="finish",
    )(in_hbm(factor), in_hbm(grad_first), in_hbm(blocked), in_hbm(gate_grad))


def radices(count):
    steps, stride = [], 1
    while stride < count:
        radix = 4 if stride >= 4 and count // stride == 4 else 2
        steps.append((stride, radix))
        stride *= radix
    return steps


def swap(values, count, stride, s):
    return lax.ppermute(values, "seq", [(i, i ^ (stride * s)) for i in range(count)])


def add_and_cut(terms, digit, radix):
    rows, columns = terms[0].shape
    share = rows // radix

    number = len(terms)

    number = len(terms)
    shape = (radix, share, columns)

    def body(digit_ref, *refs):
        ins, outs = refs[:number], refs[number : number + radix]
        held, made, sems = refs[number + radix : -radix - 1], refs[-radix - 1 : -1], refs[-1]
        copies = [pltpu.make_async_copy(ins[i], held[i], sems.at[i]) for i in range(number)]
        for c in copies:
            c.start()
        for c in copies:
            c.wait()
        copies = []
        for s, ref in enumerate(made):
            total = held[0][digit_ref[0] ^ s].astype(F32)
            for term in held[1:]:
                total = total + term[digit_ref[0] ^ s].astype(F32)
            ref[...] = total.astype(ref.dtype)
            copies.append(pltpu.make_async_copy(ref, outs[s], sems.at[number + s]))
            copies[-1].start()
        for c in copies:
            c.wait()

    types = [F32] + [BF] * (radix - 1)
    return pl.pallas_call(
        body,
        in_specs=[SCALAR] + [ANY] * number,
        out_specs=[ANY] * radix,
        out_shape=[pltpu.HBM((share, columns), t) for t in types],
        scratch_shapes=[pltpu.VMEM(shape, t.dtype) for t in terms]
        + [pltpu.VMEM((share, columns), t) for t in types]
        + [pltpu.SemaphoreType.DMA((number + radix,))],
        compiler_params=params(0),
        cost_estimate=cost(rows * columns, 8 * rows * columns),
        name="add_and_cut",
    )(digit.reshape(1), *[t.reshape(shape) for t in terms])


def scatter_step(terms, count, stride, radix):
    digit = (lax.axis_index("seq").astype(jnp.int32) // stride) % radix
    kept, *send = add_and_cut(terms, digit, radix)
    return [kept] + [swap(a, count, stride, s + 1) for s, a in enumerate(send)]


def gather_step(share, count, stride, radix, after=()):
    digit = (lax.axis_index("seq") // stride) % radix
    got = [share] + [swap(share, count, stride, s) for s in range(1, radix)]
    got, after = lax.optimization_barrier((got, after))
    if radix == 2:
        low = jnp.where(digit == 0, got[0], got[1])
        high = jnp.where(digit == 0, got[1], got[0])
        return jnp.concatenate([low, high], axis=0)
    whole = jnp.zeros((radix,) + share.shape, share.dtype)
    for s in range(radix):
        whole = lax.dynamic_update_index_in_dim(whole, got[s], digit ^ s, 0)
    return whole.reshape(radix * share.shape[0], share.shape[1])


def write_weights(total, up_shape, down_shape, scale):
    groups, width, inner = up_shape

    def body(up_in, down_in, up_ref, down_ref):
        up_ref[0] = up_in[...].astype(F32) * scale
        down_ref[0] = (down_in[...].astype(F32) * scale).T

    return pl.pallas_call(
        body,
        grid=(groups,),
        in_specs=[
            pl.BlockSpec((width, inner), lambda b: (b, 0)),
            pl.BlockSpec((width, inner), lambda b: (groups + b, 0)),
        ],
        out_specs=[
            pl.BlockSpec((1, width, inner), lambda b: (b, 0, 0)),
            pl.BlockSpec((1, inner, width), lambda b: (b, 0, 0)),
        ],
        out_shape=[
            jax.ShapeDtypeStruct(up_shape, F32),
            jax.ShapeDtypeStruct(down_shape, F32),
        ],
        compiler_params=params(),
        cost_estimate=cost(groups * width * inner, 12 * groups * width * inner),
        name="write_weights",
    )(total, total)


def on_device(tokens, cotangent, factor_one, factor_two, up_blocks, down_blocks):
    count = lax.axis_size("seq")
    block, channels = factor_one.shape[1], tokens.shape[1]
    here = block // count
    scale = float(count * tokens.shape[0]) ** (-0.5)
    factor = factor_one.reshape(block, block)
    grouped = here % 16 == 0

    def exchange(values):
        cut = values.reshape(count, here, channels)
        return lax.all_to_all(cut, "seq", split_axis=0, concat_axis=0, tiled=True)

    if grouped:
        spread = spread_factor(factor_two)

    def second(cols, back):
        if grouped:
            return mix_second(spread, cols, back)
        names = "kmj,mkc->jkc" if back else "kmj,jkc->mkc"
        return jnp.einsum(names, factor_two, cols, preferred_element_type=F32).astype(BF)

    def second_grad(grads, firsts):
        if grouped:
            return grad_second(grads, firsts, scale)
        return jnp.einsum("mkc,jkc->kmj", grads, firsts, preferred_element_type=F32) * scale

    half = (lax.axis_index("seq") % 2).astype(jnp.int32).reshape(1)
    firsts = exchange(mix_first(factor, tokens))
    mixed = exchange(second(firsts, False)).reshape(block, channels)
    dv, gate_grad, kept, sent = middle(half, tokens, cotangent, mixed, up_blocks, down_blocks)
    grad_mixed = exchange(dv)
    back = second(grad_mixed, True)
    terms = [kept, swap(sent, count, 1, 1)]
    terms = [t.reshape(-1, t.shape[-1]) for t in terms]
    steps = radices(count)
    for step in steps[1:]:
        terms = scatter_step(terms, count, *step)
    terms, back = lax.optimization_barrier((terms, back))
    total = sum(t.astype(F32) for t in terms).astype(BF)
    back, total = lax.optimization_barrier((back, total))
    grad_first = exchange(back).reshape(block, channels)
    two = second_grad(grad_mixed, firsts)
    for step in reversed(steps):
        total = gather_step(total, count, *step, after=two if step == steps[1] else ())
    grad_up, grad_down = write_weights(total, up_blocks.shape, down_blocks.shape, scale)
    one, grad_tokens = finish(factor, grad_first, tokens, gate_grad, scale)
    return (grad_tokens, one.reshape(1, block, block), two, grad_up, grad_down)


def solution(mesh):
    return jax.shard_map(
        on_device,
        mesh=mesh,
        in_specs=(
            P(("grp", "seq"), None),
            P(("grp", "seq"), None),
            P("seq", None, None),
            P("seq", None, None),
            P(),
            P(),
        ),
        out_specs=(
            P(("grp", "seq"), None),
            P(("grp", "seq"), None, None),
            P(("grp", "seq"), None, None),
            P("grp", None, None),
            P("grp", None, None),
        ),
        check_vma=False,
    )
```

```python
import jax
import jax.numpy as jnp
from jax import lax
from jax.experimental import pallas as pl
from jax.experimental.pallas import tpu as pltpu
from jax.sharding import PartitionSpec as P

BF = jnp.bfloat16
F32 = jnp.float32
VMEM_BYTES = 40 * 1024 * 1024
ANY = pl.BlockSpec(memory_space=pl.ANY)
VMEM = pl.BlockSpec(memory_space=pltpu.VMEM)
SCALAR = pl.BlockSpec(memory_space=pltpu.SMEM)


def in_hbm(array):
    return pltpu.with_memory_space_constraint(array, pltpu.HBM)


def in_vmem(array):
    return pltpu.with_memory_space_constraint(array, pltpu.VMEM)


def sigmoid(z):
    return 0.5 + 0.5 * jnp.tanh(0.5 * z)


def dot(a, b, ca, cb, **kw):
    return lax.dot_general(a, b, (((ca,), (cb,)), ((), ())), preferred_element_type=F32, **kw)


def params(steps=1):
    return pltpu.CompilerParams(
        dimension_semantics=("arbitrary",) * steps, vmem_limit_bytes=VMEM_BYTES
    )


def cost(flops, moved, trans=0):
    return pl.CostEstimate(flops=int(flops), bytes_accessed=int(moved), transcendentals=int(trans))


def row_copies(src, dst, sems, first, parts):
    rows = src.shape[0] // parts
    return [
        pltpu.make_async_copy(
            src.at[pl.ds(i * rows, rows)], dst.at[pl.ds(i * rows, rows)], sems.at[first + i]
        )
        for i in range(parts)
    ]


def mix_first(factor, blocked):
    block, channels = factor.shape[0], blocked.shape[1]
    tiles = 4
    step = block // tiles

    def body(f_hbm, x_hbm, u_hbm, f_all, x_all, u_all, sems):
        xs = row_copies(x_hbm, x_all, sems, 0, tiles)
        fs = row_copies(f_hbm, f_all, sems, tiles, tiles)
        us = row_copies(u_all, u_hbm, sems, 2 * tiles, tiles)
        for c in xs + fs:
            c.start()
        for c in xs:
            c.wait()
        for t in range(tiles):
            fs[t].wait()
            at = slice(t * step, (t + 1) * step)
            u_all[at, :] = dot(f_all[at, :], x_all[...], 1, 0).astype(BF)
            us[t].start()
        for c in us:
            c.wait()

    return pl.pallas_call(
        body,
        in_specs=[ANY, ANY],
        out_specs=ANY,
        out_shape=pltpu.HBM((block, channels), BF),
        scratch_shapes=[
            pltpu.VMEM((block, block), BF),
            pltpu.VMEM((block, channels), BF),
            pltpu.VMEM((block, channels), BF),
            pltpu.SemaphoreType.DMA((3 * tiles,)),
        ],
        compiler_params=params(0),
        cost_estimate=cost(2 * block * block * channels, 2 * block * (block + 2 * channels)),
        name="mix_first",
    )(in_hbm(factor), in_hbm(blocked))


def spread_factor(factor_two):
    here, n, _ = factor_two.shape
    groups = here // 16
    wide = n * 16
    turned = factor_two.reshape(groups, 16, n, n).transpose(0, 2, 1, 3).reshape(groups, wide, n)

    def body(in_ref, out_ref):
        col = lax.broadcasted_iota(jnp.int32, (n, wide), 1)
        row = lax.broadcasted_iota(jnp.int32, (n, wide), 0)
        pick = jnp.where(col // 16 == row, 1.0, 0.0).astype(BF)
        r = lax.broadcasted_iota(jnp.int32, (wide, wide), 0)
        c = lax.broadcasted_iota(jnp.int32, (wide, wide), 1)
        same = r % 16 == c % 16
        full = dot(in_ref[0], pick, 1, 0)
        out_ref[0] = jnp.where(same, full, 0.0).astype(BF)

    return pl.pallas_call(
        body,
        grid=(groups,),
        in_specs=[pl.BlockSpec((1, wide, n), lambda g: (g, 0, 0))],
        out_specs=pl.BlockSpec((1, wide, wide), lambda g: (g, 0, 0)),
        out_shape=jax.ShapeDtypeStruct((groups, wide, wide), BF),
        compiler_params=params(),
        cost_estimate=cost(2 * groups * wide * wide * n, 2 * groups * wide * wide),
        name="spread_factor",
    )(turned)


def mix_second(spread, cols, back):
    n, here, channels = cols.shape
    wide = n * 16
    groups = here // 16

    def body(m_ref, in_ref, out_hbm, out, sems):
        copies = []
        for g in range(groups):
            at = pl.ds(g * 16, 16)
            rows = in_ref[:, at, :].reshape(wide, channels)
            got = dot(m_ref[g], rows, 0 if back else 1, 0).astype(BF)
            out[:, at, :] = got.reshape(n, 16, channels)
            copies.append(
                pltpu.make_async_copy(out.at[:, at, :], out_hbm.at[:, at, :], sems.at[g])
            )
            copies[-1].start()
        for c in copies:
            c.wait()

    return pl.pallas_call(
        body,
        in_specs=[VMEM, VMEM],
        out_specs=ANY,
        out_shape=pltpu.HBM(cols.shape, BF),
        scratch_shapes=[pltpu.VMEM(cols.shape, BF), pltpu.SemaphoreType.DMA((groups,))],
        compiler_params=params(0),
        cost_estimate=cost(
            2 * groups * wide * wide * channels, 4 * cols.size + 2 * groups * wide * wide
        ),
        name="mix_second_back" if back else "mix_second",
    )(in_vmem(spread), in_vmem(cols))


def grad_second(grads, firsts, scale):
    n, here, channels = grads.shape
    wide = n * 16
    groups = here // 16

    def body(g_ref, u_ref, out_ref):
        r = lax.broadcasted_iota(jnp.int32, (wide, wide), 0)
        c = lax.broadcasted_iota(jnp.int32, (wide, wide), 1)
        same = r % 16 == c % 16
        row = lax.broadcasted_iota(jnp.int32, (wide, n), 0)
        col = lax.broadcasted_iota(jnp.int32, (wide, n), 1)
        pick = jnp.where(row // 16 == col, 1.0, 0.0)
        for k in range(groups):
            at = pl.ds(k * 16, 16)
            g = g_ref[:, at, :].reshape(wide, channels)
            u = u_ref[:, at, :].reshape(wide, channels)
            kept = jnp.where(same, dot(g, u, 1, 1), 0.0)
            out_ref[k] = dot(kept, pick, 1, 0, precision=lax.Precision.HIGHEST) * scale

    out = pl.pallas_call(
        body,
        in_specs=[VMEM, VMEM],
        out_specs=VMEM,
        out_shape=jax.ShapeDtypeStruct((groups, wide, n), F32),
        compiler_params=params(0),
        cost_estimate=cost(2 * groups * wide * wide * channels, 4 * grads.size),
        name="grad_second",
    )(in_vmem(grads), in_vmem(firsts))
    return out.reshape(groups, n, 16, n).transpose(0, 2, 1, 3).reshape(here, n, n)


def middle(half, blocked, incoming, mixed, up_blocks, down_blocks):
    groups, width, inner = up_blocks.shape
    sub = inner // groups
    rows, channels = blocked.shape
    step = min(256, rows)
    tiles = rows // step

    def body(half_ref, x_hbm, g_hbm, v_ref, up_hbm, down_hbm, *refs):
        dv_hbm, r_hbm, kept_hbm, sent_hbm = refs[:4]
        x_ref, g_ref, up_ref, down_ref, dv, r_ref, w, halves, sems = refs[4:]

        def rows_copy(src, dst, kind, t):
            at = pl.ds(t * step, step)
            return pltpu.make_async_copy(src.at[at], dst.at[at], sems.at[kind * tiles + t])

        def whole_copy(src, dst, number):
            return pltpu.make_async_copy(src, dst, sems.at[4 * tiles + number])

        fetch_up = whole_copy(up_hbm, up_ref, 0)
        fetch_down = whole_copy(down_hbm, down_ref, 1)
        rows_copy(x_hbm, x_ref, 0, 0).start()
        fetch_up.start()
        rows_copy(g_hbm, g_ref, 1, 0).start()
        fetch_down.start()
        for t in range(1, tiles):
            rows_copy(x_hbm, x_ref, 0, t).start()
            rows_copy(g_hbm, g_ref, 1, t).start()
        w[...] = jnp.zeros_like(w)
        fetch_up.wait()
        fetch_down.wait()

        def tile(t, carry):
            rows_copy(x_hbm, x_ref, 0, t).wait()
            rows_copy(g_hbm, g_ref, 1, t).wait()
            at = pl.ds(pl.multiple_of(t * step, step), step)
            x = x_ref[at, :].astype(F32)
            g = g_ref[at, :]
            v = v_ref[at, :].astype(F32)
            sx = sigmoid(x)
            gate = x * sx
            h = (x + v * gate).astype(BF)
            h_parts = [h[:, b * width : (b + 1) * width] for b in range(groups)]
            g_parts = [g[:, b * width : (b + 1) * width] for b in range(groups)]
            acts, slopes, back = [], [], []
            for b in range(groups):
                a = dot(h_parts[b], up_ref[b], 1, 0).astype(BF)
                s = sigmoid(a)
                q = a * s
                acts.append(q)
                slopes.append(s + q * (1 - s))
                back.append(dot(g_parts[b], down_ref[b], 1, 1).astype(BF))
            grads = []
            for b in range(groups):
                lanes = slice(b * sub, (b + 1) * sub)
                perm = jnp.concatenate([acts[p][:, lanes] for p in range(groups)], axis=1)
                w[1, b] += dot(g_parts[b], perm, 0, 0)
                dq = jnp.concatenate([back[p][:, lanes] for p in range(groups)], axis=1)
                da = dq * slopes[b]
                w[0, b] += dot(h_parts[b], da, 0, 0)
                grads.append(dot(da, up_ref[b], 1, 1))
            dh = (g.astype(F32) + jnp.concatenate(grads, axis=1)).astype(BF).astype(F32)
            dv[at, :] = (dh * gate).astype(BF)
            rows_copy(dv, dv_hbm, 2, t).start()
            r_ref[at, :] = (dh * (1.0 + v * (sx + gate * (1.0 - sx)))).astype(BF)
            rows_copy(r_ref, r_hbm, 3, t).start()
            return carry

        lax.fori_loop(0, tiles, tile, 0)
        halves[1] = w[1 - half_ref[0]].astype(BF)
        send = whole_copy(halves.at[1], sent_hbm, 2)
        send.start()
        halves[0] = w[half_ref[0]].astype(BF)
        keep = whole_copy(halves.at[0], kept_hbm, 3)
        keep.start()
        for t in range(tiles):
            rows_copy(dv, dv_hbm, 2, t).wait()
            rows_copy(r_ref, r_hbm, 3, t).wait()
        send.wait()
        keep.wait()

    hidden = rows * groups * inner
    return pl.pallas_call(
        body,
        in_specs=[SCALAR, ANY, ANY, VMEM, ANY, ANY],
        out_specs=[ANY] * 4,
        out_shape=[
            pltpu.HBM((rows, channels), BF),
            pltpu.HBM((rows, channels), BF),
            pltpu.HBM(up_blocks.shape, BF),
            pltpu.HBM(up_blocks.shape, BF),
        ],
        scratch_shapes=[
            pltpu.VMEM((rows, channels), BF),
            pltpu.VMEM((rows, channels), BF),
            pltpu.VMEM(up_blocks.shape, BF),
            pltpu.VMEM(down_blocks.shape, BF),
            pltpu.VMEM((rows, channels), BF),
            pltpu.VMEM((rows, channels), BF),
            pltpu.VMEM((2, groups, width, inner), F32),
            pltpu.VMEM((2, groups, width, inner), BF),
            pltpu.SemaphoreType.DMA((4 * tiles + 4,)),
        ],
        compiler_params=params(0),
        cost_estimate=cost(
            10 * hidden * width, 10 * rows * channels + 8 * groups * width * inner, hidden
        ),
        name="middle",
    )(half, in_hbm(blocked), in_hbm(incoming), in_vmem(mixed), in_hbm(up_blocks), in_hbm(down_blocks))


def finish(factor, grad_first, blocked, gate_grad, scale):
    block, channels = blocked.shape
    tiles = 4
    step = block // tiles

    def body(f_hbm, d_hbm, x_hbm, r_hbm, one_hbm, out_hbm, f, d, x, r, one, out, sems):
        ds = row_copies(d_hbm, d, sems, 0, tiles)
        xs = row_copies(x_hbm, x, sems, tiles, tiles)
        fs = row_copies(f_hbm, f, sems, 2 * tiles, tiles)
        rs = row_copies(r_hbm, r, sems, 3 * tiles, tiles)
        ones = row_copies(one, one_hbm, sems, 4 * tiles, tiles)
        outs = row_copies(out, out_hbm, sems, 5 * tiles, tiles)
        for c in xs + ds + fs + rs:
            c.start()
        for c in xs:
            c.wait()
        for t in range(tiles):
            at = slice(t * step, (t + 1) * step)
            ds[t].wait()
            one[at, :] = dot(d[at, :], x[...], 1, 1) * scale
            ones[t].start()
        for c in fs:
            c.wait()
        for t in range(tiles):
            at = slice(t * step, (t + 1) * step)
            rs[t].wait()
            total = dot(f[:, at], d[...], 0, 0) + r[at, :].astype(F32)
            out[at, :] = total.astype(BF)
            outs[t].start()
        for c in ones + outs:
            c.wait()

    return pl.pallas_call(
        body,
        in_specs=[ANY] * 4,
        out_specs=[ANY] * 2,
        out_shape=[pltpu.HBM((block, block), F32), pltpu.HBM((block, channels), BF)],
        scratch_shapes=[
            pltpu.VMEM((block, block), BF),
            pltpu.VMEM((block, channels), BF),
            pltpu.VMEM((block, channels), BF),
            pltpu.VMEM((block, channels), BF),
            pltpu.VMEM((block, block), F32),
            pltpu.VMEM((block, channels), BF),
            pltpu.SemaphoreType.DMA((6 * tiles,)),
        ],
        compiler_params=params(0),
        cost_estimate=cost(4 * block * block * channels, 6 * block * block + 8 * block * channels),
        name="finish",
    )(in_hbm(factor), in_hbm(grad_first), in_hbm(blocked), in_hbm(gate_grad))


def radices(count):
    steps, stride = [], 1
    while stride < count:
        radix = 4 if stride >= 4 and count // stride == 4 else 2
        steps.append((stride, radix))
        stride *= radix
    return steps


def swap(values, count, stride, s):
    return lax.ppermute(values, "seq", [(i, i ^ (stride * s)) for i in range(count)])


def add_and_cut(terms, digit, radix):
    rows, columns = terms[0].shape
    share = rows // radix

    number = len(terms)

    number = len(terms)
    shape = (radix, share, columns)

    def body(digit_ref, *refs):
        ins, outs = refs[:number], refs[number : number + radix]
        held, made, sems = refs[number + radix : -radix - 1], refs[-radix - 1 : -1], refs[-1]
        copies = [pltpu.make_async_copy(ins[i], held[i], sems.at[i]) for i in range(number)]
        for c in copies:
            c.start()
        for c in copies:
            c.wait()
        copies = []
        for s, ref in enumerate(made):
            total = held[0][digit_ref[0] ^ s].astype(F32)
            for term in held[1:]:
                total = total + term[digit_ref[0] ^ s].astype(F32)
            ref[...] = total.astype(ref.dtype)
            copies.append(pltpu.make_async_copy(ref, outs[s], sems.at[number + s]))
            copies[-1].start()
        for c in copies:
            c.wait()

    types = [F32] + [BF] * (radix - 1)
    return pl.pallas_call(
        body,
        in_specs=[SCALAR] + [ANY] * number,
        out_specs=[ANY] * radix,
        out_shape=[pltpu.HBM((share, columns), t) for t in types],
        scratch_shapes=[pltpu.VMEM(shape, t.dtype) for t in terms]
        + [pltpu.VMEM((share, columns), t) for t in types]
        + [pltpu.SemaphoreType.DMA((number + radix,))],
        compiler_params=params(0),
        cost_estimate=cost(rows * columns, 8 * rows * columns),
        name="add_and_cut",
    )(digit.reshape(1), *[t.reshape(shape) for t in terms])


def scatter_step(terms, count, stride, radix):
    digit = (lax.axis_index("seq").astype(jnp.int32) // stride) % radix
    kept, *send = add_and_cut(terms, digit, radix)
    return [kept] + [swap(a, count, stride, s + 1) for s, a in enumerate(send)]


def gather_step(share, count, stride, radix, before=(), after=()):
    digit = (lax.axis_index("seq") // stride) % radix
    near, before = lax.optimization_barrier((share, before))
    far = [swap(share, count, stride, s) for s in range(2, radix)]
    got = [share, swap(near, count, stride, 1)] + far
    got, after = lax.optimization_barrier((got, after))
    if radix == 2:
        low = jnp.where(digit == 0, got[0], got[1])
        high = jnp.where(digit == 0, got[1], got[0])
        return jnp.concatenate([low, high], axis=0)
    whole = jnp.zeros((radix,) + share.shape, share.dtype)
    for s in range(radix):
        whole = lax.dynamic_update_index_in_dim(whole, got[s], digit ^ s, 0)
    return whole.reshape(radix * share.shape[0], share.shape[1])


def write_weights(half, mine, other, up_shape, down_shape, scale):
    groups, width, inner = up_shape

    def body(half_ref, mine_ref, other_ref, up_ref, down_ref):
        first = half_ref[0] == 0
        a, b = mine_ref[...].astype(F32) * scale, other_ref[...].astype(F32) * scale
        up_ref[0] = jnp.where(first, a, b)
        down_ref[0] = jnp.where(first, b, a).T

    block = pl.BlockSpec((width, inner), lambda b: (b, 0))
    return pl.pallas_call(
        body,
        grid=(groups,),
        in_specs=[SCALAR, block, block],
        out_specs=[
            pl.BlockSpec((1, width, inner), lambda b: (b, 0, 0)),
            pl.BlockSpec((1, inner, width), lambda b: (b, 0, 0)),
        ],
        out_shape=[
            jax.ShapeDtypeStruct(up_shape, F32),
            jax.ShapeDtypeStruct(down_shape, F32),
        ],
        compiler_params=params(),
        cost_estimate=cost(groups * width * inner, 12 * groups * width * inner),
        name="write_weights",
    )(half, mine, other)


def on_device(tokens, cotangent, factor_one, factor_two, up_blocks, down_blocks):
    count = lax.axis_size("seq")
    block, channels = factor_one.shape[1], tokens.shape[1]
    here = block // count
    scale = float(count * tokens.shape[0]) ** (-0.5)
    factor = factor_one.reshape(block, block)
    grouped = here % 16 == 0

    def exchange(values):
        cut = values.reshape(count, here, channels)
        return lax.all_to_all(cut, "seq", split_axis=0, concat_axis=0, tiled=True)

    if grouped:
        spread = spread_factor(factor_two)

    def second(cols, back):
        if grouped:
            return mix_second(spread, cols, back)
        names = "kmj,mkc->jkc" if back else "kmj,jkc->mkc"
        return jnp.einsum(names, factor_two, cols, preferred_element_type=F32).astype(BF)

    def second_grad(grads, firsts):
        if grouped:
            return grad_second(grads, firsts, scale)
        return jnp.einsum("mkc,jkc->kmj", grads, firsts, preferred_element_type=F32) * scale

    half = (lax.axis_index("seq") % 2).astype(jnp.int32).reshape(1)
    firsts = exchange(mix_first(factor, tokens))
    mixed = exchange(second(firsts, False)).reshape(block, channels)
    dv, gate_grad, kept, sent = middle(half, tokens, cotangent, mixed, up_blocks, down_blocks)
    grad_mixed = exchange(dv)
    back = second(grad_mixed, True)
    terms = [kept, swap(sent, count, 1, 1)]
    terms = [t.reshape(-1, t.shape[-1]) for t in terms]
    steps = radices(count)
    for step in steps[1:]:
        terms = scatter_step(terms, count, *step)
    terms, back = lax.optimization_barrier((terms, back))
    total = sum(t.astype(F32) for t in terms).astype(BF)
    back, total = lax.optimization_barrier((back, total))
    grad_first = exchange(back).reshape(block, channels)
    two = second_grad(grad_mixed, firsts)
    for step in reversed(steps[1:]):
        last = step == steps[-1]
        total = gather_step(
            total, count, *step, before=two if last else (), after=() if last else two
        )
    other = swap(total, count, 1, 1)
    grad_up, grad_down = write_weights(half, total, other, up_blocks.shape, down_blocks.shape, scale)
    one, grad_tokens = finish(factor, grad_first, tokens, gate_grad, scale)
    return (grad_tokens, one.reshape(1, block, block), two, grad_up, grad_down)


def solution(mesh):
    return jax.shard_map(
        on_device,
        mesh=mesh,
        in_specs=(
            P(("grp", "seq"), None),
            P(("grp", "seq"), None),
            P("seq", None, None),
            P("seq", None, None),
            P(),
            P(),
        ),
        out_specs=(
            P(("grp", "seq"), None),
            P(("grp", "seq"), None, None),
            P(("grp", "seq"), None, None),
            P("grp", None, None),
            P("grp", None, None),
        ),
        check_vma=False,
    )
```

```python
import jax
import jax.numpy as jnp
from jax import lax
from jax.experimental import pallas as pl
from jax.experimental.pallas import tpu as pltpu
from jax.sharding import PartitionSpec as P

BF = jnp.bfloat16
F32 = jnp.float32
VMEM_BYTES = 40 * 1024 * 1024
ANY = pl.BlockSpec(memory_space=pl.ANY)
VMEM = pl.BlockSpec(memory_space=pltpu.VMEM)
SCALAR = pl.BlockSpec(memory_space=pltpu.SMEM)


def in_hbm(array):
    return pltpu.with_memory_space_constraint(array, pltpu.HBM)


def in_vmem(array):
    return pltpu.with_memory_space_constraint(array, pltpu.VMEM)


def sigmoid(z):
    return 0.5 + 0.5 * jnp.tanh(0.5 * z)


def dot(a, b, ca, cb, **kw):
    return lax.dot_general(a, b, (((ca,), (cb,)), ((), ())), preferred_element_type=F32, **kw)


def params(steps=1):
    return pltpu.CompilerParams(
        dimension_semantics=("arbitrary",) * steps, vmem_limit_bytes=VMEM_BYTES
    )


def cost(flops, moved, trans=0):
    return pl.CostEstimate(flops=int(flops), bytes_accessed=int(moved), transcendentals=int(trans))


def row_copies(src, dst, sems, first, parts):
    rows = src.shape[0] // parts
    return [
        pltpu.make_async_copy(
            src.at[pl.ds(i * rows, rows)], dst.at[pl.ds(i * rows, rows)], sems.at[first + i]
        )
        for i in range(parts)
    ]


def mix_first(factor, blocked):
    block, channels = factor.shape[0], blocked.shape[1]
    tiles = 4
    step = block // tiles

    def body(f_hbm, x_hbm, u_hbm, f_all, x_all, u_all, sems):
        xs = row_copies(x_hbm, x_all, sems, 0, tiles)
        fs = row_copies(f_hbm, f_all, sems, tiles, tiles)
        us = row_copies(u_all, u_hbm, sems, 2 * tiles, tiles)
        for c in xs + fs:
            c.start()
        for c in xs:
            c.wait()
        for t in range(tiles):
            fs[t].wait()
            at = slice(t * step, (t + 1) * step)
            u_all[at, :] = dot(f_all[at, :], x_all[...], 1, 0).astype(BF)
            us[t].start()
        for c in us:
            c.wait()

    return pl.pallas_call(
        body,
        in_specs=[ANY, ANY],
        out_specs=ANY,
        out_shape=pltpu.HBM((block, channels), BF),
        scratch_shapes=[
            pltpu.VMEM((block, block), BF),
            pltpu.VMEM((block, channels), BF),
            pltpu.VMEM((block, channels), BF),
            pltpu.SemaphoreType.DMA((3 * tiles,)),
        ],
        compiler_params=params(0),
        cost_estimate=cost(2 * block * block * channels, 2 * block * (block + 2 * channels)),
        name="mix_first",
    )(in_hbm(factor), in_hbm(blocked))


def spread_factor(factor_two):
    here, n, _ = factor_two.shape
    groups = here // 16
    wide = n * 16
    turned = factor_two.reshape(groups, 16, n, n).transpose(0, 2, 1, 3).reshape(groups, wide, n)

    def body(in_ref, out_ref):
        col = lax.broadcasted_iota(jnp.int32, (n, wide), 1)
        row = lax.broadcasted_iota(jnp.int32, (n, wide), 0)
        pick = jnp.where(col // 16 == row, 1.0, 0.0).astype(BF)
        r = lax.broadcasted_iota(jnp.int32, (wide, wide), 0)
        c = lax.broadcasted_iota(jnp.int32, (wide, wide), 1)
        same = r % 16 == c % 16
        full = dot(in_ref[0], pick, 1, 0)
        out_ref[0] = jnp.where(same, full, 0.0).astype(BF)

    return pl.pallas_call(
        body,
        grid=(groups,),
        in_specs=[pl.BlockSpec((1, wide, n), lambda g: (g, 0, 0))],
        out_specs=pl.BlockSpec((1, wide, wide), lambda g: (g, 0, 0)),
        out_shape=jax.ShapeDtypeStruct((groups, wide, wide), BF),
        compiler_params=params(),
        cost_estimate=cost(2 * groups * wide * wide * n, 2 * groups * wide * wide),
        name="spread_factor",
    )(turned)


def mix_second(spread, cols, back):
    n, here, channels = cols.shape
    wide = n * 16
    groups = here // 16

    def body(m_ref, in_ref, out_hbm, out, sems):
        copies = []
        for g in range(groups):
            at = pl.ds(g * 16, 16)
            rows = in_ref[:, at, :].reshape(wide, channels)
            got = dot(m_ref[g], rows, 0 if back else 1, 0).astype(BF)
            out[:, at, :] = got.reshape(n, 16, channels)
            copies.append(
                pltpu.make_async_copy(out.at[:, at, :], out_hbm.at[:, at, :], sems.at[g])
            )
            copies[-1].start()
        for c in copies:
            c.wait()

    return pl.pallas_call(
        body,
        in_specs=[VMEM, VMEM],
        out_specs=ANY,
        out_shape=pltpu.HBM(cols.shape, BF),
        scratch_shapes=[pltpu.VMEM(cols.shape, BF), pltpu.SemaphoreType.DMA((groups,))],
        compiler_params=params(0),
        cost_estimate=cost(
            2 * groups * wide * wide * channels, 4 * cols.size + 2 * groups * wide * wide
        ),
        name="mix_second_back" if back else "mix_second",
    )(in_vmem(spread), in_vmem(cols))


def grad_second(grads, firsts, scale):
    n, here, channels = grads.shape
    wide = n * 16
    groups = here // 16

    def body(g_ref, u_ref, out_ref):
        r = lax.broadcasted_iota(jnp.int32, (wide, wide), 0)
        c = lax.broadcasted_iota(jnp.int32, (wide, wide), 1)
        same = r % 16 == c % 16
        row = lax.broadcasted_iota(jnp.int32, (wide, n), 0)
        col = lax.broadcasted_iota(jnp.int32, (wide, n), 1)
        pick = jnp.where(row // 16 == col, 1.0, 0.0)
        for k in range(groups):
            at = pl.ds(k * 16, 16)
            g = g_ref[:, at, :].reshape(wide, channels)
            u = u_ref[:, at, :].reshape(wide, channels)
            kept = jnp.where(same, dot(g, u, 1, 1), 0.0)
            out_ref[k] = dot(kept, pick, 1, 0, precision=lax.Precision.HIGHEST) * scale

    out = pl.pallas_call(
        body,
        in_specs=[VMEM, VMEM],
        out_specs=VMEM,
        out_shape=jax.ShapeDtypeStruct((groups, wide, n), F32),
        compiler_params=params(0),
        cost_estimate=cost(2 * groups * wide * wide * channels, 4 * grads.size),
        name="grad_second",
    )(in_vmem(grads), in_vmem(firsts))
    return out.reshape(groups, n, 16, n).transpose(0, 2, 1, 3).reshape(here, n, n)


def middle(half, blocked, incoming, mixed, up_blocks, down_blocks):
    groups, width, inner = up_blocks.shape
    sub = inner // groups
    rows, channels = blocked.shape
    step = min(256, rows)
    tiles = rows // step

    def body(half_ref, x_hbm, g_hbm, v_ref, up_hbm, down_hbm, *refs):
        dv_hbm, r_hbm, kept_hbm, sent_hbm = refs[:4]
        x_ref, g_ref, up_ref, down_ref, dv, r_ref, w, halves, sems = refs[4:]

        def rows_copy(src, dst, kind, t):
            at = pl.ds(t * step, step)
            return pltpu.make_async_copy(src.at[at], dst.at[at], sems.at[kind * tiles + t])

        def whole_copy(src, dst, number):
            return pltpu.make_async_copy(src, dst, sems.at[4 * tiles + number])

        fetch_up = whole_copy(up_hbm, up_ref, 0)
        fetch_down = whole_copy(down_hbm, down_ref, 1)
        rows_copy(x_hbm, x_ref, 0, 0).start()
        fetch_up.start()
        rows_copy(g_hbm, g_ref, 1, 0).start()
        fetch_down.start()
        for t in range(1, tiles):
            rows_copy(x_hbm, x_ref, 0, t).start()
            rows_copy(g_hbm, g_ref, 1, t).start()
        w[...] = jnp.zeros_like(w)
        fetch_up.wait()
        fetch_down.wait()

        def tile(t, carry):
            rows_copy(x_hbm, x_ref, 0, t).wait()
            rows_copy(g_hbm, g_ref, 1, t).wait()
            at = pl.ds(pl.multiple_of(t * step, step), step)
            x = x_ref[at, :].astype(F32)
            g = g_ref[at, :]
            v = v_ref[at, :].astype(F32)
            sx = sigmoid(x)
            gate = x * sx
            h = (x + v * gate).astype(BF)
            h_parts = [h[:, b * width : (b + 1) * width] for b in range(groups)]
            g_parts = [g[:, b * width : (b + 1) * width] for b in range(groups)]
            acts, slopes, back = [], [], []
            for b in range(groups):
                a = dot(h_parts[b], up_ref[b], 1, 0).astype(BF)
                s = sigmoid(a)
                q = a * s
                acts.append(q)
                slopes.append(s + q * (1 - s))
                back.append(dot(g_parts[b], down_ref[b], 1, 1).astype(BF))
            grads = []
            for b in range(groups):
                lanes = slice(b * sub, (b + 1) * sub)
                perm = jnp.concatenate([acts[p][:, lanes] for p in range(groups)], axis=1)
                w[1, b] += dot(g_parts[b], perm, 0, 0)
                dq = jnp.concatenate([back[p][:, lanes] for p in range(groups)], axis=1)
                da = dq * slopes[b]
                w[0, b] += dot(h_parts[b], da, 0, 0)
                grads.append(dot(da, up_ref[b], 1, 1))
            dh = (g.astype(F32) + jnp.concatenate(grads, axis=1)).astype(BF).astype(F32)
            dv[at, :] = (dh * gate).astype(BF)
            rows_copy(dv, dv_hbm, 2, t).start()
            r_ref[at, :] = (dh * (1.0 + v * (sx + gate * (1.0 - sx)))).astype(BF)
            rows_copy(r_ref, r_hbm, 3, t).start()
            return carry

        lax.fori_loop(0, tiles, tile, 0)
        halves[1] = w[1 - half_ref[0]].astype(BF)
        send = whole_copy(halves.at[1], sent_hbm, 2)
        send.start()
        halves[0] = w[half_ref[0]].astype(BF)
        keep = whole_copy(halves.at[0], kept_hbm, 3)
        keep.start()
        for t in range(tiles):
            rows_copy(dv, dv_hbm, 2, t).wait()
            rows_copy(r_ref, r_hbm, 3, t).wait()
        send.wait()
        keep.wait()

    hidden = rows * groups * inner
    return pl.pallas_call(
        body,
        in_specs=[SCALAR, ANY, ANY, VMEM, ANY, ANY],
        out_specs=[ANY] * 4,
        out_shape=[
            pltpu.HBM((rows, channels), BF),
            pltpu.HBM((rows, channels), BF),
            pltpu.HBM(up_blocks.shape, BF),
            pltpu.HBM(up_blocks.shape, BF),
        ],
        scratch_shapes=[
            pltpu.VMEM((rows, channels), BF),
            pltpu.VMEM((rows, channels), BF),
            pltpu.VMEM(up_blocks.shape, BF),
            pltpu.VMEM(down_blocks.shape, BF),
            pltpu.VMEM((rows, channels), BF),
            pltpu.VMEM((rows, channels), BF),
            pltpu.VMEM((2, groups, width, inner), F32),
            pltpu.VMEM((2, groups, width, inner), BF),
            pltpu.SemaphoreType.DMA((4 * tiles + 4,)),
        ],
        compiler_params=params(0),
        cost_estimate=cost(
            10 * hidden * width, 10 * rows * channels + 8 * groups * width * inner, hidden
        ),
        name="middle",
    )(half, in_hbm(blocked), in_hbm(incoming), in_vmem(mixed), in_hbm(up_blocks), in_hbm(down_blocks))


def finish(factor, grad_first, blocked, gate_grad, scale):
    block, channels = blocked.shape
    tiles = 4
    step = block // tiles

    def body(f_hbm, d_hbm, x_hbm, r_hbm, one_hbm, out_hbm, f, d, x, r, one, out, sems):
        ds = row_copies(d_hbm, d, sems, 0, tiles)
        xs = row_copies(x_hbm, x, sems, tiles, tiles)
        fs = row_copies(f_hbm, f, sems, 2 * tiles, tiles)
        rs = row_copies(r_hbm, r, sems, 3 * tiles, tiles)
        ones = row_copies(one, one_hbm, sems, 4 * tiles, tiles)
        outs = row_copies(out, out_hbm, sems, 5 * tiles, tiles)
        for c in xs + ds + fs + rs:
            c.start()
        for c in xs:
            c.wait()
        for t in range(tiles):
            at = slice(t * step, (t + 1) * step)
            ds[t].wait()
            one[at, :] = dot(d[at, :], x[...], 1, 1) * scale
            ones[t].start()
        for c in fs:
            c.wait()
        for t in range(tiles):
            at = slice(t * step, (t + 1) * step)
            rs[t].wait()
            total = dot(f[:, at], d[...], 0, 0) + r[at, :].astype(F32)
            out[at, :] = total.astype(BF)
            outs[t].start()
        for c in ones + outs:
            c.wait()

    return pl.pallas_call(
        body,
        in_specs=[ANY] * 4,
        out_specs=[ANY] * 2,
        out_shape=[pltpu.HBM((block, block), F32), pltpu.HBM((block, channels), BF)],
        scratch_shapes=[
            pltpu.VMEM((block, block), BF),
            pltpu.VMEM((block, channels), BF),
            pltpu.VMEM((block, channels), BF),
            pltpu.VMEM((block, channels), BF),
            pltpu.VMEM((block, block), F32),
            pltpu.VMEM((block, channels), BF),
            pltpu.SemaphoreType.DMA((6 * tiles,)),
        ],
        compiler_params=params(0),
        cost_estimate=cost(4 * block * block * channels, 6 * block * block + 8 * block * channels),
        name="finish",
    )(in_hbm(factor), in_hbm(grad_first), in_hbm(blocked), in_hbm(gate_grad))


def radices(count):
    steps, stride = [], 1
    while stride < count:
        radix = 4 if stride >= 4 and count // stride == 4 else 2
        steps.append((stride, radix))
        stride *= radix
    return steps


def swap(values, count, stride, s):
    return lax.ppermute(values, "seq", [(i, i ^ (stride * s)) for i in range(count)])


def add_and_cut(terms, digit, radix):
    rows, columns = terms[0].shape
    share = rows // radix

    number = len(terms)

    number = len(terms)
    shape = (radix, share, columns)

    def body(digit_ref, *refs):
        ins, outs = refs[:number], refs[number : number + radix]
        held, made, sems = refs[number + radix : -radix - 1], refs[-radix - 1 : -1], refs[-1]
        copies = [pltpu.make_async_copy(ins[i], held[i], sems.at[i]) for i in range(number)]
        for c in copies:
            c.start()
        for c in copies:
            c.wait()
        copies = []
        for s, ref in enumerate(made):
            total = held[0][digit_ref[0] ^ s].astype(F32)
            for term in held[1:]:
                total = total + term[digit_ref[0] ^ s].astype(F32)
            ref[...] = total.astype(ref.dtype)
            copies.append(pltpu.make_async_copy(ref, outs[s], sems.at[number + s]))
            copies[-1].start()
        for c in copies:
            c.wait()

    types = [F32] + [BF] * (radix - 1)
    return pl.pallas_call(
        body,
        in_specs=[SCALAR] + [ANY] * number,
        out_specs=[ANY] * radix,
        out_shape=[pltpu.HBM((share, columns), t) for t in types],
        scratch_shapes=[pltpu.VMEM(shape, t.dtype) for t in terms]
        + [pltpu.VMEM((share, columns), t) for t in types]
        + [pltpu.SemaphoreType.DMA((number + radix,))],
        compiler_params=params(0),
        cost_estimate=cost(rows * columns, 8 * rows * columns),
        name="add_and_cut",
    )(digit.reshape(1), *[t.reshape(shape) for t in terms])


def scatter_step(terms, count, stride, radix):
    digit = (lax.axis_index("seq").astype(jnp.int32) // stride) % radix
    kept, *send = add_and_cut(terms, digit, radix)
    return [kept] + [swap(a, count, stride, s + 1) for s, a in enumerate(send)]


def gather_step(share, count, stride, radix, after=()):
    digit = (lax.axis_index("seq") // stride) % radix
    got = [share] + [swap(share, count, stride, s) for s in range(1, radix)]
    got, after = lax.optimization_barrier((got, after))
    if radix == 2:
        low = jnp.where(digit == 0, got[0], got[1])
        high = jnp.where(digit == 0, got[1], got[0])
        return jnp.concatenate([low, high], axis=0)
    whole = jnp.zeros((radix,) + share.shape, share.dtype)
    for s in range(radix):
        owner = digit ^ s
        place = 2 * (owner % 2) + owner // 2
        whole = lax.dynamic_update_index_in_dim(whole, got[s], place, 0)
    return whole.reshape(radix * share.shape[0], share.shape[1])


def write_weights(total, up_shape, down_shape, scale):
    groups, width, inner = up_shape

    def body(up_in, down_in, up_ref, down_ref):
        up_ref[0] = up_in[...].astype(F32) * scale
        down_ref[0] = (down_in[...].astype(F32) * scale).T

    return pl.pallas_call(
        body,
        grid=(groups,),
        in_specs=[
            pl.BlockSpec((width, inner), lambda b: (b, 0)),
            pl.BlockSpec((width, inner), lambda b: (groups + b, 0)),
        ],
        out_specs=[
            pl.BlockSpec((1, width, inner), lambda b: (b, 0, 0)),
            pl.BlockSpec((1, inner, width), lambda b: (b, 0, 0)),
        ],
        out_shape=[
            jax.ShapeDtypeStruct(up_shape, F32),
            jax.ShapeDtypeStruct(down_shape, F32),
        ],
        compiler_params=params(),
        cost_estimate=cost(groups * width * inner, 12 * groups * width * inner),
        name="write_weights",
    )(total, total)


def on_device(tokens, cotangent, factor_one, factor_two, up_blocks, down_blocks):
    count = lax.axis_size("seq")
    block, channels = factor_one.shape[1], tokens.shape[1]
    here = block // count
    scale = float(count * tokens.shape[0]) ** (-0.5)
    factor = factor_one.reshape(block, block)
    grouped = here % 16 == 0

    def exchange(values):
        cut = values.reshape(count, here, channels)
        return lax.all_to_all(cut, "seq", split_axis=0, concat_axis=0, tiled=True)

    if grouped:
        spread = spread_factor(factor_two)

    def second(cols, back):
        if grouped:
            return mix_second(spread, cols, back)
        names = "kmj,mkc->jkc" if back else "kmj,jkc->mkc"
        return jnp.einsum(names, factor_two, cols, preferred_element_type=F32).astype(BF)

    def second_grad(grads, firsts):
        if grouped:
            return grad_second(grads, firsts, scale)
        return jnp.einsum("mkc,jkc->kmj", grads, firsts, preferred_element_type=F32) * scale

    half = (lax.axis_index("seq") % 2).astype(jnp.int32).reshape(1)
    firsts = exchange(mix_first(factor, tokens))
    mixed = exchange(second(firsts, False)).reshape(block, channels)
    dv, gate_grad, kept, sent = middle(half, tokens, cotangent, mixed, up_blocks, down_blocks)
    grad_mixed = exchange(dv)
    back = second(grad_mixed, True)
    terms = [kept, swap(sent, count, 1, 1)]
    terms = [t.reshape(-1, t.shape[-1]) for t in terms]
    steps = radices(count)
    for stride, radix in steps[1:]:
        terms = scatter_step(terms, count, stride, 2)
        if radix == 4:
            terms = scatter_step(terms, count, 2 * stride, 2)
    terms, back = lax.optimization_barrier((terms, back))
    total = sum(t.astype(F32) for t in terms).astype(BF)
    back, total = lax.optimization_barrier((back, total))
    grad_first = exchange(back).reshape(block, channels)
    two = second_grad(grad_mixed, firsts)
    for step in reversed(steps):
        total = gather_step(total, count, *step, after=two if step == steps[1] else ())
    grad_up, grad_down = write_weights(total, up_blocks.shape, down_blocks.shape, scale)
    one, grad_tokens = finish(factor, grad_first, tokens, gate_grad, scale)
    return (grad_tokens, one.reshape(1, block, block), two, grad_up, grad_down)


def solution(mesh):
    return jax.shard_map(
        on_device,
        mesh=mesh,
        in_specs=(
            P(("grp", "seq"), None),
            P(("grp", "seq"), None),
            P("seq", None, None),
            P("seq", None, None),
            P(),
            P(),
        ),
        out_specs=(
            P(("grp", "seq"), None),
            P(("grp", "seq"), None, None),
            P(("grp", "seq"), None, None),
            P("grp", None, None),
            P("grp", None, None),
        ),
        check_vma=False,
    )
```

```python
import jax
import jax.numpy as jnp
from jax import lax
from jax.experimental import pallas as pl
from jax.experimental.pallas import tpu as pltpu
from jax.sharding import PartitionSpec as P

BF = jnp.bfloat16
F32 = jnp.float32
VMEM_BYTES = 40 * 1024 * 1024
ANY = pl.BlockSpec(memory_space=pl.ANY)
VMEM = pl.BlockSpec(memory_space=pltpu.VMEM)
SCALAR = pl.BlockSpec(memory_space=pltpu.SMEM)


def in_hbm(array):
    return pltpu.with_memory_space_constraint(array, pltpu.HBM)


def in_vmem(array):
    return pltpu.with_memory_space_constraint(array, pltpu.VMEM)


def sigmoid(z):
    return 0.5 + 0.5 * jnp.tanh(0.5 * z)


def dot(a, b, ca, cb, **kw):
    return lax.dot_general(a, b, (((ca,), (cb,)), ((), ())), preferred_element_type=F32, **kw)


def params(steps=1):
    return pltpu.CompilerParams(
        dimension_semantics=("arbitrary",) * steps, vmem_limit_bytes=VMEM_BYTES
    )


def cost(flops, moved, trans=0):
    return pl.CostEstimate(flops=int(flops), bytes_accessed=int(moved), transcendentals=int(trans))


def row_copies(src, dst, sems, first, parts):
    rows = src.shape[0] // parts
    return [
        pltpu.make_async_copy(
            src.at[pl.ds(i * rows, rows)], dst.at[pl.ds(i * rows, rows)], sems.at[first + i]
        )
        for i in range(parts)
    ]


def mix_first(factor, blocked):
    block, channels = factor.shape[0], blocked.shape[1]
    tiles = 4
    step = block // tiles

    def body(f_hbm, x_hbm, u_hbm, f_all, x_all, u_all, sems):
        xs = row_copies(x_hbm, x_all, sems, 0, tiles)
        fs = row_copies(f_hbm, f_all, sems, tiles, tiles)
        us = row_copies(u_all, u_hbm, sems, 2 * tiles, tiles)
        for c in xs + fs:
            c.start()
        for c in xs:
            c.wait()
        for t in range(tiles):
            fs[t].wait()
            at = slice(t * step, (t + 1) * step)
            u_all[at, :] = dot(f_all[at, :], x_all[...], 1, 0).astype(BF)
            us[t].start()
        for c in us:
            c.wait()

    return pl.pallas_call(
        body,
        in_specs=[ANY, ANY],
        out_specs=ANY,
        out_shape=pltpu.HBM((block, channels), BF),
        scratch_shapes=[
            pltpu.VMEM((block, block), BF),
            pltpu.VMEM((block, channels), BF),
            pltpu.VMEM((block, channels), BF),
            pltpu.SemaphoreType.DMA((3 * tiles,)),
        ],
        compiler_params=params(0),
        cost_estimate=cost(2 * block * block * channels, 2 * block * (block + 2 * channels)),
        name="mix_first",
    )(in_hbm(factor), in_hbm(blocked))


def spread_factor(factor_two):
    here, n, _ = factor_two.shape
    groups = here // 16
    wide = n * 16
    turned = factor_two.reshape(groups, 16, n, n).transpose(0, 2, 1, 3).reshape(groups, wide, n)

    def body(in_ref, out_ref):
        col = lax.broadcasted_iota(jnp.int32, (n, wide), 1)
        row = lax.broadcasted_iota(jnp.int32, (n, wide), 0)
        pick = jnp.where(col // 16 == row, 1.0, 0.0).astype(BF)
        r = lax.broadcasted_iota(jnp.int32, (wide, wide), 0)
        c = lax.broadcasted_iota(jnp.int32, (wide, wide), 1)
        same = r % 16 == c % 16
        full = dot(in_ref[0], pick, 1, 0)
        out_ref[0] = jnp.where(same, full, 0.0).astype(BF)

    return pl.pallas_call(
        body,
        grid=(groups,),
        in_specs=[pl.BlockSpec((1, wide, n), lambda g: (g, 0, 0))],
        out_specs=pl.BlockSpec((1, wide, wide), lambda g: (g, 0, 0)),
        out_shape=jax.ShapeDtypeStruct((groups, wide, wide), BF),
        compiler_params=params(),
        cost_estimate=cost(2 * groups * wide * wide * n, 2 * groups * wide * wide),
        name="spread_factor",
    )(turned)


def mix_second(spread, cols, back):
    n, here, channels = cols.shape
    wide = n * 16
    groups = here // 16

    def body(m_ref, in_ref, out_hbm, out, sems):
        copies = []
        for g in range(groups):
            at = pl.ds(g * 16, 16)
            rows = in_ref[:, at, :].reshape(wide, channels)
            got = dot(m_ref[g], rows, 0 if back else 1, 0).astype(BF)
            out[:, at, :] = got.reshape(n, 16, channels)
            copies.append(
                pltpu.make_async_copy(out.at[:, at, :], out_hbm.at[:, at, :], sems.at[g])
            )
            copies[-1].start()
        for c in copies:
            c.wait()

    return pl.pallas_call(
        body,
        in_specs=[VMEM, VMEM],
        out_specs=ANY,
        out_shape=pltpu.HBM(cols.shape, BF),
        scratch_shapes=[pltpu.VMEM(cols.shape, BF), pltpu.SemaphoreType.DMA((groups,))],
        compiler_params=params(0),
        cost_estimate=cost(
            2 * groups * wide * wide * channels, 4 * cols.size + 2 * groups * wide * wide
        ),
        name="mix_second_back" if back else "mix_second",
    )(in_vmem(spread), in_vmem(cols))


def grad_second(grads, firsts, scale):
    n, here, channels = grads.shape
    wide = n * 16
    groups = here // 16

    def body(g_ref, u_ref, out_ref):
        r = lax.broadcasted_iota(jnp.int32, (wide, wide), 0)
        c = lax.broadcasted_iota(jnp.int32, (wide, wide), 1)
        same = r % 16 == c % 16
        row = lax.broadcasted_iota(jnp.int32, (wide, n), 0)
        col = lax.broadcasted_iota(jnp.int32, (wide, n), 1)
        pick = jnp.where(row // 16 == col, 1.0, 0.0)
        for k in range(groups):
            at = pl.ds(k * 16, 16)
            g = g_ref[:, at, :].reshape(wide, channels)
            u = u_ref[:, at, :].reshape(wide, channels)
            kept = jnp.where(same, dot(g, u, 1, 1), 0.0)
            out_ref[k] = dot(kept, pick, 1, 0, precision=lax.Precision.HIGHEST) * scale

    out = pl.pallas_call(
        body,
        in_specs=[VMEM, VMEM],
        out_specs=VMEM,
        out_shape=jax.ShapeDtypeStruct((groups, wide, n), F32),
        compiler_params=params(0),
        cost_estimate=cost(2 * groups * wide * wide * channels, 4 * grads.size),
        name="grad_second",
    )(in_vmem(grads), in_vmem(firsts))
    return out.reshape(groups, n, 16, n).transpose(0, 2, 1, 3).reshape(here, n, n)


def pull_back(incoming, down_blocks):
    rows, channels = incoming.shape
    groups, inner, width = down_blocks.shape
    sub = inner // groups
    step = min(256, rows)

    def body(g_ref, down_ref, out_ref):
        for p in range(groups):
            back = dot(g_ref[:, p * width : (p + 1) * width], down_ref[p], 1, 1).astype(BF)
            for b in range(groups):
                at = b * inner + p * sub
                out_ref[:, at : at + sub] = back[:, b * sub : (b + 1) * sub]

    return pl.pallas_call(
        body,
        grid=(rows // step,),
        in_specs=[
            pl.BlockSpec((step, channels), lambda i: (i, 0)),
            pl.BlockSpec(down_blocks.shape, lambda i: (0, 0, 0)),
        ],
        out_specs=pl.BlockSpec((step, groups * inner), lambda i: (i, 0)),
        out_shape=pltpu.HBM((rows, groups * inner), BF),
        compiler_params=params(),
        cost_estimate=cost(2 * rows * groups * inner * width, 2 * rows * groups * inner),
        name="pull_back",
    )(in_hbm(incoming), in_hbm(down_blocks))


def middle(half, blocked, incoming, mixed, up_blocks, pulled):
    groups, width, inner = up_blocks.shape
    sub = inner // groups
    rows, channels = blocked.shape
    step = min(256, rows)
    tiles = rows // step

    def body(half_ref, x_hbm, g_hbm, v_ref, up_hbm, dq_hbm, *refs):
        dv_hbm, r_hbm, kept_hbm, sent_hbm = refs[:4]
        x_ref, g_ref, up_ref, dq_ref, dv, r_ref, w, halves, sems = refs[4:]

        def rows_copy(src, dst, kind, t):
            at = pl.ds(t * step, step)
            return pltpu.make_async_copy(src.at[at], dst.at[at], sems.at[kind * tiles + t])

        def whole_copy(src, dst, number):
            return pltpu.make_async_copy(src, dst, sems.at[5 * tiles + number])

        fetch_up = whole_copy(up_hbm, up_ref, 0)
        rows_copy(x_hbm, x_ref, 0, 0).start()
        fetch_up.start()
        rows_copy(g_hbm, g_ref, 1, 0).start()
        rows_copy(dq_hbm, dq_ref, 4, 0).start()
        for t in range(1, tiles):
            rows_copy(x_hbm, x_ref, 0, t).start()
            rows_copy(g_hbm, g_ref, 1, t).start()
            rows_copy(dq_hbm, dq_ref, 4, t).start()
        w[...] = jnp.zeros_like(w)
        fetch_up.wait()

        def tile(t, carry):
            rows_copy(x_hbm, x_ref, 0, t).wait()
            rows_copy(g_hbm, g_ref, 1, t).wait()
            at = pl.ds(pl.multiple_of(t * step, step), step)
            x = x_ref[at, :].astype(F32)
            g = g_ref[at, :]
            v = v_ref[at, :].astype(F32)
            sx = sigmoid(x)
            gate = x * sx
            h = (x + v * gate).astype(BF)
            h_parts = [h[:, b * width : (b + 1) * width] for b in range(groups)]
            g_parts = [g[:, b * width : (b + 1) * width] for b in range(groups)]
            acts, slopes = [], []
            for b in range(groups):
                a = dot(h_parts[b], up_ref[b], 1, 0).astype(BF)
                s = sigmoid(a)
                q = a * s
                acts.append(q)
                slopes.append(s + q * (1 - s))
            rows_copy(dq_hbm, dq_ref, 4, t).wait()
            grads = []
            for b in range(groups):
                lanes = slice(b * sub, (b + 1) * sub)
                perm = jnp.concatenate([acts[p][:, lanes] for p in range(groups)], axis=1)
                w[1, b] += dot(g_parts[b], perm, 0, 0)
                dq = dq_ref[at, b * inner : (b + 1) * inner]
                da = dq * slopes[b]
                w[0, b] += dot(h_parts[b], da, 0, 0)
                grads.append(dot(da, up_ref[b], 1, 1))
            dh = (g.astype(F32) + jnp.concatenate(grads, axis=1)).astype(BF).astype(F32)
            dv[at, :] = (dh * gate).astype(BF)
            rows_copy(dv, dv_hbm, 2, t).start()
            r_ref[at, :] = (dh * (1.0 + v * (sx + gate * (1.0 - sx)))).astype(BF)
            rows_copy(r_ref, r_hbm, 3, t).start()
            return carry

        lax.fori_loop(0, tiles, tile, 0)
        halves[1] = w[1 - half_ref[0]].astype(BF)
        send = whole_copy(halves.at[1], sent_hbm, 2)
        send.start()
        halves[0] = w[half_ref[0]].astype(BF)
        keep = whole_copy(halves.at[0], kept_hbm, 3)
        keep.start()
        for t in range(tiles):
            rows_copy(dv, dv_hbm, 2, t).wait()
            rows_copy(r_ref, r_hbm, 3, t).wait()
        send.wait()
        keep.wait()

    hidden = rows * groups * inner
    return pl.pallas_call(
        body,
        in_specs=[SCALAR, ANY, ANY, VMEM, ANY, ANY],
        out_specs=[ANY] * 4,
        out_shape=[
            pltpu.HBM((rows, channels), BF),
            pltpu.HBM((rows, channels), BF),
            pltpu.HBM(up_blocks.shape, BF),
            pltpu.HBM(up_blocks.shape, BF),
        ],
        scratch_shapes=[
            pltpu.VMEM((rows, channels), BF),
            pltpu.VMEM((rows, channels), BF),
            pltpu.VMEM(up_blocks.shape, BF),
            pltpu.VMEM(pulled.shape, BF),
            pltpu.VMEM((rows, channels), BF),
            pltpu.VMEM((rows, channels), BF),
            pltpu.VMEM((2, groups, width, inner), F32),
            pltpu.VMEM((2, groups, width, inner), BF),
            pltpu.SemaphoreType.DMA((5 * tiles + 4,)),
        ],
        compiler_params=params(0),
        cost_estimate=cost(
            10 * hidden * width, 10 * rows * channels + 8 * groups * width * inner, hidden
        ),
        name="middle",
    )(half, in_hbm(blocked), in_hbm(incoming), in_vmem(mixed), in_hbm(up_blocks), in_hbm(pulled))


def finish(factor, grad_first, blocked, gate_grad, scale):
    block, channels = blocked.shape
    tiles = 4
    step = block // tiles

    def body(f_hbm, d_hbm, x_hbm, r_hbm, one_hbm, out_hbm, f, d, x, r, one, out, sems):
        ds = row_copies(d_hbm, d, sems, 0, tiles)
        xs = row_copies(x_hbm, x, sems, tiles, tiles)
        fs = row_copies(f_hbm, f, sems, 2 * tiles, tiles)
        rs = row_copies(r_hbm, r, sems, 3 * tiles, tiles)
        ones = row_copies(one, one_hbm, sems, 4 * tiles, tiles)
        outs = row_copies(out, out_hbm, sems, 5 * tiles, tiles)
        for c in ds + xs + fs + rs:
            c.start()
        for c in xs:
            c.wait()
        for t in range(tiles):
            at = slice(t * step, (t + 1) * step)
            ds[t].wait()
            one[at, :] = dot(d[at, :], x[...], 1, 1) * scale
            ones[t].start()
        for c in fs:
            c.wait()
        for t in range(tiles):
            at = slice(t * step, (t + 1) * step)
            rs[t].wait()
            total = dot(f[:, at], d[...], 0, 0) + r[at, :].astype(F32)
            out[at, :] = total.astype(BF)
            outs[t].start()
        for c in ones + outs:
            c.wait()

    return pl.pallas_call(
        body,
        in_specs=[ANY] * 4,
        out_specs=[ANY] * 2,
        out_shape=[pltpu.HBM((block, block), F32), pltpu.HBM((block, channels), BF)],
        scratch_shapes=[
            pltpu.VMEM((block, block), BF),
            pltpu.VMEM((block, channels), BF),
            pltpu.VMEM((block, channels), BF),
            pltpu.VMEM((block, channels), BF),
            pltpu.VMEM((block, block), F32),
            pltpu.VMEM((block, channels), BF),
            pltpu.SemaphoreType.DMA((6 * tiles,)),
        ],
        compiler_params=params(0),
        cost_estimate=cost(4 * block * block * channels, 6 * block * block + 8 * block * channels),
        name="finish",
    )(in_hbm(factor), in_hbm(grad_first), in_hbm(blocked), in_hbm(gate_grad))


def radices(count):
    steps, stride = [], 1
    while stride < count:
        radix = 4 if stride >= 4 and count // stride == 4 else 2
        steps.append((stride, radix))
        stride *= radix
    return steps


def swap(values, count, stride, s):
    return lax.ppermute(values, "seq", [(i, i ^ (stride * s)) for i in range(count)])


def add_and_cut(terms, digit, radix):
    rows, columns = terms[0].shape
    share = rows // radix

    number = len(terms)

    number = len(terms)
    shape = (radix, share, columns)

    def body(digit_ref, *refs):
        ins, outs = refs[:number], refs[number : number + radix]
        held, made, sems = refs[number + radix : -radix - 1], refs[-radix - 1 : -1], refs[-1]
        copies = [pltpu.make_async_copy(ins[i], held[i], sems.at[i]) for i in range(number)]
        for c in copies:
            c.start()
        for c in copies:
            c.wait()
        copies = []
        for s, ref in enumerate(made):
            total = held[0][digit_ref[0] ^ s].astype(F32)
            for term in held[1:]:
                total = total + term[digit_ref[0] ^ s].astype(F32)
            ref[...] = total.astype(ref.dtype)
            copies.append(pltpu.make_async_copy(ref, outs[s], sems.at[number + s]))
            copies[-1].start()
        for c in copies:
            c.wait()

    types = [F32] + [BF] * (radix - 1)
    return pl.pallas_call(
        body,
        in_specs=[SCALAR] + [ANY] * number,
        out_specs=[ANY] * radix,
        out_shape=[pltpu.HBM((share, columns), t) for t in types],
        scratch_shapes=[pltpu.VMEM(shape, t.dtype) for t in terms]
        + [pltpu.VMEM((share, columns), t) for t in types]
        + [pltpu.SemaphoreType.DMA((number + radix,))],
        compiler_params=params(0),
        cost_estimate=cost(rows * columns, 8 * rows * columns),
        name="add_and_cut",
    )(digit.reshape(1), *[t.reshape(shape) for t in terms])


def scatter_step(terms, count, stride, radix):
    digit = (lax.axis_index("seq").astype(jnp.int32) // stride) % radix
    kept, *send = add_and_cut(terms, digit, radix)
    return [kept] + [swap(a, count, stride, s + 1) for s, a in enumerate(send)]


def gather_step(share, count, stride, radix, after=()):
    digit = (lax.axis_index("seq") // stride) % radix
    got = [share] + [swap(share, count, stride, s) for s in range(1, radix)]
    got, after = lax.optimization_barrier((got, after))
    if radix == 2:
        low = jnp.where(digit == 0, got[0], got[1])
        high = jnp.where(digit == 0, got[1], got[0])
        return jnp.concatenate([low, high], axis=0)
    whole = jnp.zeros((radix,) + share.shape, share.dtype)
    for s in range(radix):
        whole = lax.dynamic_update_index_in_dim(whole, got[s], digit ^ s, 0)
    return whole.reshape(radix * share.shape[0], share.shape[1])


def write_weights(total, up_shape, down_shape, scale):
    groups, width, inner = up_shape

    def body(up_in, down_in, up_ref, down_ref):
        up_ref[0] = up_in[...].astype(F32) * scale
        down_ref[0] = (down_in[...].astype(F32) * scale).T

    return pl.pallas_call(
        body,
        grid=(groups,),
        in_specs=[
            pl.BlockSpec((width, inner), lambda b: (b, 0)),
            pl.BlockSpec((width, inner), lambda b: (groups + b, 0)),
        ],
        out_specs=[
            pl.BlockSpec((1, width, inner), lambda b: (b, 0, 0)),
            pl.BlockSpec((1, inner, width), lambda b: (b, 0, 0)),
        ],
        out_shape=[
            jax.ShapeDtypeStruct(up_shape, F32),
            jax.ShapeDtypeStruct(down_shape, F32),
        ],
        compiler_params=params(),
        cost_estimate=cost(groups * width * inner, 12 * groups * width * inner),
        name="write_weights",
    )(total, total)


def on_device(tokens, cotangent, factor_one, factor_two, up_blocks, down_blocks):
    count = lax.axis_size("seq")
    block, channels = factor_one.shape[1], tokens.shape[1]
    here = block // count
    scale = float(count * tokens.shape[0]) ** (-0.5)
    factor = factor_one.reshape(block, block)
    grouped = here % 16 == 0

    def exchange(values):
        cut = values.reshape(count, here, channels)
        return lax.all_to_all(cut, "seq", split_axis=0, concat_axis=0, tiled=True)

    if grouped:
        spread = spread_factor(factor_two)

    def second(cols, back):
        if grouped:
            return mix_second(spread, cols, back)
        names = "kmj,mkc->jkc" if back else "kmj,jkc->mkc"
        return jnp.einsum(names, factor_two, cols, preferred_element_type=F32).astype(BF)

    def second_grad(grads, firsts):
        if grouped:
            return grad_second(grads, firsts, scale)
        return jnp.einsum("mkc,jkc->kmj", grads, firsts, preferred_element_type=F32) * scale

    half = (lax.axis_index("seq") % 2).astype(jnp.int32).reshape(1)
    firsts = exchange(mix_first(factor, tokens))
    mixed = exchange(second(firsts, False)).reshape(block, channels)
    late = (cotangent, down_blocks)
    firsts, late = lax.optimization_barrier((firsts, late))
    pulled = pull_back(*late)
    dv, gate_grad, kept, sent = middle(half, tokens, cotangent, mixed, up_blocks, pulled)
    grad_mixed = exchange(dv)
    back = second(grad_mixed, True)
    terms = [kept, swap(sent, count, 1, 1)]
    terms = [t.reshape(-1, t.shape[-1]) for t in terms]
    steps = radices(count)
    for step in steps[1:]:
        terms = scatter_step(terms, count, *step)
    terms, back = lax.optimization_barrier((terms, back))
    total = sum(t.astype(F32) for t in terms).astype(BF)
    back, total = lax.optimization_barrier((back, total))
    grad_first = exchange(back).reshape(block, channels)
    two = second_grad(grad_mixed, firsts)
    for step in reversed(steps):
        total = gather_step(total, count, *step, after=two if step == steps[1] else ())
    grad_up, grad_down = write_weights(total, up_blocks.shape, down_blocks.shape, scale)
    one, grad_tokens = finish(factor, grad_first, tokens, gate_grad, scale)
    return (grad_tokens, one.reshape(1, block, block), two, grad_up, grad_down)


def solution(mesh):
    return jax.shard_map(
        on_device,
        mesh=mesh,
        in_specs=(
            P(("grp", "seq"), None),
            P(("grp", "seq"), None),
            P("seq", None, None),
            P("seq", None, None),
            P(),
            P(),
        ),
        out_specs=(
            P(("grp", "seq"), None),
            P(("grp", "seq"), None, None),
            P(("grp", "seq"), None, None),
            P("grp", None, None),
            P("grp", None, None),
        ),
        check_vma=False,
    )
```

```python
import jax
import jax.numpy as jnp
from jax import lax
from jax.experimental import pallas as pl
from jax.experimental.pallas import tpu as pltpu
from jax.sharding import PartitionSpec as P

BF = jnp.bfloat16
F32 = jnp.float32
VMEM_BYTES = 40 * 1024 * 1024
ANY = pl.BlockSpec(memory_space=pl.ANY)
VMEM = pl.BlockSpec(memory_space=pltpu.VMEM)
SCALAR = pl.BlockSpec(memory_space=pltpu.SMEM)


def in_hbm(array):
    return pltpu.with_memory_space_constraint(array, pltpu.HBM)


def in_vmem(array):
    return pltpu.with_memory_space_constraint(array, pltpu.VMEM)


def sigmoid(z):
    return 0.5 + 0.5 * jnp.tanh(0.5 * z)


def dot(a, b, ca, cb, **kw):
    return lax.dot_general(a, b, (((ca,), (cb,)), ((), ())), preferred_element_type=F32, **kw)


def params(steps=1):
    return pltpu.CompilerParams(
        dimension_semantics=("arbitrary",) * steps, vmem_limit_bytes=VMEM_BYTES
    )


def cost(flops, moved, trans=0):
    return pl.CostEstimate(flops=int(flops), bytes_accessed=int(moved), transcendentals=int(trans))


def row_copies(src, dst, sems, first, parts):
    rows = src.shape[0] // parts
    return [
        pltpu.make_async_copy(
            src.at[pl.ds(i * rows, rows)], dst.at[pl.ds(i * rows, rows)], sems.at[first + i]
        )
        for i in range(parts)
    ]


def mix_first(factor, blocked):
    block, channels = factor.shape[0], blocked.shape[1]
    tiles = 4
    step = block // tiles

    def body(f_hbm, x_hbm, u_hbm, f_all, x_all, u_all, sems):
        xs = row_copies(x_hbm, x_all, sems, 0, tiles)
        fs = row_copies(f_hbm, f_all, sems, tiles, tiles)
        us = row_copies(u_all, u_hbm, sems, 2 * tiles, tiles)
        for c in xs + fs:
            c.start()
        for c in xs:
            c.wait()
        for t in range(tiles):
            fs[t].wait()
            at = slice(t * step, (t + 1) * step)
            u_all[at, :] = dot(f_all[at, :], x_all[...], 1, 0).astype(BF)
            us[t].start()
        for c in us:
            c.wait()

    return pl.pallas_call(
        body,
        in_specs=[ANY, ANY],
        out_specs=ANY,
        out_shape=pltpu.HBM((block, channels), BF),
        scratch_shapes=[
            pltpu.VMEM((block, block), BF),
            pltpu.VMEM((block, channels), BF),
            pltpu.VMEM((block, channels), BF),
            pltpu.SemaphoreType.DMA((3 * tiles,)),
        ],
        compiler_params=params(0),
        cost_estimate=cost(2 * block * block * channels, 2 * block * (block + 2 * channels)),
        name="mix_first",
    )(in_hbm(factor), in_hbm(blocked))


def spread_factor(factor_two):
    here, n, _ = factor_two.shape
    groups = here // 16
    wide = n * 16
    turned = factor_two.reshape(groups, 16, n, n).transpose(0, 2, 1, 3).reshape(groups, wide, n)

    def body(in_ref, out_ref):
        col = lax.broadcasted_iota(jnp.int32, (n, wide), 1)
        row = lax.broadcasted_iota(jnp.int32, (n, wide), 0)
        pick = jnp.where(col // 16 == row, 1.0, 0.0).astype(BF)
        r = lax.broadcasted_iota(jnp.int32, (wide, wide), 0)
        c = lax.broadcasted_iota(jnp.int32, (wide, wide), 1)
        same = r % 16 == c % 16
        full = dot(in_ref[0], pick, 1, 0)
        out_ref[0] = jnp.where(same, full, 0.0).astype(BF)

    return pl.pallas_call(
        body,
        grid=(groups,),
        in_specs=[pl.BlockSpec((1, wide, n), lambda g: (g, 0, 0))],
        out_specs=pl.BlockSpec((1, wide, wide), lambda g: (g, 0, 0)),
        out_shape=jax.ShapeDtypeStruct((groups, wide, wide), BF),
        compiler_params=params(),
        cost_estimate=cost(2 * groups * wide * wide * n, 2 * groups * wide * wide),
        name="spread_factor",
    )(turned)


def mix_second(spread, cols, back):
    n, here, channels = cols.shape
    wide = n * 16
    groups = here // 16

    def body(m_ref, in_ref, out_hbm, out, sems):
        copies = []
        for g in range(groups):
            at = pl.ds(g * 16, 16)
            rows = in_ref[:, at, :].reshape(wide, channels)
            got = dot(m_ref[g], rows, 0 if back else 1, 0).astype(BF)
            out[:, at, :] = got.reshape(n, 16, channels)
            copies.append(
                pltpu.make_async_copy(out.at[:, at, :], out_hbm.at[:, at, :], sems.at[g])
            )
            copies[-1].start()
        for c in copies:
            c.wait()

    return pl.pallas_call(
        body,
        in_specs=[VMEM, VMEM],
        out_specs=ANY,
        out_shape=pltpu.HBM(cols.shape, BF),
        scratch_shapes=[pltpu.VMEM(cols.shape, BF), pltpu.SemaphoreType.DMA((groups,))],
        compiler_params=params(0),
        cost_estimate=cost(
            2 * groups * wide * wide * channels, 4 * cols.size + 2 * groups * wide * wide
        ),
        name="mix_second_back" if back else "mix_second",
    )(in_vmem(spread), in_vmem(cols))


def grad_second(grads, firsts, scale):
    n, here, channels = grads.shape
    wide = n * 16
    groups = here // 16

    def body(g_ref, u_ref, out_ref):
        r = lax.broadcasted_iota(jnp.int32, (wide, wide), 0)
        c = lax.broadcasted_iota(jnp.int32, (wide, wide), 1)
        same = r % 16 == c % 16
        row = lax.broadcasted_iota(jnp.int32, (wide, n), 0)
        col = lax.broadcasted_iota(jnp.int32, (wide, n), 1)
        pick = jnp.where(row // 16 == col, 1.0, 0.0)
        for k in range(groups):
            at = pl.ds(k * 16, 16)
            g = g_ref[:, at, :].reshape(wide, channels)
            u = u_ref[:, at, :].reshape(wide, channels)
            kept = jnp.where(same, dot(g, u, 1, 1), 0.0)
            out_ref[k] = dot(kept, pick, 1, 0, precision=lax.Precision.HIGHEST) * scale

    out = pl.pallas_call(
        body,
        in_specs=[VMEM, VMEM],
        out_specs=VMEM,
        out_shape=jax.ShapeDtypeStruct((groups, wide, n), F32),
        compiler_params=params(0),
        cost_estimate=cost(2 * groups * wide * wide * channels, 4 * grads.size),
        name="grad_second",
    )(in_vmem(grads), in_vmem(firsts))
    return out.reshape(groups, n, 16, n).transpose(0, 2, 1, 3).reshape(here, n, n)


def pull_back(incoming, down_blocks):
    rows, channels = incoming.shape
    groups, inner, width = down_blocks.shape
    sub = inner // groups
    step = min(256, rows)

    def body(g_ref, down_ref, out_ref):
        for p in range(groups):
            back = dot(g_ref[:, p * width : (p + 1) * width], down_ref[p], 1, 1).astype(BF)
            for b in range(groups):
                at = b * inner + p * sub
                out_ref[:, at : at + sub] = back[:, b * sub : (b + 1) * sub]

    return pl.pallas_call(
        body,
        grid=(rows // step,),
        in_specs=[
            pl.BlockSpec((step, channels), lambda i: (i, 0)),
            pl.BlockSpec(down_blocks.shape, lambda i: (0, 0, 0)),
        ],
        out_specs=pl.BlockSpec((step, groups * inner), lambda i: (i, 0)),
        out_shape=pltpu.HBM((rows, groups * inner), BF),
        compiler_params=params(),
        cost_estimate=cost(2 * rows * groups * inner * width, 2 * rows * groups * inner),
        name="pull_back",
    )(in_hbm(incoming), in_hbm(down_blocks))


def middle(half, blocked, incoming, mixed, up_blocks, pulled):
    groups, width, inner = up_blocks.shape
    sub = inner // groups
    rows, channels = blocked.shape
    step = min(256, rows)
    tiles = rows // step

    def body(half_ref, x_hbm, g_hbm, v_ref, up_hbm, dq_hbm, *refs):
        dv_hbm, r_hbm, kept_hbm, sent_hbm = refs[:4]
        x_ref, g_ref, up_ref, dq_ref, dv, r_ref, w, halves, sems = refs[4:]

        def rows_copy(src, dst, kind, t):
            at = pl.ds(t * step, step)
            return pltpu.make_async_copy(src.at[at], dst.at[at], sems.at[kind * tiles + t])

        def whole_copy(src, dst, number):
            return pltpu.make_async_copy(src, dst, sems.at[5 * tiles + number])

        fetch_up = whole_copy(up_hbm, up_ref, 0)
        rows_copy(x_hbm, x_ref, 0, 0).start()
        fetch_up.start()
        rows_copy(g_hbm, g_ref, 1, 0).start()
        rows_copy(dq_hbm, dq_ref, 4, 0).start()
        for t in range(1, tiles):
            rows_copy(x_hbm, x_ref, 0, t).start()
            rows_copy(g_hbm, g_ref, 1, t).start()
            rows_copy(dq_hbm, dq_ref, 4, t).start()
        w[...] = jnp.zeros_like(w)
        fetch_up.wait()

        def tile(t, carry):
            rows_copy(x_hbm, x_ref, 0, t).wait()
            rows_copy(g_hbm, g_ref, 1, t).wait()
            at = pl.ds(pl.multiple_of(t * step, step), step)
            x = x_ref[at, :].astype(F32)
            g = g_ref[at, :]
            v = v_ref[at, :].astype(F32)
            sx = sigmoid(x)
            gate = x * sx
            h = (x + v * gate).astype(BF)
            h_parts = [h[:, b * width : (b + 1) * width] for b in range(groups)]
            g_parts = [g[:, b * width : (b + 1) * width] for b in range(groups)]
            acts, slopes = [], []
            for b in range(groups):
                a = dot(h_parts[b], up_ref[b], 1, 0).astype(BF)
                s = sigmoid(a)
                q = a * s
                acts.append(q)
                slopes.append(s + q * (1 - s))
            rows_copy(dq_hbm, dq_ref, 4, t).wait()
            grads = []
            for b in range(groups):
                lanes = slice(b * sub, (b + 1) * sub)
                perm = jnp.concatenate([acts[p][:, lanes] for p in range(groups)], axis=1)
                w[1, b] += dot(g_parts[b], perm, 0, 0)
                dq = dq_ref[at, b * inner : (b + 1) * inner]
                da = dq * slopes[b]
                w[0, b] += dot(h_parts[b], da, 0, 0)
                grads.append(dot(da, up_ref[b], 1, 1))
            dh = (g.astype(F32) + jnp.concatenate(grads, axis=1)).astype(BF).astype(F32)
            dv[at, :] = (dh * gate).astype(BF)
            rows_copy(dv, dv_hbm, 2, t).start()
            r_ref[at, :] = (dh * (1.0 + v * (sx + gate * (1.0 - sx)))).astype(BF)
            rows_copy(r_ref, r_hbm, 3, t).start()
            return carry

        lax.fori_loop(0, tiles, tile, 0)
        halves[1] = w[1 - half_ref[0]].astype(BF)
        send = whole_copy(halves.at[1], sent_hbm, 2)
        send.start()
        halves[0] = w[half_ref[0]].astype(BF)
        keep = whole_copy(halves.at[0], kept_hbm, 3)
        keep.start()
        for t in range(tiles):
            rows_copy(dv, dv_hbm, 2, t).wait()
            rows_copy(r_ref, r_hbm, 3, t).wait()
        send.wait()
        keep.wait()

    hidden = rows * groups * inner
    return pl.pallas_call(
        body,
        in_specs=[SCALAR, ANY, ANY, VMEM, ANY, ANY],
        out_specs=[ANY] * 4,
        out_shape=[
            pltpu.HBM((rows, channels), BF),
            pltpu.HBM((rows, channels), BF),
            pltpu.HBM(up_blocks.shape, BF),
            pltpu.HBM(up_blocks.shape, BF),
        ],
        scratch_shapes=[
            pltpu.VMEM((rows, channels), BF),
            pltpu.VMEM((rows, channels), BF),
            pltpu.VMEM(up_blocks.shape, BF),
            pltpu.VMEM(pulled.shape, BF),
            pltpu.VMEM((rows, channels), BF),
            pltpu.VMEM((rows, channels), BF),
            pltpu.VMEM((2, groups, width, inner), F32),
            pltpu.VMEM((2, groups, width, inner), BF),
            pltpu.SemaphoreType.DMA((5 * tiles + 4,)),
        ],
        compiler_params=params(0),
        cost_estimate=cost(
            10 * hidden * width, 10 * rows * channels + 8 * groups * width * inner, hidden
        ),
        name="middle",
    )(half, in_hbm(blocked), in_hbm(incoming), in_vmem(mixed), in_hbm(up_blocks), in_hbm(pulled))


def bring(arrays, name):
    number = len(arrays)

    def body(*refs):
        sems = refs[-1]
        copies = [
            pltpu.make_async_copy(refs[i], refs[number + i], sems.at[i]) for i in range(number)
        ]
        for c in copies:
            c.start()
        for c in copies:
            c.wait()

    return pl.pallas_call(
        body,
        in_specs=[ANY] * number,
        out_specs=[pl.BlockSpec(memory_space=pltpu.VMEM)] * number,
        out_shape=[pltpu.VMEM(a.shape, a.dtype) for a in arrays],
        scratch_shapes=[pltpu.SemaphoreType.DMA((number,))],
        compiler_params=pltpu.CompilerParams(vmem_limit_bytes=16 * 1024 * 1024),
        cost_estimate=cost(0, sum(2 * a.size * a.dtype.itemsize for a in arrays)),
        name=name,
    )(*[in_hbm(a) for a in arrays])


def finish(factor, grad_first, blocked, gate_grad, scale):
    block, channels = blocked.shape
    tiles = 4
    step = block // tiles

    def body(f, x, d_hbm, r_hbm, one_hbm, out_hbm, d, r, one, out, sems):
        ds = row_copies(d_hbm, d, sems, 0, tiles)
        rs = row_copies(r_hbm, r, sems, tiles, tiles)
        ones = row_copies(one, one_hbm, sems, 2 * tiles, tiles)
        outs = row_copies(out, out_hbm, sems, 3 * tiles, tiles)
        for c in ds + rs:
            c.start()
        for t in range(tiles):
            at = slice(t * step, (t + 1) * step)
            ds[t].wait()
            one[at, :] = dot(d[at, :], x[...], 1, 1) * scale
            ones[t].start()
        for t in range(tiles):
            at = slice(t * step, (t + 1) * step)
            rs[t].wait()
            total = dot(f[:, at], d[...], 0, 0) + r[at, :].astype(F32)
            out[at, :] = total.astype(BF)
            outs[t].start()
        for c in ones + outs:
            c.wait()

    return pl.pallas_call(
        body,
        in_specs=[VMEM, VMEM, ANY, ANY],
        out_specs=[ANY] * 2,
        out_shape=[pltpu.HBM((block, block), F32), pltpu.HBM((block, channels), BF)],
        scratch_shapes=[
            pltpu.VMEM((block, channels), BF),
            pltpu.VMEM((block, channels), BF),
            pltpu.VMEM((block, block), F32),
            pltpu.VMEM((block, channels), BF),
            pltpu.SemaphoreType.DMA((4 * tiles,)),
        ],
        compiler_params=params(0),
        cost_estimate=cost(4 * block * block * channels, 6 * block * block + 8 * block * channels),
        name="finish",
    )(in_vmem(factor), in_vmem(blocked), in_hbm(grad_first), in_hbm(gate_grad))


def radices(count):
    steps, stride = [], 1
    while stride < count:
        radix = 4 if stride >= 4 and count // stride == 4 else 2
        steps.append((stride, radix))
        stride *= radix
    return steps


def swap(values, count, stride, s):
    return lax.ppermute(values, "seq", [(i, i ^ (stride * s)) for i in range(count)])


def add_and_cut(terms, digit, radix):
    rows, columns = terms[0].shape
    share = rows // radix

    number = len(terms)

    number = len(terms)
    shape = (radix, share, columns)

    def body(digit_ref, *refs):
        ins, outs = refs[:number], refs[number : number + radix]
        held, made, sems = refs[number + radix : -radix - 1], refs[-radix - 1 : -1], refs[-1]
        copies = [pltpu.make_async_copy(ins[i], held[i], sems.at[i]) for i in range(number)]
        for c in copies:
            c.start()
        for c in copies:
            c.wait()
        copies = []
        for s, ref in enumerate(made):
            total = held[0][digit_ref[0] ^ s].astype(F32)
            for term in held[1:]:
                total = total + term[digit_ref[0] ^ s].astype(F32)
            ref[...] = total.astype(ref.dtype)
            copies.append(pltpu.make_async_copy(ref, outs[s], sems.at[number + s]))
            copies[-1].start()
        for c in copies:
            c.wait()

    types = [F32] + [BF] * (radix - 1)
    return pl.pallas_call(
        body,
        in_specs=[SCALAR] + [ANY] * number,
        out_specs=[ANY] * radix,
        out_shape=[pltpu.HBM((share, columns), t) for t in types],
        scratch_shapes=[pltpu.VMEM(shape, t.dtype) for t in terms]
        + [pltpu.VMEM((share, columns), t) for t in types]
        + [pltpu.SemaphoreType.DMA((number + radix,))],
        compiler_params=params(0),
        cost_estimate=cost(rows * columns, 8 * rows * columns),
        name="add_and_cut",
    )(digit.reshape(1), *[t.reshape(shape) for t in terms])


def scatter_step(terms, count, stride, radix):
    digit = (lax.axis_index("seq").astype(jnp.int32) // stride) % radix
    kept, *send = add_and_cut(terms, digit, radix)
    return [kept] + [swap(a, count, stride, s + 1) for s, a in enumerate(send)]


def gather_step(share, count, stride, radix, after=()):
    digit = (lax.axis_index("seq") // stride) % radix
    got = [share] + [swap(share, count, stride, s) for s in range(1, radix)]
    got, after = lax.optimization_barrier((got, after))
    if radix == 2:
        low = jnp.where(digit == 0, got[0], got[1])
        high = jnp.where(digit == 0, got[1], got[0])
        return jnp.concatenate([low, high], axis=0)
    whole = jnp.zeros((radix,) + share.shape, share.dtype)
    for s in range(radix):
        whole = lax.dynamic_update_index_in_dim(whole, got[s], digit ^ s, 0)
    return whole.reshape(radix * share.shape[0], share.shape[1])


def write_weights(total, up_shape, down_shape, scale):
    groups, width, inner = up_shape

    def body(up_in, down_in, up_ref, down_ref):
        up_ref[0] = up_in[...].astype(F32) * scale
        down_ref[0] = (down_in[...].astype(F32) * scale).T

    return pl.pallas_call(
        body,
        grid=(groups,),
        in_specs=[
            pl.BlockSpec((width, inner), lambda b: (b, 0)),
            pl.BlockSpec((width, inner), lambda b: (groups + b, 0)),
        ],
        out_specs=[
            pl.BlockSpec((1, width, inner), lambda b: (b, 0, 0)),
            pl.BlockSpec((1, inner, width), lambda b: (b, 0, 0)),
        ],
        out_shape=[
            jax.ShapeDtypeStruct(up_shape, F32),
            jax.ShapeDtypeStruct(down_shape, F32),
        ],
        compiler_params=params(),
        cost_estimate=cost(groups * width * inner, 12 * groups * width * inner),
        name="write_weights",
    )(total, total)


def on_device(tokens, cotangent, factor_one, factor_two, up_blocks, down_blocks):
    count = lax.axis_size("seq")
    block, channels = factor_one.shape[1], tokens.shape[1]
    here = block // count
    scale = float(count * tokens.shape[0]) ** (-0.5)
    factor = factor_one.reshape(block, block)
    grouped = here % 16 == 0

    def exchange(values):
        cut = values.reshape(count, here, channels)
        return lax.all_to_all(cut, "seq", split_axis=0, concat_axis=0, tiled=True)

    if grouped:
        spread = spread_factor(factor_two)

    def second(cols, back):
        if grouped:
            return mix_second(spread, cols, back)
        names = "kmj,mkc->jkc" if back else "kmj,jkc->mkc"
        return jnp.einsum(names, factor_two, cols, preferred_element_type=F32).astype(BF)

    def second_grad(grads, firsts):
        if grouped:
            return grad_second(grads, firsts, scale)
        return jnp.einsum("mkc,jkc->kmj", grads, firsts, preferred_element_type=F32) * scale

    half = (lax.axis_index("seq") % 2).astype(jnp.int32).reshape(1)
    firsts = exchange(mix_first(factor, tokens))
    mixed = exchange(second(firsts, False)).reshape(block, channels)
    late = (cotangent, down_blocks)
    firsts, late = lax.optimization_barrier((firsts, late))
    pulled = pull_back(*late)
    dv, gate_grad, kept, sent = middle(half, tokens, cotangent, mixed, up_blocks, pulled)
    grad_mixed = exchange(dv)
    back = second(grad_mixed, True)
    terms = [kept, swap(sent, count, 1, 1)]
    terms = [t.reshape(-1, t.shape[-1]) for t in terms]
    steps = radices(count)
    for step in steps[1:]:
        terms = scatter_step(terms, count, *step)
    terms, back = lax.optimization_barrier((terms, back))
    total = sum(t.astype(F32) for t in terms).astype(BF)
    back, total = lax.optimization_barrier((back, total))
    grad_first = exchange(back).reshape(block, channels)
    two = second_grad(grad_mixed, firsts)
    for step in reversed(steps):
        total = gather_step(total, count, *step, after=two if step == steps[1] else ())
    grad_up, grad_down = write_weights(total, up_blocks.shape, down_blocks.shape, scale)
    late = (factor, tokens)
    late, grad_up, grad_down = lax.optimization_barrier((late, grad_up, grad_down))
    factor, tokens = bring(late, "bring")
    one, grad_tokens = finish(factor, grad_first, tokens, gate_grad, scale)
    return (grad_tokens, one.reshape(1, block, block), two, grad_up, grad_down)


def solution(mesh):
    return jax.shard_map(
        on_device,
        mesh=mesh,
        in_specs=(
            P(("grp", "seq"), None),
            P(("grp", "seq"), None),
            P("seq", None, None),
            P("seq", None, None),
            P(),
            P(),
        ),
        out_specs=(
            P(("grp", "seq"), None),
            P(("grp", "seq"), None, None),
            P(("grp", "seq"), None, None),
            P("grp", None, None),
            P("grp", None, None),
        ),
        check_vma=False,
    )
```
